512 devices in a mesh: group: 2 (over core), gx: 16 (over z, y_hi), gy: 16 (over y_lo, x).
Axes of the slice: x: 4, y: 8 (y_hi: 2, y_lo: 4; y = y_hi * 4 + y_lo), z: 8, core: 2. Of those that a mesh axis runs over, the one named last changes fastest.
Arguments:
- forcing: float32 [256, 128, 256], P('gx', 'gy', 'group'), may hold values from -6 to 6
- metric: float32 [256, 128, 256], P('gx', 'gy', 'group'), may hold values from 0.5 to 2
- sweeps: int32 [2, 3], replicated, may hold values from 1 to 4, as said below
Outputs:
- solution: float32 [256, 128, 256], P('gx', 'gy', 'group')
- residual: float32 [256, 128, 256], P('gx', 'gy', 'group')
The draws below stay inside these ranges and needn't reach their ends.
Inputs may be any that keep to these rules, and one draw needn't show every extreme that they name: `sweeps`: at least one entry is 4.
All inputs are finite; a program needn't handle non-finite values.
Results may differ from the reference program's by a relative error of at most 0.0001.
Values sent between devices are 32-bit elements; how exact they have to be, the bound alone decides.
No kernel may reach another device: no remote copies, remote signals or barrier semaphores. Data moves between devices by JAX's collectives and lax.ppermute only.
A program may use at most 64 MiB of HBM per device.

```python
import math
import jax
import jax.numpy as jnp

MAXSWEEPS = 4
CYCLES = 2
NX = 256
NY = 128
NZ = 256


def draw_sweeps(key, part):
    key = jax.random.fold_in(key, 11)
    first_key, second_key = jax.random.split(key)
    counts = jax.random.randint(first_key, (CYCLES * 3,), 1, MAXSWEEPS + 1)
    longest = jax.random.randint(second_key, (), 0, CYCLES * 3)
    filled = jnp.where(jnp.arange(CYCLES * 3) == longest, MAXSWEEPS, counts)
    return filled.reshape(CYCLES, 3).astype(jnp.int32)


def shard_levels(own_key, shape, pieces, smallest, high):
    factor_of, own = 1.0, jax.random.fold_in(own_key, 6)
    for dim, shards_of in pieces:
        steps = jnp.exp(jax.random.uniform(jax.random.fold_in(own, dim), (shards_of,), jnp.float32, smallest / len(pieces), high / len(pieces)))
        factor_of = factor_of * jnp.repeat(steps, shape[dim] // shards_of).reshape([-1 if axis == dim else 1 for axis in range(len(shape))])
    return factor_of


def bell_draw(stream_key, shape, width, most, cuts=(), kind=jnp.bfloat16):
    entries = width * jax.random.normal(stream_key, shape, jnp.float32)
    if cuts:
        entries = entries * shard_levels(stream_key, shape, cuts, -0.22, 0.18)
    return jnp.clip(entries, -most, most).astype(kind)


def setup_inputs(seed: int = 0) -> dict:
    key_list = jax.random.split(jax.random.key(seed), 4)
    forcing = bell_draw(key_list[0], (NX, NY, NZ), 1.0, 6.0, ((0, 16), (1, 16), (2, 2)), jnp.float32)
    metric = jnp.clip(jnp.exp(math.log(2.0) - 1.3862944 * jax.random.uniform(key_list[1], (NX, NY, NZ), jnp.float32) ** shard_levels(key_list[1], (NX, NY, NZ), ((0, 16), (1, 16), (2, 2)), -0.2, 0.2)), 0.5, 2.0)
    sweeps = draw_sweeps(jax.random.fold_in(key_list[3], 71), 0)
    return {"forcing": forcing, "metric": metric, "sweeps": sweeps}


RELAXATION = 0.8
SIDE_WEIGHT = 0.05 ** (1.0 / 3.0)
MID_WEIGHT = 2.0 * SIDE_WEIGHT
SELF_WEIGHT = 3.4


def stencil_padded(padded):
    summed = MID_WEIGHT * padded[1:-1] + SIDE_WEIGHT * (padded[2:] + padded[:-2])
    summed = MID_WEIGHT * summed[:, 1:-1] + SIDE_WEIGHT * (summed[:, 2:] + summed[:, :-2])
    return MID_WEIGHT * summed[:, :, 1:-1] + SIDE_WEIGHT * (summed[:, :, 2:] + summed[:, :, :-2])


def block_sum(field):
    dims = field.shape
    return field.reshape(dims[0] // 2, 2, dims[1] // 2, 2, dims[2] // 2, 2).sum(axis=(1, 3, 5))


def prolong(coarse):
    dims = coarse.shape
    spread = jnp.broadcast_to(coarse[:, None, :, None, :, None], (dims[0], 2, dims[1], 2, dims[2], 2))
    return 0.5 * spread.reshape(2 * dims[0], 2 * dims[1], 2 * dims[2])


def apply_level(field, weights, factor):
    weighted = weights * field
    return factor * weights * (SELF_WEIGHT * weighted - stencil_padded(jnp.pad(weighted, 1)))


def relax(rhs_field, diagonal, count, operator):
    update = jnp.zeros_like(rhs_field)
    for sweep_index in range(MAXSWEEPS):
        active = (sweep_index < count).astype(jnp.float32)
        update = update + active * (RELAXATION * (rhs_field - operator(update)) / diagonal)
    return update


def reference(forcing, metric, sweeps):
    metric_one = 0.125 * block_sum(metric)
    metric_two = 0.125 * block_sum(metric_one)
    diag_zero = (1.0 * 3.0) * metric * metric
    diag_one = (0.25 * 3.0) * metric_one * metric_one
    diag_two = (0.0625 * 3.0) * metric_two * metric_two
    solution = jnp.zeros_like(forcing)
    for cycle_index in range(CYCLES):
        res_zero = forcing - apply_level(solution, metric, 1.0)
        fine_corr = relax(res_zero, diag_zero, sweeps[cycle_index, 0], lambda field: apply_level(field, metric, 1.0))
        res_one = 0.5 * block_sum(res_zero)
        mid_corr = relax(res_one, diag_one, sweeps[cycle_index, 1], lambda field: apply_level(field, metric_one, 0.25))
        res_two = 0.5 * block_sum(res_one)
        low_corr = relax(res_two, diag_two, sweeps[cycle_index, 2], lambda field: apply_level(field, metric_two, 0.0625))
        mid_corr = mid_corr + prolong(low_corr)
        solution = solution + fine_corr + prolong(mid_corr)
    residual = forcing - apply_level(solution, metric, 1.0)
    return solution, residual
```

```python
import jax
import jax.numpy as jnp
import numpy as np
from jax import lax
from jax.experimental import pallas as pl
from jax.experimental.pallas import tpu as pltpu
from jax.sharding import PartitionSpec as P

CYCLES = 2
RELAXATION = 0.8
SIDE_WEIGHT = 0.05 ** (1.0 / 3.0)
SELF_WEIGHT = 3.4
SIDE_CUBE = SIDE_WEIGHT**3

KEEP = 1.0 - RELAXATION * SELF_WEIGHT / 3.0
SPREAD = RELAXATION * SIDE_CUBE / 3.0
LEVEL = [RELAXATION / (3.0 * 4.0**-level) for level in range(3)]

F32 = jnp.float32
TILE = (8, 128)

X_FIRST = dict(h0=0, w=8, h1=10, w12=12, h2=13, size=14)
X_SECOND = dict(h0=0, h1=8, h2=10, size=11)
Y_FIRST = dict(h0=0, w=24, h1=42, w1=50, h2=55, w2=58, size=60, far=60)
Y_SECOND = dict(h0=0, h1=24, h2=32, size=35, far=35)


def sums_of_pairs(rows):
    out = np.zeros((8, 8), np.float32)
    for row in range(rows):
        out[row, 2 * row] = out[row, 2 * row + 1] = 1.0
    return out


def doubling(sources):
    out = np.zeros((16, 16), np.float32)
    for target, source in sources.items():
        out[target, source] = 0.5
    return out


LANE_SUMS = (np.arange(256)[:, None] // 2 == np.arange(128)[None]).astype(np.float32)
ROW_SUMS_ONE = np.kron(np.eye(16, dtype=np.float32), sums_of_pairs(4))
ROW_SUMS_TWO = np.kron(np.eye(8, dtype=np.float32), sums_of_pairs(2))
LANE_COPIES = np.ascontiguousarray(LANE_SUMS.T)
ROW_COPIES_TWO = np.kron(
    np.eye(6, dtype=np.float32), doubling({0: 0, 1: 0, 2: 1, 3: 1, 4: 2, 15: 15})
)
ROW_COPIES_ONE = np.kron(
    np.eye(10, dtype=np.float32),
    doubling({**{row: row // 2 for row in range(8)}, 8: 4, 15: 15}),
)


def dot(a, b):
    return lax.dot_general(
        a,
        b,
        (((1,), (0,)), ((), ())),
        precision=lax.Precision.HIGHEST,
        preferred_element_type=F32,
    )


def sub_index():
    return lax.broadcasted_iota(jnp.int32, TILE, 0)


def lane_index():
    return lax.broadcasted_iota(jnp.int32, TILE, 1)


def turn(tile, by):
    by %= 8
    return pltpu.roll(tile, by, 0) if by else tile


def keep(where, tile):
    return jnp.where(where, tile, 0.0)


def inverse(tile):
    return jnp.where(tile > 0, 1.0 / jnp.where(tile > 0, tile, 1.0), 0.0)


def flags(s):
    return [s[k].astype(F32) for k in range(7, 13)]


def coarse_sides(planes, row_one, row_two, lane_sums):
    one = dot(row_one, dot(jnp.concatenate(planes, axis=0), lane_sums))
    pairs = [one[16 * k : 16 * k + 8] + one[16 * k + 8 : 16 * k + 16] for k in range(len(planes) // 2)]
    two = dot(row_two, dot(jnp.concatenate(pairs, axis=0), lane_sums[:128]))
    return one, two


def tiles_of(value):
    return value.reshape(value.shape[0] // 8, 8, 128)


def pack_x(s, h0, h1, h2, xp, at):
    core = s[6]
    fine = jnp.where(core == 0, 12, 0)
    middle = jnp.where(core == 0, 4, 0)
    for k in range(4):
        for z in range(2):
            xp[at["h0"] + 2 * k + z] = h0[fine + k, z]
    for k in range(2):
        xp[at["h1"] + k] = h1[middle + 2 * k] + turn(h1[middle + 2 * k + 1], 4)
    xp[at["h2"]] = quad([h2[k] for k in range(4)])


def quad(tiles):
    total = tiles[0]
    for k in range(1, len(tiles)):
        total = total + turn(tiles[k], 2 * k)
    return total


def first_kernel(s, mg, fg, lane_sums, row_one, row_two, xp, h0, h1, w1, h2, w2):
    for z in range(2):
        h0[:, z] = LEVEL[0] * fg[z] / mg[z]
    planes = [
        jnp.concatenate([ref[z, 2 * k] + ref[z, 2 * k + 1] for z in range(2)], axis=1)
        for ref in (mg, fg)
        for k in range(8)
    ]
    one, two = coarse_sides(planes, row_one[...], row_two[...], lane_sums[...])
    w1_own = 0.125 * one[:64]
    w2_own = 0.125 * 0.125 * two[:32]
    w1[...] = tiles_of(w1_own)
    w2[...] = tiles_of(w2_own)
    h1[...] = tiles_of(LEVEL[1] * 0.5 * one[64:] * inverse(w1_own))
    h2[...] = tiles_of(LEVEL[2] * 0.25 * two[32:] * inverse(w2_own))
    pack_x(s, h0, h1, h2, xp, X_FIRST)
    core = s[6]
    edge = jnp.where(core == 0, 15, 0)
    for z in range(2):
        xp[X_FIRST["w"] + z] = mg[z, edge]
    xp[X_FIRST["w12"]] = w1[jnp.where(core == 0, 7, 0)] + turn(w2[jnp.where(core == 0, 3, 0)], 4)


def column_h0(p, z, h0, xr, at, lo, hi):
    if p < 4:
        return xr[1, 0, at["h0"] + 2 * p + z] * lo
    if p < 20:
        return h0[p - 4, z]
    return xr[0, 1, at["h0"] + 2 * (p - 20) + z] * hi


def column_w(p, z, mg, xr, at):
    if p == 0:
        return xr[1, 0, at["w"] + z]
    if p < 17:
        return mg[z, p - 1]
    return xr[0, 1, at["w"] + z]


def column_h1(p, h1, xr, at, lo, hi):
    if 4 <= p < 12:
        return h1[p - 4]
    if p < 4:
        packed = xr[1, 0, at["h1"] + p // 2] * lo
    else:
        packed = xr[0, 1, at["h1"] + (p - 12) // 2] * hi
    return keep(sub_index() < 4, turn(packed, 4 * (p % 2)))


def column_w1(p, w1, xr, at):
    if 1 <= p < 9:
        return w1[p - 1]
    packed = xr[1, 0, at["w12"]] if p == 0 else xr[0, 1, at["w12"]]
    return keep(sub_index() < 4, packed)


def column_h2(p, h2, xr, at, lo, hi):
    if 4 <= p < 8:
        return h2[p - 4]
    packed = xr[1, 0, at["h2"]] * lo if p < 4 else xr[0, 1, at["h2"]] * hi
    return keep(sub_index() < 2, turn(packed, -2 * (p % 4)))


def column_w2(p, w2, xr, at):
    if 1 <= p < 5:
        return w2[p - 1]
    packed = xr[1, 0, at["w12"]] if p == 0 else xr[0, 1, at["w12"]]
    return keep(sub_index() < 2, turn(packed, 4))


def pack_y(s, h0, h1, h2, xr, yp, x_at, at):
    lo, hi = flags(s)[:2]
    mine = (sub_index() < 4) == (s[6] == 1)
    for k in range(12):
        for z in range(2):
            first, second = (column_h0(2 * k + i, z, h0, xr, x_at, lo, hi) for i in range(2))
            yp[at["h0"] + 2 * k + z] = jnp.where(mine, first, turn(second, 4))
    for k in range(2):
        yp[at["h1"] + k] = xr[1, 0, x_at["h1"] + k] * lo
        yp[at["h1"] + 6 + k] = xr[0, 1, x_at["h1"] + k] * hi
    for k in range(4):
        yp[at["h1"] + 2 + k] = h1[2 * k] + turn(h1[2 * k + 1], 4)
    yp[at["h2"]] = xr[1, 0, x_at["h2"]] * lo
    yp[at["h2"] + 1] = quad([h2[k] for k in range(4)])
    yp[at["h2"] + 2] = xr[0, 1, x_at["h2"]] * hi


def first_rows_kernel(s, h0, mg, h1, w1, h2, w2, xr, yp, y2p):
    at = Y_FIRST
    pack_y(s, h0, h1, h2, xr, yp, X_FIRST, at)
    mine = (sub_index() < 4) == (s[6] == 1)
    for k in range(9):
        for z in range(2):
            first, second = (column_w(2 * k + i, z, mg, xr, X_FIRST) for i in range(2))
            yp[at["w"] + 2 * k + z] = jnp.where(mine, first, turn(second, 4))
    for k in range(5):
        first, second = (column_w1(2 * k + i, w1, xr, X_FIRST) for i in range(2))
        yp[at["w1"] + k] = first + turn(second, 4)
    w2_planes = [column_w2(p, w2, xr, X_FIRST) for p in range(6)]
    yp[at["w2"]] = quad(w2_planes[:4])
    yp[at["w2"] + 1] = quad(w2_planes[4:])
    for k in range(3):
        y2p[k] = yp[at["h2"] + k]


def second_rows_kernel(s, h0, h1, h2, xr, yp, y2p):
    pack_y(s, h0, h1, h2, xr, yp, X_SECOND, Y_SECOND)
    for k in range(3):
        y2p[k] = yp[Y_SECOND["h2"] + k]


def split_rows(above, below):
    sub = sub_index()
    first = jnp.where(sub < 4, above, below)
    second = turn(jnp.where(sub < 4, below, above), 4)
    return first, second


def join_h0(s, h0, xr, yr, out, x_at, at):
    lo, hi, ylo, yhi = flags(s)[:4]
    for k in range(12):
        for z in range(2):
            tile = at["h0"] + 2 * k + z
            halos = split_rows(yr[0, tile] * yhi, yr[1, tile] * ylo)
            for i in range(2):
                out[2 * k + i, z] = column_h0(2 * k + i, z, h0, xr, x_at, lo, hi)
                out[2 * k + i, 2 + z] = halos[i]


def join_w(mg, xr, yr, out):
    for k in range(9):
        for z in range(2):
            tile = Y_FIRST["w"] + 2 * k + z
            halos = split_rows(yr[0, tile], yr[1, tile])
            for i in range(2):
                out[2 * k + i, z] = column_w(2 * k + i, z, mg, xr, X_FIRST)
                out[2 * k + i, 2 + z] = halos[i]


def join_four(own, above, below, i):
    sub = sub_index()
    turned = 4 * (1 - i)
    return own + keep(sub >= 4, turn(above, turned)), keep(sub >= 4, turn(below, turned))


def join_h1(s, h1, xr, yr, out, x_at, at):
    lo, hi, ylo, yhi = flags(s)[:4]
    for k in range(8):
        above, below = yr[0, at["h1"] + k] * yhi, yr[1, at["h1"] + k] * ylo
        for i in range(2):
            own = column_h1(2 * k + i, h1, xr, x_at, lo, hi)
            out[2 * k + i, 0], out[2 * k + i, 1] = join_four(own, above, below, i)


def join_w1(w1, xr, yr, out):
    for k in range(5):
        above, below = (yr[j, Y_FIRST["w1"] + k] for j in range(2))
        for i in range(2):
            own = column_w1(2 * k + i, w1, xr, X_FIRST)
            both = join_four(own, above, below, i)
            for j in range(2):
                out[2 * k + i, j] = inverse(both[j])


def join_h2(s, h2, xr, yr, out, x_at, at):
    lo, hi, ylo, yhi, ylo2, yhi2 = flags(s)
    sub = sub_index()
    for k in range(3):
        above, below = yr[0, at["h2"] + k] * yhi, yr[1, at["h2"] + k] * ylo
        above2, below2 = yr[0, at["far"] + k] * yhi2, yr[1, at["far"] + k] * ylo2
        for i in range(4):
            p = 4 * k + i
            own = column_h2(p, h2, xr, x_at, lo, hi)
            upper = jnp.where(
                sub < 4, turn(above, 2 - 2 * i), keep(sub < 6, turn(above2, 4 - 2 * i))
            )
            out[p, 0] = own + keep(sub >= 2, upper)
            lower = jnp.where(sub < 6, turn(below2, 4 - 2 * i), turn(below, 6 - 2 * i))
            out[p, 1] = keep(sub >= 4, lower)


def join_w2(w2, xr, yr, out):
    sub = sub_index()
    for p in range(6):
        above, below = (yr[j, Y_FIRST["w2"] + p // 4] for j in range(2))
        i = p % 4
        own = column_w2(p, w2, xr, X_FIRST)
        out[p, 0] = inverse(own + keep((sub >= 2) & (sub < 4), turn(above, 2 - 2 * i)))
        out[p, 1] = inverse(keep(sub >= 6, turn(below, 6 - 2 * i)))


def along_y(first, second):
    sub = sub_index()
    up_first, up_second = turn(first, 7), turn(second, 7)
    first = first + jnp.where(sub == 7, up_second, up_first)
    second = second + jnp.where(sub == 7, up_first, up_second)
    down_first, down_second = turn(first, 1), turn(second, 1)
    return (
        first + jnp.where(sub == 0, down_second, down_first),
        second + jnp.where(sub == 0, down_first, down_second),
    )


def along_z_fine(left, right):
    lane = lane_index()
    down_left, down_right = pltpu.roll(left, 1, 1), pltpu.roll(right, 1, 1)
    up_left, up_right = pltpu.roll(left, 127, 1), pltpu.roll(right, 127, 1)
    out_left = (left + left) + (keep(lane > 0, down_left) + jnp.where(lane < 127, up_left, up_right))
    out_right = (right + right) + (
        jnp.where(lane > 0, down_right, down_left) + keep(lane < 127, up_right)
    )
    return out_left, out_right


def along_z_coarse(tile):
    lane = lane_index()
    return (tile + tile) + (
        keep(lane > 0, pltpu.roll(tile, 1, 1)) + keep(lane < 127, pltpu.roll(tile, 127, 1))
    )


def planes_to_stencil(tiles):
    if len(tiles) == 4:
        tiles = list(tiles)
        for z in range(2):
            tiles[z], tiles[2 + z] = along_y(tiles[z], tiles[2 + z])
        for y in range(2):
            tiles[2 * y], tiles[2 * y + 1] = along_z_fine(tiles[2 * y], tiles[2 * y + 1])
        return tiles
    return [along_z_coarse(tile) for tile in along_y(*tiles)]


def relax(q, h, planes, parts, count, masks, lo, hi):
    q[...] = h[...]

    def load(x):
        return [q[x, part] for part in range(parts)]

    def sweep(k, _):
        def step(j, before):
            x = k + 2 * j
            here, after, next_after = load(x), load(x + 1), load(x + 2)
            left = [a + b for a, b in zip(before, here)]
            middle = [a + b for a, b in zip(here, after)]
            right = [a + b for a, b in zip(after, next_after)]
            for place, olds, low, high in ((x, here, left, middle), (x + 1, after, middle, right)):
                spread = SPREAD * jnp.where(place < 4, lo, jnp.where(place >= planes - 4, hi, 1.0))
                summed = planes_to_stencil([a + b for a, b in zip(low, high)])
                for part in range(parts):
                    mask = spread * masks[part // (parts // 2)]
                    q[place, part] = KEEP * olds[part] + mask * summed[part] + h[place, part]
            return tuple(after)

        lax.fori_loop(0, planes // 2 - k, step, tuple(load(k - 1)))
        return 0

    lax.fori_loop(1, count, sweep, 0)


def relax_levels(s, cycle, h0, q0, h1, q1, h2, q2):
    lo, hi, ylo, yhi, ylo2, yhi2 = flags(s)
    sub, lane = sub_index(), lane_index()
    ones = jnp.ones(TILE, F32)
    masks0 = (ones, jnp.where(sub < 4, yhi, ylo) * ones)
    masks1 = (jnp.where(sub < 4, 1.0, yhi) * ones, jnp.where(sub < 4, 0.0, ylo) * ones)
    above = jnp.where(sub < 2, 1.0, jnp.where(sub < 4, yhi, jnp.where(sub < 6, yhi2, 0.0)))
    below = jnp.where(sub < 4, 0.0, jnp.where(sub < 6, ylo2, ylo))
    masks2 = (keep(lane < 64, above * ones), keep(lane < 64, below * ones))
    relax(q2, h2, 12, 2, s[3 * cycle + 2], masks2, lo, hi)
    relax(q1, h1, 16, 2, s[3 * cycle + 1], masks1, lo, hi)
    relax(q0, h0, 24, 4, s[3 * cycle], masks0, lo, hi)


def corrections(q1, iw1, q2, iw2, lane_copies, rows_two, rows_one):
    two = [q2[p + 3, part] * iw2[p, part] for p in range(6) for part in range(2)]
    spread = dot(rows_two[...], dot(jnp.concatenate(two, axis=0), lane_copies[:, :128]))
    one = []
    for p in range(10):
        for part in range(2):
            row = 16 * ((p + 1) // 2) + 8 * part
            one.append(q1[p + 3, part] * iw1[p, part] + spread[row : row + 8])
    return dot(rows_one[...], dot(jnp.concatenate(one, axis=0), lane_copies[...]))


def correction_tile(coarse, p, part):
    row, lane = 16 * ((p + 1) // 2) + 8 * (part // 2), 128 * (part % 2)
    return coarse[row : row + 8, lane : lane + 128]


def operator_rows(pf, x):
    planes = [[pf[x + i, part] for part in range(4)] for i in range(3)]
    summed = planes_to_stencil([a + (b + b) + c for a, b, c in zip(*planes)])
    return planes[1][:2], summed[:2]


def middle_kernel(
    s, h0, mg, fg, h1, w1, h2, w2, xr, yr,
    lane_sums, row_one, row_two, lane_copies, rows_two, rows_one,
    xp, pf, w, iw1, iw2, h0_next, h1_next, h2_next,
    h0_all, q0, h1_all, q1, h2_all, q2, g,
):
    join_h0(s, h0, xr, yr, h0_all, X_FIRST, Y_FIRST)
    join_w(mg, xr, yr, w)
    join_h1(s, h1, xr, yr, h1_all, X_FIRST, Y_FIRST)
    join_w1(w1, xr, yr, iw1)
    join_h2(s, h2, xr, yr, h2_all, X_FIRST, Y_FIRST)
    join_w2(w2, xr, yr, iw2)
    relax_levels(s, 0, h0_all, q0, h1_all, q1, h2_all, q2)
    coarse = corrections(q1, iw1, q2, iw2, lane_copies, rows_two, rows_one)
    for p in range(18):
        for part in range(4):
            pf[p, part] = q0[p + 3, part] + w[p, part] * correction_tile(coarse, p, part)

    def residual(x, _):
        iterate, summed = operator_rows(pf, x)
        for z in range(2):
            weight = mg[z, x]
            rest = fg[z, x] - weight * (SELF_WEIGHT * iterate[z] - SIDE_CUBE * summed[z])
            g[x, z] = rest
            h0_next[x, z] = LEVEL[0] * rest / weight
        return 0

    lax.fori_loop(0, 16, residual, 0)
    planes = [
        jnp.concatenate([g[2 * k, z] + g[2 * k + 1, z] for z in range(2)], axis=1)
        for k in range(8)
    ]
    one, two = coarse_sides(planes, row_one[:64, :64], row_two[:32, :32], lane_sums[...])
    w1_own, w2_own = w1[...], w2[...]
    h1_next[...] = LEVEL[1] * 0.5 * tiles_of(one) * inverse(w1_own)
    h2_next[...] = LEVEL[2] * 0.25 * tiles_of(two) * inverse(w2_own)
    pack_x(s, h0_next, h1_next, h2_next, xp, X_SECOND)


def last_kernel(
    s, h0, mg, fg, h1, h2, xr, yr, pf, w, iw1, iw2, lane_copies, rows_two, rows_one,
    solution_out, residual_out,
    h0_all, q0, h1_all, q1, h2_all, q2, pl_all,
):
    join_h0(s, h0, xr, yr, h0_all, X_SECOND, Y_SECOND)
    join_h1(s, h1, xr, yr, h1_all, X_SECOND, Y_SECOND)
    join_h2(s, h2, xr, yr, h2_all, X_SECOND, Y_SECOND)
    relax_levels(s, 1, h0_all, q0, h1_all, q1, h2_all, q2)
    coarse = corrections(q1, iw1, q2, iw2, lane_copies, rows_two, rows_one)
    for p in range(18):
        for part in range(4):
            pl_all[p, part] = (
                pf[p, part] + q0[p + 3, part] + w[p, part] * correction_tile(coarse, p, part)
            )
    first = s[6] == 0

    def finish(x, _):
        iterate, summed = operator_rows(pl_all, x)
        mine, spread = (jnp.where(first, both[0], both[1]) for both in (iterate, summed))
        weight = jnp.where(first, mg[0, x], mg[1, x])
        force = jnp.where(first, fg[0, x], fg[1, x])
        solution_out[x] = mine / weight
        residual_out[x] = force - weight * (SELF_WEIGHT * mine - SIDE_CUBE * spread)
        return 0

    lax.fori_loop(0, 16, finish, 0)


def call(kernel, outs, scratch, name, *operands):
    smem = pl.BlockSpec(memory_space=pltpu.SMEM)
    vmem = pl.BlockSpec(memory_space=pltpu.VMEM)
    return pl.pallas_call(
        kernel,
        out_shape=[jax.ShapeDtypeStruct(shape, F32) for shape in outs],
        in_specs=[smem] + [vmem] * (len(operands) - 1),
        out_specs=[vmem] * len(outs),
        scratch_shapes=[pltpu.VMEM(shape, F32) for shape in scratch],
        compiler_params=pltpu.CompilerParams(vmem_limit_bytes=32 * 2**20),
        name=name,
    )(*operands)


def tiles(*dims):
    return (*dims, *TILE)


def pairs(axis, distance):
    size = lax.axis_size(axis)
    return [[i, size + (i + distance) % size] for i in range(size)]


def share(value):
    return lax.all_gather(value, "group", axis=0)


def trade_x(packed):
    both = lax.all_gather(packed, ("group", "gx"), axis=0, axis_index_groups=pairs("gx", 1))
    return share(both)


def swap(packed, distance):
    moves = [move for a, b in pairs("gy", distance) for move in ((a, b), (b, a))]
    return lax.ppermute(packed, ("group", "gy"), moves)


def trade_y(packed, packed_far):
    far = swap(packed_far, 2)
    near = swap(packed, 1)
    return share(jnp.concatenate([near, far], axis=0))


def on_device(forcing, metric, sweeps):
    gx, gy = lax.axis_index("gx"), lax.axis_index("gy")
    x_last, y_last = lax.axis_size("gx") - 1, lax.axis_size("gy") - 1
    places = [gx > 0, gx < x_last, gy > 0, gy < y_last, gy > 1, gy < y_last - 1]
    s = jnp.concatenate(
        [sweeps.reshape(-1), jnp.stack([lax.axis_index("group"), *places]).astype(jnp.int32)]
    )
    mg, fg = share(metric), share(forcing)
    down = [jnp.asarray(LANE_SUMS), jnp.asarray(ROW_SUMS_ONE), jnp.asarray(ROW_SUMS_TWO)]
    up = [jnp.asarray(LANE_COPIES), jnp.asarray(ROW_COPIES_TWO), jnp.asarray(ROW_COPIES_ONE)]
    own = [tiles(16, 2), tiles(8), tiles(4)]
    spaces = [tiles(24, 4)] * 2 + [tiles(16, 2)] * 2 + [tiles(12, 2)] * 2

    xp, h0, h1, w1, h2, w2 = call(
        first_kernel,
        [tiles(X_FIRST["size"]), own[0], own[1], own[1], own[2], own[2]],
        [],
        "first_sides",
        *(s, mg, fg, *down),
    )
    xr = trade_x(xp)
    yp, y2p = call(
        first_rows_kernel,
        [tiles(Y_FIRST["size"]), tiles(3)],
        [],
        "first_rows",
        *(s, h0, mg, h1, w1, h2, w2, xr),
    )
    yr = trade_y(yp, y2p)
    xp, pf, w, iw1, iw2, h0, h1, h2 = call(
        middle_kernel,
        [tiles(X_SECOND["size"]), tiles(18, 4), tiles(18, 4), tiles(10, 2), tiles(6, 2), *own],
        [*spaces, tiles(16, 2)],
        "first_cycle",
        *(s, h0, mg, fg, h1, w1, h2, w2, xr, yr, *down, *up),
    )
    xr = trade_x(xp)
    yp, y2p = call(
        second_rows_kernel,
        [tiles(Y_SECOND["size"]), tiles(3)],
        [],
        "second_rows",
        *(s, h0, h1, h2, xr),
    )
    yr = trade_y(yp, y2p)
    return call(
        last_kernel,
        [tiles(16), tiles(16)],
        [*spaces, tiles(18, 4)],
        "second_cycle",
        *(s, h0, mg, fg, h1, h2, xr, yr, pf, w, iw1, iw2, *up),
    )


def solution(mesh):
    def program(forcing, metric, sweeps):
        return tuple(on_device(forcing, metric, sweeps))

    return jax.shard_map(
        program,
        mesh=mesh,
        in_specs=(P("gx", "gy", "group"), P("gx", "gy", "group"), P()),
        out_specs=(P("gx", "gy", "group"), P("gx", "gy", "group")),
        check_vma=False,
    )
```

```python
import jax
import jax.numpy as jnp
import numpy as np
from jax import lax
from jax.experimental import pallas as pl
from jax.experimental.pallas import tpu as pltpu
from jax.sharding import PartitionSpec as P

RELAXATION = 0.8
SIDE_WEIGHT = 0.05 ** (1.0 / 3.0)
SELF_WEIGHT = 3.4
SIDE_CUBE = SIDE_WEIGHT**3

KEEP = 1.0 - RELAXATION * SELF_WEIGHT / 3.0
SPREAD = RELAXATION * SIDE_CUBE / 3.0
LEVEL = [RELAXATION / (3.0 * 4.0**-level) for level in range(3)]

F32 = jnp.float32
TILE = (8, 128)

OWN = dict(h0=0, w=16, h1=32, w1=36, h2=40, w2=41, size=42)
COARSE = dict(h1=0, w1=4, h2=8, w2=9, size=10)
X_FIRST = dict(h0=0, h1=8, h2=10, w=11, w12=13, size=14)
X_SECOND = dict(h0=0, h1=8, h2=10, size=11)
Y_FIRST = dict(h0=0, h1=24, h2=32, w=35, w1=53, w2=58, size=60, far=60)
Y_SECOND = dict(h0=0, h1=24, h2=32, size=35, far=35)

LANES = np.arange(256)
HALF_SUMS = np.concatenate(
    [LANES[:128, None] // 2 == LANES[None, :128], LANES[:128, None] // 4 == LANES[None, :128]], axis=1
).astype(np.float32)
WHOLE_SUMS = np.concatenate(
    [LANES[:, None] // 2 == LANES[None, :128], LANES[:, None] // 4 == LANES[None, :128]], axis=1
).astype(np.float32)
COPIES = WHOLE_SUMS.T * np.where(LANES[:, None] < 128, 0.5, 0.25).astype(np.float32)


def exact_dot(rows, matrix):
    parts = []
    rest = rows
    for _ in range(3):
        parts.append(rest.astype(jnp.bfloat16))
        rest = rest - parts[-1].astype(F32)
    out = lax.dot_general(
        jnp.concatenate(parts, axis=0),
        matrix,
        (((1,), (0,)), ((), ())),
        preferred_element_type=F32,
    )
    count = rows.shape[0]
    return out[:count] + (out[count : 2 * count] + out[2 * count :])


def sub_index():
    return lax.broadcasted_iota(jnp.int32, TILE, 0)


def lane_index():
    return lax.broadcasted_iota(jnp.int32, TILE, 1)


def turn(tile, by):
    by %= 8
    return pltpu.roll(tile, by, 0) if by else tile


def keep(where, tile):
    return jnp.where(where, tile, 0.0)


def inverse(tile):
    return jnp.where(tile > 0, 1.0 / jnp.where(tile > 0, tile, 1.0), 0.0)


def flags(s):
    return [s[k].astype(F32) for k in range(7, 13)]


def pair_rows(first, second):
    sub = sub_index()
    first, second = (tile + turn(tile, 7) for tile in (first, second))
    low = jnp.where(sub == 0, first, turn(first, 7))
    low = jnp.where(sub < 2, low, jnp.where(sub == 2, turn(first, 6), turn(first, 5)))
    high = jnp.where(sub == 4, turn(second, 4), turn(second, 3))
    high = jnp.where(sub < 6, high, jnp.where(sub == 6, turn(second, 2), turn(second, 1)))
    return jnp.where(sub < 4, low, high)


def plane_sums(fine):
    sub = sub_index()
    sums = [fine[2 * k] + fine[2 * k + 1] for k in range(8)]
    one = [pair_rows(sums[2 * k], sums[2 * k + 1]) for k in range(4)]
    two = None
    for k in range(4):
        both = one[k] + turn(one[k], 4)
        both = both + turn(both, 7)
        placed = jnp.where(sub == 2 * k, turn(both, 2 * k), turn(both, 2 * k - 1))
        two = placed if k == 0 else jnp.where(sub < 2 * k, two, placed)
    return one + [two]


def first_kernel(s, m, f, sums, out):
    m_tiles, f_tiles = ([ref[x] for x in range(16)] for ref in (m, f))
    for x in range(16):
        out[OWN["h0"] + x] = LEVEL[0] * f_tiles[x] / m_tiles[x]
        out[OWN["w"] + x] = m_tiles[x]
    rows = jnp.concatenate(plane_sums(m_tiles) + plane_sums(f_tiles), axis=0)
    total = exact_dot(rows, sums[...])
    upper = s[6] == 1
    for k in range(5):
        left, width = (0, 64) if k < 4 else (128, 32)
        weight, force = (
            total[row : row + 8, left : left + 128] for row in (8 * k, 40 + 8 * k)
        )
        weight = (0.125 if k < 4 else 0.125 * 0.125) * weight
        force = (0.5 * LEVEL[1] if k < 4 else 0.25 * LEVEL[2]) * force * inverse(weight)
        weight, force = (
            jnp.where(upper, pltpu.roll(tile, width, 1), tile) for tile in (weight, force)
        )
        out[(OWN["w1"] + k) if k < 4 else OWN["w2"]] = weight
        out[(OWN["h1"] + k) if k < 4 else OWN["h2"]] = force


def pack_x(s, fine, h1, h2, xp, at):
    upward = s[6] == 0
    start = jnp.where(upward, 12, 0)
    for k in range(4):
        for z in range(2):
            xp[at["h0"] + 2 * k + z] = fine(start + k, z)
    for k in range(2):
        xp[at["h1"] + k] = jnp.where(upward, h1[2 + k], h1[k])
    xp[at["h2"]] = h2


def first_sides_kernel(s, own, xp, coarse):
    total = [own[0, k] + own[1, k] for k in range(OWN["h1"], OWN["size"])]
    for k in range(COARSE["size"]):
        coarse[k] = total[k]
    h1, w1 = total[:4], total[4:8]
    h2, w2 = total[8:]
    pack_x(s, lambda x, z: own[z, x], h1, h2, xp, X_FIRST)
    upward = s[6] == 0
    edge = OWN["w"] + jnp.where(upward, 15, 0)
    for z in range(2):
        xp[X_FIRST["w"] + z] = own[z, edge]
    sub = sub_index()
    edge_one = jnp.where(upward, turn(w1[3], 4), w1[0])
    edge_two = jnp.where(upward, turn(w2, 6), turn(w2, 4))
    xp[X_FIRST["w12"]] = jnp.where(sub < 4, edge_one, edge_two)


def column_fine(own, planes, xr, at, lo, hi):
    def load(p, z):
        if p < planes:
            return xr[1, 0, at + 2 * p + z] * lo
        if p < 16 + planes:
            return own(p - planes, z)
        return xr[0, 1, at + 2 * (p - 16 - planes) + z] * hi

    return load


def pack_fine(load, planes, mine, yp, at):
    for k in range(planes // 2):
        for z in range(2):
            yp[at + 2 * k + z] = jnp.where(mine, load(2 * k, z), turn(load(2 * k + 1, z), 4))


def pack_y(s, own, h1, h2, xr, yp, y2p, x_at, at):
    lo, hi = flags(s)[:2]
    mine = (sub_index() < 4) == (s[6] == 1)
    pack_fine(column_fine(own, 4, xr, x_at["h0"], lo, hi), 24, mine, yp, at["h0"])
    for k in range(2):
        yp[at["h1"] + k] = xr[1, 0, x_at["h1"] + k] * lo
        yp[at["h1"] + 6 + k] = xr[0, 1, x_at["h1"] + k] * hi
    for k in range(4):
        yp[at["h1"] + 2 + k] = h1(k)
    two = [xr[1, 0, x_at["h2"]] * lo, h2(), xr[0, 1, x_at["h2"]] * hi]
    for k in range(3):
        yp[at["h2"] + k] = two[k]
        y2p[k] = two[k]


def first_rows_kernel(s, own, coarse, xr, yp, y2p):
    at = Y_FIRST
    pack_y(
        s,
        lambda x, z: own[z, x],
        lambda k: coarse[k],
        lambda: coarse[COARSE["h2"]],
        *(xr, yp, y2p, X_FIRST, at),
    )
    sub = sub_index()
    mine = (sub < 4) == (s[6] == 1)
    weights = column_fine(lambda x, z: own[z, OWN["w"] + x], 1, xr, X_FIRST["w"], 1.0, 1.0)
    pack_fine(weights, 18, mine, yp, at["w"])
    low, high = xr[1, 0, X_FIRST["w12"]], xr[0, 1, X_FIRST["w12"]]
    for k in range(4):
        yp[at["w1"] + k] = coarse[COARSE["w1"] + k]
    yp[at["w1"] + 4] = jnp.where(sub < 4, low, turn(high, 4))
    yp[at["w2"]] = coarse[COARSE["w2"]]
    yp[at["w2"] + 1] = jnp.where(sub < 2, turn(low, 4), turn(high, 6))


def second_rows_kernel(s, h0, h12, xr, yp, y2p):
    pack_y(
        s,
        lambda x, z: h0[x, z],
        lambda k: h12[k],
        lambda: h12[4],
        *(xr, yp, y2p, X_SECOND, Y_SECOND),
    )


def join_fine(load, planes, yr, at, ylo, yhi, out):
    sub = sub_index()
    for k in range(planes // 2):
        for z in range(2):
            above, below = yr[0, at + 2 * k + z] * yhi, yr[1, at + 2 * k + z] * ylo
            halos = (
                jnp.where(sub < 4, above, below),
                turn(jnp.where(sub < 4, below, above), 4),
            )
            for i in range(2):
                out[2 * k + i, z] = load(2 * k + i, z)
                out[2 * k + i, 2 + z] = halos[i]


def four_rows(own, above, below, i):
    sub = sub_index()
    turned = 4 * (1 - i)
    first = jnp.where(sub < 4, turn(own, 4 * i), turn(above, turned))
    return first, keep(sub >= 4, turn(below, turned))


def join_h1(s, yp, yr, at, out):
    ylo, yhi = flags(s)[2:4]
    for k in range(8):
        tile = at + k
        own, above, below = yp[tile], yr[0, tile] * yhi, yr[1, tile] * ylo
        for i in range(2):
            out[2 * k + i, 0], out[2 * k + i, 1] = four_rows(own, above, below, i)


def join_w1(yp, yr, out):
    for k in range(5):
        tile = Y_FIRST["w1"] + k
        own, above, below = yp[tile], yr[0, tile], yr[1, tile]
        for i in range(2):
            p = 9 * i if k == 4 else 1 + 2 * k + i
            first, second = four_rows(own, above, below, i)
            out[p, 0], out[p, 1] = 1.0 / first, inverse(second)


def join_h2(s, yp, yr, at, out):
    ylo, yhi, ylo2, yhi2 = flags(s)[2:]
    sub = sub_index()
    for k in range(3):
        tile, far = at["h2"] + k, at["far"] + k
        own, above, below = yp[tile], yr[0, tile] * yhi, yr[1, tile] * ylo
        above2, below2 = yr[0, far] * yhi2, yr[1, far] * ylo2
        for i in range(4):
            first = jnp.where(sub < 2, turn(own, -2 * i), turn(above, 2 - 2 * i))
            upper = keep(sub < 6, turn(above2, 4 - 2 * i))
            out[4 * k + i, 0] = jnp.where(sub < 4, first, upper)
            lower = jnp.where(sub < 6, turn(below2, 4 - 2 * i), turn(below, 6 - 2 * i))
            out[4 * k + i, 1] = keep(sub >= 4, lower)


def join_w2(yp, yr, out):
    sub = sub_index()
    for p in range(6):
        k, i = (1, p // 5) if p in (0, 5) else (0, p - 1)
        tile = Y_FIRST["w2"] + k
        own, above, below = yp[tile], yr[0, tile], yr[1, tile]
        first = jnp.where(sub < 2, turn(own, -2 * i), turn(above, 2 - 2 * i))
        out[p, 0] = inverse(keep(sub < 4, first))
        out[p, 1] = inverse(keep(sub >= 6, turn(below, 6 - 2 * i)))


def along_y(first, second):
    sub = sub_index()
    up_first, up_second = turn(first, 7), turn(second, 7)
    first = first + jnp.where(sub == 7, up_second, up_first)
    second = second + jnp.where(sub == 7, up_first, up_second)
    down_first, down_second = turn(first, 1), turn(second, 1)
    return (
        first + jnp.where(sub == 0, down_second, down_first),
        second + jnp.where(sub == 0, down_first, down_second),
    )


def along_z_fine(left, right):
    lane = lane_index()
    up_left, up_right = pltpu.roll(left, 127, 1), pltpu.roll(right, 127, 1)
    sum_left = left + jnp.where(lane < 127, up_left, up_right)
    sum_right = right + keep(lane < 127, up_right)
    down_left, down_right = pltpu.roll(sum_left, 1, 1), pltpu.roll(sum_right, 1, 1)
    return (
        sum_left + jnp.where(lane > 0, down_left, left),
        sum_right + jnp.where(lane > 0, down_right, down_left),
    )


def along_z_coarse(tile):
    lane = lane_index()
    summed = tile + keep(lane < 127, pltpu.roll(tile, 127, 1))
    return summed + jnp.where(lane > 0, pltpu.roll(summed, 1, 1), tile)


def along_yz(tiles):
    tiles = list(tiles)
    if len(tiles) == 4:
        for z in range(2):
            tiles[z], tiles[2 + z] = along_y(tiles[z], tiles[2 + z])
        for y in range(2):
            tiles[2 * y], tiles[2 * y + 1] = along_z_fine(tiles[2 * y], tiles[2 * y + 1])
        return tiles
    return [along_z_coarse(tile) for tile in along_y(*tiles)]


def added(first, second):
    return [a + b for a, b in zip(first, second)]


def relax(q, h, planes, parts, count, masks, lo, hi):
    sides = [[mask * factor for mask in masks] for factor in (lo, 1.0, hi)]

    def sweep(k, source):
        def load(x):
            return [source[x, part] for part in range(parts)]

        here = load(k)
        below = added(load(k - 1), here)
        for x in range(k, planes - k):
            after = load(x + 1)
            above = added(here, after)
            summed = along_yz(added(below, above))
            side = sides[0 if x < 4 else 2 if x >= planes - 4 else 1]
            for part in range(parts):
                spread = side[part // (parts // 2)] * summed[part]
                q[x, part] = (KEEP * here[part] + spread) + h[x, part]
            here, below = after, above

    @pl.when(count == 1)
    def _():
        q[...] = h[...]

    for k in range(1, 4):

        @pl.when(count > k)
        def _():
            sweep(k, h if k == 1 else q)


def relax_levels(s, cycle, h0, q0, h1, q1, h2, q2):
    lo, hi, ylo, yhi, ylo2, yhi2 = [flag * 1.0 for flag in flags(s)]
    sub, lane = sub_index(), lane_index()
    spread = jnp.full(TILE, SPREAD, F32)
    above = jnp.where(sub < 2, 1.0, jnp.where(sub < 4, yhi, jnp.where(sub < 6, yhi2, 0.0)))
    below = jnp.where(sub < 4, 0.0, jnp.where(sub < 6, ylo2, ylo))
    masks2 = (keep(lane < 64, above * spread), keep(lane < 64, below * spread))
    masks1 = (jnp.where(sub < 4, 1.0, yhi) * spread, jnp.where(sub < 4, 0.0, ylo) * spread)
    masks0 = (spread, jnp.where(sub < 4, yhi, ylo) * spread)
    relax(q2, h2, 12, 2, s[3 * cycle + 2], masks2, lo, hi)
    relax(q1, h1, 16, 2, s[3 * cycle + 1], masks1, lo, hi)
    relax(q0, h0, 24, 4, s[3 * cycle], masks0, lo, hi)


def corrections(q1, iw1, q2, iw2, copies):
    sub = sub_index()
    one, two = (
        [
            jnp.where(sub < 7, q[p + 3, 0] * iw[p, 0], q[p + 3, 1] * iw[p, 1])
            for p in range(planes)
        ]
        for q, iw, planes in ((q1, iw1, 10), (q2, iw2, 6))
    )
    spread = []
    for tile in two:
        inner = jnp.where(sub < 3, turn(tile, 1), turn(tile, 2))
        spread.append(jnp.where((sub == 0) | (sub == 7), tile, inner))
    rows = [jnp.concatenate([one[p], spread[(p + 1) // 2]], axis=1) for p in range(10)]
    return exact_dot(jnp.concatenate(rows, axis=0), copies[...])


def iterate(coarse, q0, w, before, out):
    sub = sub_index()
    for k in range(10):
        for z in range(2):
            tile = coarse[8 * k : 8 * k + 8, 128 * z : 128 * z + 128]
            turned = [tile] + [turn(tile, by) for by in range(1, 5)]
            rows = turned[4]
            for by, last in ((3, 6), (2, 4), (1, 2), (0, 0)):
                rows = jnp.where(sub <= last, turned[by], rows)
            halo = jnp.where(sub < 7, turned[4], tile)
            for p in (2 * k - 1, 2 * k):
                if 0 <= p < 18:
                    for part, value in ((z, rows), (2 + z, halo)):
                        total = q0[p + 3, part] + w[p, part] * value
                        if before is not None:
                            total = before[p, part] + total
                        out[p, part] = total


def defects(pf):
    def load(p):
        return [pf[p, part] for part in range(4)]

    here = load(1)
    below = added(load(0), here)
    for x in range(16):
        after = load(x + 2)
        above = added(here, after)
        summed = along_yz(added(below, above))
        yield here[:2], [SELF_WEIGHT * here[z] - SIDE_CUBE * summed[z] for z in range(2)]
        here, below = after, above


def middle_kernel(
    s, own, coarse, xr, yp, yr, sums, copies,
    xp, pf, w, iw1, iw2, h0_next, h12_next,
    h0_all, q0, h1_all, q1, h2_all, q2,
):
    lo, hi, ylo, yhi = flags(s)[:4]
    load = column_fine(lambda x, z: own[z, x], 4, xr, X_FIRST["h0"], lo, hi)
    join_fine(load, 24, yr, Y_FIRST["h0"], ylo, yhi, h0_all)
    load = column_fine(lambda x, z: own[z, OWN["w"] + x], 1, xr, X_FIRST["w"], 1.0, 1.0)
    join_fine(load, 18, yr, Y_FIRST["w"], 1.0, 1.0, w)
    join_h1(s, yp, yr, Y_FIRST["h1"], h1_all)
    join_w1(yp, yr, iw1)
    join_h2(s, yp, yr, Y_FIRST, h2_all)
    join_w2(yp, yr, iw2)
    relax_levels(s, 0, h0_all, q0, h1_all, q1, h2_all, q2)
    iterate(corrections(q1, iw1, q2, iw2, copies), q0, w, None, pf)

    rests = [[], []]
    for x, (_, defect) in enumerate(defects(pf)):
        for z in range(2):
            h0 = own[z, x] - LEVEL[0] * defect[z]
            h0_next[x, z] = h0
            rests[z].append(own[z, OWN["w"] + x] * h0)
    summed = [plane_sums(rest) for rest in rests]
    rows = [jnp.concatenate([summed[0][k], summed[1][k]], axis=1) for k in range(5)]
    total = exact_dot(jnp.concatenate(rows, axis=0), sums[...])
    h1 = []
    for k in range(4):
        weight = coarse[COARSE["w1"] + k]
        h1.append(0.5 * LEVEL[1] / LEVEL[0] * total[8 * k : 8 * k + 8, :128] / weight)
        h12_next[k] = h1[k]
    weight = inverse(coarse[COARSE["w2"]])
    h2 = 0.25 * LEVEL[2] / LEVEL[0] * total[32:40, 128:] * weight
    h12_next[4] = h2
    pack_x(s, lambda x, z: h0_next[x, z], h1, h2, xp, X_SECOND)


def last_kernel(
    s, m, f, h0, xr, yp, yr, pf, w, iw1, iw2, copies,
    solution_out, residual_out,
    h0_all, q0, h1_all, q1, h2_all, q2, pf_all,
):
    lo, hi, ylo, yhi = flags(s)[:4]
    load = column_fine(lambda x, z: h0[x, z], 4, xr, X_SECOND["h0"], lo, hi)
    join_fine(load, 24, yr, Y_SECOND["h0"], ylo, yhi, h0_all)
    join_h1(s, yp, yr, Y_SECOND["h1"], h1_all)
    join_h2(s, yp, yr, Y_SECOND, h2_all)
    relax_levels(s, 1, h0_all, q0, h1_all, q1, h2_all, q2)
    iterate(corrections(q1, iw1, q2, iw2, copies), q0, w, pf, pf_all)
    first = s[6] == 0
    for x, (here, defect) in enumerate(defects(pf_all)):
        mine, rest = (jnp.where(first, both[0], both[1]) for both in (here, defect))
        weight = m[x]
        solution_out[x] = mine / weight
        residual_out[x] = f[x] - weight * rest


def call(kernel, outs, scratch, name, *operands):
    smem = pl.BlockSpec(memory_space=pltpu.SMEM)
    vmem = pl.BlockSpec(memory_space=pltpu.VMEM)
    return pl.pallas_call(
        kernel,
        out_shape=[jax.ShapeDtypeStruct(shape, F32) for shape in outs],
        in_specs=[smem] + [vmem] * (len(operands) - 1),
        out_specs=[vmem] * len(outs),
        scratch_shapes=[pltpu.VMEM(shape, F32) for shape in scratch],
        compiler_params=pltpu.CompilerParams(vmem_limit_bytes=32 * 2**20),
        name=name,
    )(*operands)


def tiles(*dims):
    return (*dims, *TILE)


def pairs(axis, distance):
    size = lax.axis_size(axis)
    return [[i, size + (i + distance) % size] for i in range(size)]


def share(value):
    return lax.all_gather(value, "group", axis=0)


def trade_x(packed):
    both = lax.all_gather(packed, ("group", "gx"), axis=0, axis_index_groups=pairs("gx", 1))
    return share(both)


def swap(packed, distance):
    moves = [move for a, b in pairs("gy", distance) for move in ((a, b), (b, a))]
    return lax.ppermute(packed, ("group", "gy"), moves)


def trade_y(packed, packed_far):
    far = swap(packed_far, 2)
    near = swap(packed, 1)
    return share(jnp.concatenate([near, far], axis=0))


def on_device(forcing, metric, sweeps):
    gx, gy = lax.axis_index("gx"), lax.axis_index("gy")
    x_last, y_last = lax.axis_size("gx") - 1, lax.axis_size("gy") - 1
    places = [gx > 0, gx < x_last, gy > 0, gy < y_last, gy > 1, gy < y_last - 1]
    s = jnp.concatenate(
        [sweeps.reshape(-1), jnp.stack([lax.axis_index("group"), *places]).astype(jnp.int32)]
    )
    half_sums, sums, copies = (
        jnp.asarray(matrix, jnp.bfloat16) for matrix in (HALF_SUMS, WHOLE_SUMS, COPIES)
    )
    spaces = [tiles(24, 4)] * 2 + [tiles(16, 2)] * 2 + [tiles(12, 2)] * 2

    (own,) = call(
        first_kernel, [tiles(OWN["size"])], [], "block_sums", *(s, metric, forcing, half_sums)
    )
    own = share(own)
    xp, coarse = call(
        first_sides_kernel,
        [tiles(X_FIRST["size"]), tiles(COARSE["size"])],
        [],
        "first_sides",
        *(s, own),
    )
    xr = trade_x(xp)
    yp, y2p = call(
        first_rows_kernel,
        [tiles(Y_FIRST["size"]), tiles(3)],
        [],
        "first_rows",
        *(s, own, coarse, xr),
    )
    yr = trade_y(yp, y2p)
    xp, pf, w, iw1, iw2, h0, h12 = call(
        middle_kernel,
        [
            *(tiles(X_SECOND["size"]), tiles(18, 4), tiles(18, 4), tiles(10, 2), tiles(6, 2)),
            *(tiles(16, 2), tiles(5)),
        ],
        spaces,
        "first_cycle",
        *(s, own, coarse, xr, yp, yr, sums, copies),
    )
    xr = trade_x(xp)
    yp, y2p = call(
        second_rows_kernel,
        [tiles(Y_SECOND["size"]), tiles(3)],
        [],
        "second_rows",
        *(s, h0, h12, xr),
    )
    yr = trade_y(yp, y2p)
    return call(
        last_kernel,
        [tiles(16), tiles(16)],
        [*spaces, tiles(18, 4)],
        "second_cycle",
        *(s, metric, forcing, h0, xr, yp, yr, pf, w, iw1, iw2, copies),
    )


def solution(mesh):
    def program(forcing, metric, sweeps):
        return tuple(on_device(forcing, metric, sweeps))

    return jax.shard_map(
        program,
        mesh=mesh,
        in_specs=(P("gx", "gy", "group"), P("gx", "gy", "group"), P()),
        out_specs=(P("gx", "gy", "group"), P("gx", "gy", "group")),
        check_vma=False,
    )
```

```python
import jax
import jax.numpy as jnp
import numpy as np
from jax import lax
from jax.experimental import pallas as pl
from jax.experimental.pallas import tpu as pltpu
from jax.sharding import PartitionSpec as P

RELAXATION = 0.8
SIDE_WEIGHT = 0.05 ** (1.0 / 3.0)
SELF_WEIGHT = 3.4
SIDE_CUBE = SIDE_WEIGHT**3

KEEP = 1.0 - RELAXATION * SELF_WEIGHT / 3.0
SPREAD = RELAXATION * SIDE_CUBE / 3.0
LEVEL = [RELAXATION / (3.0 * 4.0**-level) for level in range(3)]

F32 = jnp.float32
TILE = (8, 128)

OWN = dict(h0=0, w=16, h1=32, w1=36, h2=40, w2=41, size=42)
COARSE = dict(h1=0, w1=4, h2=8, w2=9, size=10)
X_FIRST = dict(h0=0, h1=8, h2=10, w=11, w12=13, size=14)
X_SECOND = dict(h0=0, h1=8, h2=10, size=11)
Y_FIRST = dict(h0=0, h1=24, h2=32, w=35, w1=53, w2=58, size=60, far=60)
Y_SECOND = dict(h0=0, h1=24, h2=32, size=35, far=35)

LANES = np.arange(256)
WHOLE_SUMS = np.concatenate(
    [LANES[:, None] // 2 == LANES[None, :128], LANES[:, None] // 4 == LANES[None, :128]], axis=1
).astype(np.float32)
COPIES = WHOLE_SUMS.T * np.where(LANES[:, None] < 128, 0.5, 0.25).astype(np.float32)


def exact_dot(rows, matrix):
    parts = []
    rest = rows
    for _ in range(3):
        parts.append(rest.astype(jnp.bfloat16))
        rest = rest - parts[-1].astype(F32)
    out = lax.dot_general(
        jnp.concatenate(parts, axis=0),
        matrix,
        (((1,), (0,)), ((), ())),
        preferred_element_type=F32,
    )
    count = rows.shape[0]
    return out[:count] + (out[count : 2 * count] + out[2 * count :])


def sub_index():
    return lax.broadcasted_iota(jnp.int32, TILE, 0)


def lane_index():
    return lax.broadcasted_iota(jnp.int32, TILE, 1)


def turn(tile, by):
    by %= 8
    return pltpu.roll(tile, by, 0) if by else tile


def keep(where, tile):
    return jnp.where(where, tile, 0.0)


def inverse(tile):
    return jnp.where(tile > 0, 1.0 / jnp.where(tile > 0, tile, 1.0), 0.0)


def core():
    return lax.axis_index("group")


def flags():
    gx, gy = lax.axis_index("gx"), lax.axis_index("gy")
    x_last, y_last = lax.axis_size("gx") - 1, lax.axis_size("gy") - 1
    places = [gx > 0, gx < x_last, gy > 0, gy < y_last, gy > 1, gy < y_last - 1]
    return [place.astype(F32) for place in places]


def pair_rows(first, second):
    sub = sub_index()
    first, second = (tile + turn(tile, 7) for tile in (first, second))
    low = jnp.where(sub == 0, first, turn(first, 7))
    low = jnp.where(sub < 2, low, jnp.where(sub == 2, turn(first, 6), turn(first, 5)))
    high = jnp.where(sub == 4, turn(second, 4), turn(second, 3))
    high = jnp.where(sub < 6, high, jnp.where(sub == 6, turn(second, 2), turn(second, 1)))
    return jnp.where(sub < 4, low, high)


def plane_sums(fine):
    sub = sub_index()
    sums = [fine[2 * k] + fine[2 * k + 1] for k in range(8)]
    one = [pair_rows(sums[2 * k], sums[2 * k + 1]) for k in range(4)]
    two = None
    for k in range(4):
        both = one[k] + turn(one[k], 4)
        both = both + turn(both, 7)
        placed = jnp.where(sub == 2 * k, turn(both, 2 * k), turn(both, 2 * k - 1))
        two = placed if k == 0 else jnp.where(sub < 2 * k, two, placed)
    return one + [two]


def half_sums():
    row = lax.broadcasted_iota(jnp.int32, (128, 128), 0)
    column = lax.broadcasted_iota(jnp.int32, (128, 128), 1)
    matrix = jnp.concatenate([row >> 1 == column, row >> 2 == column], axis=1)
    return jnp.where(matrix, 1.0, 0.0).astype(jnp.bfloat16)


def first_kernel(m_whole, f_whole, out, m, f, arrived):
    copies = [
        pltpu.make_async_copy(source, target, arrived.at[k])
        for k, (source, target) in enumerate(((m_whole, m), (f_whole, f)))
    ]
    for copy in copies:
        copy.start()
    sums = half_sums()
    for copy in copies:
        copy.wait()
    m_tiles, f_tiles = ([ref[x] for x in range(16)] for ref in (m, f))
    for x in range(16):
        out[OWN["h0"] + x] = LEVEL[0] * f_tiles[x] / m_tiles[x]
        out[OWN["w"] + x] = m_tiles[x]
    rows = jnp.concatenate(plane_sums(m_tiles) + plane_sums(f_tiles), axis=0)
    total = exact_dot(rows, sums)
    upper = core() == 1
    for k in range(5):
        left, width = (0, 64) if k < 4 else (128, 32)
        weight, force = (
            total[row : row + 8, left : left + 128] for row in (8 * k, 40 + 8 * k)
        )
        weight = (0.125 if k < 4 else 0.125 * 0.125) * weight
        force = (0.5 * LEVEL[1] if k < 4 else 0.25 * LEVEL[2]) * force * inverse(weight)
        weight, force = (
            jnp.where(upper, pltpu.roll(tile, width, 1), tile) for tile in (weight, force)
        )
        out[(OWN["w1"] + k) if k < 4 else OWN["w2"]] = weight
        out[(OWN["h1"] + k) if k < 4 else OWN["h2"]] = force


def pack_x(fine, h1, h2, xp, at):
    upward = core() == 0
    start = jnp.where(upward, 12, 0)
    for k in range(4):
        for z in range(2):
            xp[at["h0"] + 2 * k + z] = fine(start + k, z)
    for k in range(2):
        xp[at["h1"] + k] = jnp.where(upward, h1[2 + k], h1[k])
    xp[at["h2"]] = h2


def first_sides_kernel(own, xp, coarse):
    total = [own[0, k] + own[1, k] for k in range(OWN["h1"], OWN["size"])]
    for k in range(COARSE["size"]):
        coarse[k] = total[k]
    h1, w1 = total[:4], total[4:8]
    h2, w2 = total[8:]
    pack_x(lambda x, z: own[z, x], h1, h2, xp, X_FIRST)
    upward = core() == 0
    edge = OWN["w"] + jnp.where(upward, 15, 0)
    for z in range(2):
        xp[X_FIRST["w"] + z] = own[z, edge]
    sub = sub_index()
    edge_one = jnp.where(upward, turn(w1[3], 4), w1[0])
    edge_two = jnp.where(upward, turn(w2, 6), turn(w2, 4))
    xp[X_FIRST["w12"]] = jnp.where(sub < 4, edge_one, edge_two)


def column_fine(own, planes, xr, at, lo, hi):
    def load(p, z):
        if p < planes:
            return xr[1, 0, at + 2 * p + z] * lo
        if p < 16 + planes:
            return own(p - planes, z)
        return xr[0, 1, at + 2 * (p - 16 - planes) + z] * hi

    return load


def pack_fine(load, planes, mine, yp, at):
    for k in range(planes // 2):
        for z in range(2):
            yp[at + 2 * k + z] = jnp.where(mine, load(2 * k, z), turn(load(2 * k + 1, z), 4))


def pack_y(own, h1, h2, xr, yp, y2p, x_at, at):
    lo, hi = flags()[:2]
    mine = (sub_index() < 4) == (core() == 1)
    pack_fine(column_fine(own, 4, xr, x_at["h0"], lo, hi), 24, mine, yp, at["h0"])
    for k in range(2):
        yp[at["h1"] + k] = xr[1, 0, x_at["h1"] + k] * lo
        yp[at["h1"] + 6 + k] = xr[0, 1, x_at["h1"] + k] * hi
    for k in range(4):
        yp[at["h1"] + 2 + k] = h1(k)
    two = [xr[1, 0, x_at["h2"]] * lo, h2(), xr[0, 1, x_at["h2"]] * hi]
    for k in range(3):
        yp[at["h2"] + k] = two[k]
        y2p[k] = two[k]


def first_rows_kernel(own, coarse, xr, yp, y2p):
    at = Y_FIRST
    pack_y(
        lambda x, z: own[z, x],
        lambda k: coarse[k],
        lambda: coarse[COARSE["h2"]],
        *(xr, yp, y2p, X_FIRST, at),
    )
    sub = sub_index()
    mine = (sub < 4) == (core() == 1)
    weights = column_fine(lambda x, z: own[z, OWN["w"] + x], 1, xr, X_FIRST["w"], 1.0, 1.0)
    pack_fine(weights, 18, mine, yp, at["w"])
    low, high = xr[1, 0, X_FIRST["w12"]], xr[0, 1, X_FIRST["w12"]]
    for k in range(4):
        yp[at["w1"] + k] = coarse[COARSE["w1"] + k]
    yp[at["w1"] + 4] = jnp.where(sub < 4, low, turn(high, 4))
    yp[at["w2"]] = coarse[COARSE["w2"]]
    yp[at["w2"] + 1] = jnp.where(sub < 2, turn(low, 4), turn(high, 6))


def second_rows_kernel(h0, h12, xr, yp, y2p):
    pack_y(
        lambda x, z: h0[x, z],
        lambda k: h12[k],
        lambda: h12[4],
        *(xr, yp, y2p, X_SECOND, Y_SECOND),
    )


def join_fine(load, planes, yr, at, ylo, yhi, out):
    sub = sub_index()
    for k in range(planes // 2):
        for z in range(2):
            above, below = yr[0, at + 2 * k + z] * yhi, yr[1, at + 2 * k + z] * ylo
            halos = (
                jnp.where(sub < 4, above, below),
                turn(jnp.where(sub < 4, below, above), 4),
            )
            for i in range(2):
                out[2 * k + i, z] = load(2 * k + i, z)
                out[2 * k + i, 2 + z] = halos[i]


def four_rows(own, above, below, i):
    sub = sub_index()
    turned = 4 * (1 - i)
    first = jnp.where(sub < 4, turn(own, 4 * i), turn(above, turned))
    return first, keep(sub >= 4, turn(below, turned))


def join_h1(yp, yr, at, out):
    ylo, yhi = flags()[2:4]
    for k in range(8):
        tile = at + k
        own, above, below = yp[tile], yr[0, tile] * yhi, yr[1, tile] * ylo
        for i in range(2):
            out[2 * k + i, 0], out[2 * k + i, 1] = four_rows(own, above, below, i)


def join_w1(yp, yr, out):
    for k in range(5):
        tile = Y_FIRST["w1"] + k
        own, above, below = yp[tile], yr[0, tile], yr[1, tile]
        for i in range(2):
            p = 9 * i if k == 4 else 1 + 2 * k + i
            first, second = four_rows(own, above, below, i)
            out[p, 0], out[p, 1] = 1.0 / first, inverse(second)


def join_h2(yp, yr, at, out):
    ylo, yhi, ylo2, yhi2 = flags()[2:]
    sub = sub_index()
    for k in range(3):
        tile, far = at["h2"] + k, at["far"] + k
        own, above, below = yp[tile], yr[0, tile] * yhi, yr[1, tile] * ylo
        above2, below2 = yr[0, far] * yhi2, yr[1, far] * ylo2
        for i in range(4):
            first = jnp.where(sub < 2, turn(own, -2 * i), turn(above, 2 - 2 * i))
            upper = keep(sub < 6, turn(above2, 4 - 2 * i))
            out[4 * k + i, 0] = jnp.where(sub < 4, first, upper)
            lower = jnp.where(sub < 6, turn(below2, 4 - 2 * i), turn(below, 6 - 2 * i))
            out[4 * k + i, 1] = keep(sub >= 4, lower)


def join_w2(yp, yr, out):
    sub = sub_index()
    for p in range(6):
        k, i = (1, p // 5) if p in (0, 5) else (0, p - 1)
        tile = Y_FIRST["w2"] + k
        own, above, below = yp[tile], yr[0, tile], yr[1, tile]
        first = jnp.where(sub < 2, turn(own, -2 * i), turn(above, 2 - 2 * i))
        out[p, 0] = inverse(keep(sub < 4, first))
        out[p, 1] = inverse(keep(sub >= 6, turn(below, 6 - 2 * i)))


def along_y(first, second):
    sub = sub_index()
    up_first, up_second = turn(first, 7), turn(second, 7)
    first = first + jnp.where(sub == 7, up_second, up_first)
    second = second + jnp.where(sub == 7, up_first, up_second)
    down_first, down_second = turn(first, 1), turn(second, 1)
    return (
        first + jnp.where(sub == 0, down_second, down_first),
        second + jnp.where(sub == 0, down_first, down_second),
    )


def along_z_fine(left, right):
    lane = lane_index()
    up_left, up_right = pltpu.roll(left, 127, 1), pltpu.roll(right, 127, 1)
    sum_left = left + jnp.where(lane < 127, up_left, up_right)
    sum_right = right + keep(lane < 127, up_right)
    down_left, down_right = pltpu.roll(sum_left, 1, 1), pltpu.roll(sum_right, 1, 1)
    return (
        sum_left + jnp.where(lane > 0, down_left, left),
        sum_right + jnp.where(lane > 0, down_right, down_left),
    )


def along_z_coarse(tile):
    lane = lane_index()
    summed = tile + keep(lane < 127, pltpu.roll(tile, 127, 1))
    return summed + jnp.where(lane > 0, pltpu.roll(summed, 1, 1), tile)


def along_yz(tiles):
    tiles = list(tiles)
    if len(tiles) == 4:
        for z in range(2):
            tiles[z], tiles[2 + z] = along_y(tiles[z], tiles[2 + z])
        for y in range(2):
            tiles[2 * y], tiles[2 * y + 1] = along_z_fine(tiles[2 * y], tiles[2 * y + 1])
        return tiles
    return [along_z_coarse(tile) for tile in along_y(*tiles)]


def added(first, second):
    return [a + b for a, b in zip(first, second)]


def relax(q, h, planes, parts, count, masks, lo, hi):
    sides = [[mask * factor for mask in masks] for factor in (lo, 1.0, hi)]

    def sweep(k, source):
        def load(x):
            return [source[x, part] for part in range(parts)]

        here = load(k)
        below = added(load(k - 1), here)
        for x in range(k, planes - k):
            after = load(x + 1)
            above = added(here, after)
            summed = along_yz(added(below, above))
            side = sides[0 if x < 4 else 2 if x >= planes - 4 else 1]
            for part in range(parts):
                spread = side[part // (parts // 2)] * summed[part]
                q[x, part] = (KEEP * here[part] + spread) + h[x, part]
            here, below = after, above

    @pl.when(count == 1)
    def _():
        q[...] = h[...]

    for k in range(1, 4):

        @pl.when(count > k)
        def _():
            sweep(k, h if k == 1 else q)


def relax_levels(counts, cycle, h0, q0, h1, q1, h2, q2):
    lo, hi, ylo, yhi, ylo2, yhi2 = [flag * 1.0 for flag in flags()]
    sub, lane = sub_index(), lane_index()
    spread = jnp.full(TILE, SPREAD, F32)
    above = jnp.where(sub < 2, 1.0, jnp.where(sub < 4, yhi, jnp.where(sub < 6, yhi2, 0.0)))
    below = jnp.where(sub < 4, 0.0, jnp.where(sub < 6, ylo2, ylo))
    masks2 = (keep(lane < 64, above * spread), keep(lane < 64, below * spread))
    masks1 = (jnp.where(sub < 4, 1.0, yhi) * spread, jnp.where(sub < 4, 0.0, ylo) * spread)
    masks0 = (spread, jnp.where(sub < 4, yhi, ylo) * spread)
    relax(q2, h2, 12, 2, counts[cycle, 2], masks2, lo, hi)
    relax(q1, h1, 16, 2, counts[cycle, 1], masks1, lo, hi)
    relax(q0, h0, 24, 4, counts[cycle, 0], masks0, lo, hi)


def corrections(q1, iw1, q2, iw2, copies):
    sub = sub_index()
    one, two = (
        [
            jnp.where(sub < 7, q[p + 3, 0] * iw[p, 0], q[p + 3, 1] * iw[p, 1])
            for p in range(planes)
        ]
        for q, iw, planes in ((q1, iw1, 10), (q2, iw2, 6))
    )
    spread = []
    for tile in two:
        inner = jnp.where(sub < 3, turn(tile, 1), turn(tile, 2))
        spread.append(jnp.where((sub == 0) | (sub == 7), tile, inner))
    rows = [jnp.concatenate([one[p], spread[(p + 1) // 2]], axis=1) for p in range(10)]
    return exact_dot(jnp.concatenate(rows, axis=0), copies[...])


def iterate(coarse, q0, w, before, out):
    sub = sub_index()
    for k in range(10):
        for z in range(2):
            tile = coarse[8 * k : 8 * k + 8, 128 * z : 128 * z + 128]
            turned = [tile] + [turn(tile, by) for by in range(1, 5)]
            rows = turned[4]
            for by, last in ((3, 6), (2, 4), (1, 2), (0, 0)):
                rows = jnp.where(sub <= last, turned[by], rows)
            halo = jnp.where(sub < 7, turned[4], tile)
            for p in (2 * k - 1, 2 * k):
                if 0 <= p < 18:
                    for part, value in ((z, rows), (2 + z, halo)):
                        total = q0[p + 3, part] + w[p, part] * value
                        if before is not None:
                            total = before[p, part] + total
                        out[p, part] = total


def defects(pf):
    def load(p):
        return [pf[p, part] for part in range(4)]

    here = load(1)
    below = added(load(0), here)
    for x in range(16):
        after = load(x + 2)
        above = added(here, after)
        summed = along_yz(added(below, above))
        yield here[:2], [SELF_WEIGHT * here[z] - SIDE_CUBE * summed[z] for z in range(2)]
        here, below = after, above


def middle_kernel(
    sweeps, own, coarse, xr, yp, yr, sums, copies,
    xp, pf, w, iw1, iw2, h0_next, h12_next,
    h0_all, q0, h1_all, q1, h2_all, q2, counts, arrived,
):
    counting = pltpu.make_async_copy(sweeps, counts, arrived)
    counting.start()
    lo, hi, ylo, yhi = flags()[:4]
    load = column_fine(lambda x, z: own[z, x], 4, xr, X_FIRST["h0"], lo, hi)
    join_fine(load, 24, yr, Y_FIRST["h0"], ylo, yhi, h0_all)
    load = column_fine(lambda x, z: own[z, OWN["w"] + x], 1, xr, X_FIRST["w"], 1.0, 1.0)
    join_fine(load, 18, yr, Y_FIRST["w"], 1.0, 1.0, w)
    join_h1(yp, yr, Y_FIRST["h1"], h1_all)
    join_w1(yp, yr, iw1)
    join_h2(yp, yr, Y_FIRST, h2_all)
    join_w2(yp, yr, iw2)
    counting.wait()
    relax_levels(counts, 0, h0_all, q0, h1_all, q1, h2_all, q2)
    iterate(corrections(q1, iw1, q2, iw2, copies), q0, w, None, pf)

    rests = [[], []]
    for x, (_, defect) in enumerate(defects(pf)):
        for z in range(2):
            h0 = own[z, x] - LEVEL[0] * defect[z]
            h0_next[x, z] = h0
            rests[z].append(own[z, OWN["w"] + x] * h0)
    summed = [plane_sums(rest) for rest in rests]
    rows = [jnp.concatenate([summed[0][k], summed[1][k]], axis=1) for k in range(5)]
    total = exact_dot(jnp.concatenate(rows, axis=0), sums[...])
    h1 = []
    for k in range(4):
        weight = coarse[COARSE["w1"] + k]
        h1.append(0.5 * LEVEL[1] / LEVEL[0] * total[8 * k : 8 * k + 8, :128] / weight)
        h12_next[k] = h1[k]
    weight = inverse(coarse[COARSE["w2"]])
    h2 = 0.25 * LEVEL[2] / LEVEL[0] * total[32:40, 128:] * weight
    h12_next[4] = h2
    pack_x(lambda x, z: h0_next[x, z], h1, h2, xp, X_SECOND)


def last_kernel(
    sweeps, m, f, h0, xr, yp, yr, pf, w, iw1, iw2, copies,
    solution_out, residual_out,
    h0_all, q0, h1_all, q1, h2_all, q2, counts, arrived, pf_all,
):
    counting = pltpu.make_async_copy(sweeps, counts, arrived)
    counting.start()
    lo, hi, ylo, yhi = flags()[:4]
    load = column_fine(lambda x, z: h0[x, z], 4, xr, X_SECOND["h0"], lo, hi)
    join_fine(load, 24, yr, Y_SECOND["h0"], ylo, yhi, h0_all)
    join_h1(yp, yr, Y_SECOND["h1"], h1_all)
    join_h2(yp, yr, Y_SECOND, h2_all)
    counting.wait()
    relax_levels(counts, 1, h0_all, q0, h1_all, q1, h2_all, q2)
    iterate(corrections(q1, iw1, q2, iw2, copies), q0, w, pf, pf_all)
    first = core() == 0
    for x, (here, defect) in enumerate(defects(pf_all)):
        mine, rest = (jnp.where(first, both[0], both[1]) for both in (here, defect))
        weight = m[x]
        solution_out[x] = mine / weight
        residual_out[x] = f[x] - weight * rest


def call(kernel, outs, scratch, name, *operands, outside=0):
    whole = pl.BlockSpec(memory_space=pltpu.HBM)
    vmem = pl.BlockSpec(memory_space=pltpu.VMEM)
    return pl.pallas_call(
        kernel,
        out_shape=[jax.ShapeDtypeStruct(shape, F32) for shape in outs],
        in_specs=[whole] * outside + [vmem] * (len(operands) - outside),
        out_specs=[vmem] * len(outs),
        scratch_shapes=scratch,
        compiler_params=pltpu.CompilerParams(vmem_limit_bytes=32 * 2**20),
        name=name,
    )(*operands)


def space(*dims):
    return pltpu.VMEM(tiles(*dims), F32)


def tiles(*dims):
    return (*dims, *TILE)


def pairs(axis, distance):
    size = lax.axis_size(axis)
    return [[i, size + (i + distance) % size] for i in range(size)]


def share(value):
    return lax.all_gather(value, "group", axis=0)


def trade_x(packed):
    both = lax.all_gather(packed, ("group", "gx"), axis=0, axis_index_groups=pairs("gx", 1))
    return share(both)


def swap(packed, distance):
    moves = [move for a, b in pairs("gy", distance) for move in ((a, b), (b, a))]
    return lax.ppermute(packed, ("group", "gy"), moves)


def trade_y(packed, packed_far):
    far = swap(packed_far, 2)
    near = swap(packed, 1)
    return share(jnp.concatenate([near, far], axis=0))


def on_device(forcing, metric, sweeps):
    sums, copies = (jnp.asarray(matrix, jnp.bfloat16) for matrix in (WHOLE_SUMS, COPIES))
    spaces = [space(24, 4)] * 2 + [space(16, 2)] * 2 + [space(12, 2)] * 2
    spaces += [pltpu.SMEM(sweeps.shape, jnp.int32), pltpu.SemaphoreType.DMA]

    (own,) = call(
        first_kernel,
        [tiles(OWN["size"])],
        [space(16), space(16), pltpu.SemaphoreType.DMA((2,))],
        "block_sums",
        *(metric, forcing),
        outside=2,
    )
    own = share(own)
    xp, coarse = call(
        first_sides_kernel,
        [tiles(X_FIRST["size"]), tiles(COARSE["size"])],
        [],
        "first_sides",
        own,
    )
    xr = trade_x(xp)
    yp, y2p = call(
        first_rows_kernel,
        [tiles(Y_FIRST["size"]), tiles(3)],
        [],
        "first_rows",
        *(own, coarse, xr),
    )
    yr = trade_y(yp, y2p)
    xp, pf, w, iw1, iw2, h0, h12 = call(
        middle_kernel,
        [
            *(tiles(X_SECOND["size"]), tiles(18, 4), tiles(18, 4), tiles(10, 2), tiles(6, 2)),
            *(tiles(16, 2), tiles(5)),
        ],
        spaces,
        "first_cycle",
        *(sweeps, own, coarse, xr, yp, yr, sums, copies),
        outside=1,
    )
    xr = trade_x(xp)
    yp, y2p = call(
        second_rows_kernel,
        [tiles(Y_SECOND["size"]), tiles(3)],
        [],
        "second_rows",
        *(h0, h12, xr),
    )
    yr = trade_y(yp, y2p)
    return call(
        last_kernel,
        [tiles(16), tiles(16)],
        [*spaces, space(18, 4)],
        "second_cycle",
        *(sweeps, metric, forcing, h0, xr, yp, yr, pf, w, iw1, iw2, copies),
        outside=1,
    )


def solution(mesh):
    def program(forcing, metric, sweeps):
        return tuple(on_device(forcing, metric, sweeps))

    return jax.shard_map(
        program,
        mesh=mesh,
        in_specs=(P("gx", "gy", "group"), P("gx", "gy", "group"), P()),
        out_specs=(P("gx", "gy", "group"), P("gx", "gy", "group")),
        check_vma=False,
    )
```

```python
import jax
import jax.numpy as jnp
import numpy as np
from jax import lax
from jax.experimental import pallas as pl
from jax.experimental.pallas import tpu as pltpu
from jax.sharding import PartitionSpec as P

RELAXATION = 0.8
SIDE_WEIGHT = 0.05 ** (1.0 / 3.0)
SELF_WEIGHT = 3.4
SIDE_CUBE = SIDE_WEIGHT**3

KEEP = 1.0 - RELAXATION * SELF_WEIGHT / 3.0
SPREAD = RELAXATION * SIDE_CUBE / 3.0
LEVEL = [RELAXATION / (3.0 * 4.0**-level) for level in range(3)]

F32 = jnp.float32
TILE = (8, 128)

OWN = dict(h0=0, w=16, h1=32, w1=36, h2=40, w2=41, size=42)
COARSE = dict(h1=0, w1=4, h2=8, w2=9, size=10)
X_FIRST = dict(h0=0, h1=8, h2=10, w=11, w12=13, size=14)
X_SECOND = dict(h0=0, h1=8, h2=10, size=11)
Y_FIRST = dict(h0=0, h1=24, h2=32, w=35, w1=53, w2=58, size=60, far=60)
Y_SECOND = dict(h0=0, h1=24, h2=32, size=35, far=35)

LANES = np.arange(256)
WHOLE_SUMS = np.concatenate(
    [LANES[:, None] // 2 == LANES[None, :128], LANES[:, None] // 4 == LANES[None, :128]], axis=1
).astype(np.float32)
COPIES = WHOLE_SUMS.T * np.where(LANES[:, None] < 128, 0.5, 0.25).astype(np.float32)


def exact_dot(rows, matrix):
    parts = []
    rest = rows
    for _ in range(3):
        parts.append(rest.astype(jnp.bfloat16))
        rest = rest - parts[-1].astype(F32)
    out = lax.dot_general(
        jnp.concatenate(parts, axis=0),
        matrix,
        (((1,), (0,)), ((), ())),
        preferred_element_type=F32,
    )
    count = rows.shape[0]
    return out[:count] + (out[count : 2 * count] + out[2 * count :])


def sub_index():
    return lax.broadcasted_iota(jnp.int32, TILE, 0)


def lane_index():
    return lax.broadcasted_iota(jnp.int32, TILE, 1)


def turn(tile, by):
    by %= 8
    return pltpu.roll(tile, by, 0) if by else tile


def keep(where, tile):
    return jnp.where(where, tile, 0.0)


def inverse(tile):
    return jnp.where(tile > 0, 1.0 / jnp.where(tile > 0, tile, 1.0), 0.0)


def core():
    return lax.axis_index("group")


def flags():
    gx, gy = lax.axis_index("gx"), lax.axis_index("gy")
    x_last, y_last = lax.axis_size("gx") - 1, lax.axis_size("gy") - 1
    places = [gx > 0, gx < x_last, gy > 0, gy < y_last, gy > 1, gy < y_last - 1]
    return [place.astype(F32) for place in places]


def pair_rows(first, second):
    sub = sub_index()
    first, second = (tile + turn(tile, 7) for tile in (first, second))
    low = jnp.where(sub == 0, first, turn(first, 7))
    low = jnp.where(sub < 2, low, jnp.where(sub == 2, turn(first, 6), turn(first, 5)))
    high = jnp.where(sub == 4, turn(second, 4), turn(second, 3))
    high = jnp.where(sub < 6, high, jnp.where(sub == 6, turn(second, 2), turn(second, 1)))
    return jnp.where(sub < 4, low, high)


def plane_sums(fine):
    sub = sub_index()
    sums = [fine[2 * k] + fine[2 * k + 1] for k in range(8)]
    one = [pair_rows(sums[2 * k], sums[2 * k + 1]) for k in range(4)]
    two = None
    for k in range(4):
        both = one[k] + turn(one[k], 4)
        both = both + turn(both, 7)
        placed = jnp.where(sub == 2 * k, turn(both, 2 * k), turn(both, 2 * k - 1))
        two = placed if k == 0 else jnp.where(sub < 2 * k, two, placed)
    return one + [two]


def half_sums():
    row = lax.broadcasted_iota(jnp.int32, (128, 128), 0)
    column = lax.broadcasted_iota(jnp.int32, (128, 128), 1)
    matrix = jnp.concatenate([row >> 1 == column, row >> 2 == column], axis=1)
    return jnp.where(matrix, 1.0, 0.0).astype(jnp.bfloat16)


def first_kernel(m_whole, f_whole, out, m, f, arrived):
    copies = [
        pltpu.make_async_copy(source, target, arrived.at[k])
        for k, (source, target) in enumerate(((m_whole, m), (f_whole, f)))
    ]
    for copy in copies:
        copy.start()
    sums = half_sums()
    for copy in copies:
        copy.wait()
    m_tiles, f_tiles = ([ref[x] for x in range(16)] for ref in (m, f))
    for x in range(16):
        out[OWN["h0"] + x] = LEVEL[0] * f_tiles[x] / m_tiles[x]
        out[OWN["w"] + x] = m_tiles[x]
    rows = jnp.concatenate(plane_sums(m_tiles) + plane_sums(f_tiles), axis=0)
    total = exact_dot(rows, sums)
    upper = core() == 1
    for k in range(5):
        left, width = (0, 64) if k < 4 else (128, 32)
        weight, force = (
            total[row : row + 8, left : left + 128] for row in (8 * k, 40 + 8 * k)
        )
        weight = (0.125 if k < 4 else 0.125 * 0.125) * weight
        force = (0.5 * LEVEL[1] if k < 4 else 0.25 * LEVEL[2]) * force * inverse(weight)
        weight, force = (
            jnp.where(upper, pltpu.roll(tile, width, 1), tile) for tile in (weight, force)
        )
        out[(OWN["w1"] + k) if k < 4 else OWN["w2"]] = weight
        out[(OWN["h1"] + k) if k < 4 else OWN["h2"]] = force


def pack_x(fine, h1, h2, xp, at):
    upward = core() == 0
    start = jnp.where(upward, 12, 0)
    for k in range(4):
        for z in range(2):
            xp[at["h0"] + 2 * k + z] = fine(start + k, z)
    for k in range(2):
        xp[at["h1"] + k] = jnp.where(upward, h1[2 + k], h1[k])
    xp[at["h2"]] = h2


def first_sides_kernel(own, xp, coarse):
    total = [own[0, k] + own[1, k] for k in range(OWN["h1"], OWN["size"])]
    for k in range(COARSE["size"]):
        coarse[k] = total[k]
    h1, w1 = total[:4], total[4:8]
    h2, w2 = total[8:]
    pack_x(lambda x, z: own[z, x], h1, h2, xp, X_FIRST)
    upward = core() == 0
    edge = OWN["w"] + jnp.where(upward, 15, 0)
    for z in range(2):
        xp[X_FIRST["w"] + z] = own[z, edge]
    sub = sub_index()
    edge_one = jnp.where(upward, turn(w1[3], 4), w1[0])
    edge_two = jnp.where(upward, turn(w2, 6), turn(w2, 4))
    xp[X_FIRST["w12"]] = jnp.where(sub < 4, edge_one, edge_two)


def column_fine(own, planes, xr, at, lo, hi):
    def load(p, z):
        if p < planes:
            return xr[1, at + 2 * p + z] * lo
        if p < 16 + planes:
            return own(p - planes, z)
        return xr[0, at + 2 * (p - 16 - planes) + z] * hi

    return load


def pack_fine(load, planes, mine, yp, at):
    for k in range(planes // 2):
        for z in range(2):
            yp[at + 2 * k + z] = jnp.where(mine, load(2 * k, z), turn(load(2 * k + 1, z), 4))


def pack_y(own, h1, h2, xr, yp, y2p, x_at, at):
    lo, hi = flags()[:2]
    mine = (sub_index() < 4) == (core() == 1)
    pack_fine(column_fine(own, 4, xr, x_at["h0"], lo, hi), 24, mine, yp, at["h0"])
    for k in range(2):
        yp[at["h1"] + k] = xr[1, x_at["h1"] + k] * lo
        yp[at["h1"] + 6 + k] = xr[0, x_at["h1"] + k] * hi
    for k in range(4):
        yp[at["h1"] + 2 + k] = h1(k)
    two = [xr[1, x_at["h2"]] * lo, h2(), xr[0, x_at["h2"]] * hi]
    for k in range(3):
        yp[at["h2"] + k] = two[k]
        y2p[k] = two[k]


def first_rows_kernel(own, coarse, xr, yp, y2p):
    at = Y_FIRST
    pack_y(
        lambda x, z: own[z, x],
        lambda k: coarse[k],
        lambda: coarse[COARSE["h2"]],
        *(xr, yp, y2p, X_FIRST, at),
    )
    sub = sub_index()
    mine = (sub < 4) == (core() == 1)
    weights = column_fine(lambda x, z: own[z, OWN["w"] + x], 1, xr, X_FIRST["w"], 1.0, 1.0)
    pack_fine(weights, 18, mine, yp, at["w"])
    low, high = xr[1, X_FIRST["w12"]], xr[0, X_FIRST["w12"]]
    for k in range(4):
        yp[at["w1"] + k] = coarse[COARSE["w1"] + k]
    yp[at["w1"] + 4] = jnp.where(sub < 4, low, turn(high, 4))
    yp[at["w2"]] = coarse[COARSE["w2"]]
    yp[at["w2"] + 1] = jnp.where(sub < 2, turn(low, 4), turn(high, 6))


def second_rows_kernel(h0, h12, xr, yp, y2p):
    pack_y(
        lambda x, z: h0[x, z],
        lambda k: h12[k],
        lambda: h12[4],
        *(xr, yp, y2p, X_SECOND, Y_SECOND),
    )


def join_fine(load, planes, yr, at, ylo, yhi, out):
    sub = sub_index()
    for k in range(planes // 2):
        for z in range(2):
            above, below = yr[0, at + 2 * k + z] * yhi, yr[1, at + 2 * k + z] * ylo
            halos = (
                jnp.where(sub < 4, above, below),
                turn(jnp.where(sub < 4, below, above), 4),
            )
            for i in range(2):
                out[2 * k + i, z] = load(2 * k + i, z)
                out[2 * k + i, 2 + z] = halos[i]


def four_rows(own, above, below, i):
    sub = sub_index()
    turned = 4 * (1 - i)
    first = jnp.where(sub < 4, turn(own, 4 * i), turn(above, turned))
    return first, keep(sub >= 4, turn(below, turned))


def join_h1(yp, yr, at, out):
    ylo, yhi = flags()[2:4]
    for k in range(8):
        tile = at + k
        own, above, below = yp[tile], yr[0, tile] * yhi, yr[1, tile] * ylo
        for i in range(2):
            out[2 * k + i, 0], out[2 * k + i, 1] = four_rows(own, above, below, i)


def join_w1(yp, yr, out):
    for k in range(5):
        tile = Y_FIRST["w1"] + k
        own, above, below = yp[tile], yr[0, tile], yr[1, tile]
        for i in range(2):
            p = 9 * i if k == 4 else 1 + 2 * k + i
            first, second = four_rows(own, above, below, i)
            out[p, 0], out[p, 1] = inverse(first), inverse(second)


def join_h2(yp, yr, at, out):
    ylo, yhi, ylo2, yhi2 = flags()[2:]
    sub = sub_index()
    for k in range(3):
        tile, far = at["h2"] + k, at["far"] + k
        own, above, below = yp[tile], yr[0, tile] * yhi, yr[1, tile] * ylo
        above2, below2 = yr[0, far + 3] * yhi2, yr[1, far] * ylo2
        for i in range(4):
            first = jnp.where(sub < 2, turn(own, -2 * i), turn(above, 2 - 2 * i))
            upper = keep(sub < 6, turn(above2, 4 - 2 * i))
            out[4 * k + i, 0] = jnp.where(sub < 4, first, upper)
            lower = jnp.where(sub < 6, turn(below2, 4 - 2 * i), turn(below, 6 - 2 * i))
            out[4 * k + i, 1] = keep(sub >= 4, lower)


def join_w2(yp, yr, out):
    sub = sub_index()
    for p in range(6):
        k, i = (1, p // 5) if p in (0, 5) else (0, p - 1)
        tile = Y_FIRST["w2"] + k
        own, above, below = yp[tile], yr[0, tile], yr[1, tile]
        first = jnp.where(sub < 2, turn(own, -2 * i), turn(above, 2 - 2 * i))
        out[p, 0] = inverse(keep(sub < 4, first))
        out[p, 1] = inverse(keep(sub >= 6, turn(below, 6 - 2 * i)))


def along_y(first, second):
    sub = sub_index()
    up_first, up_second = turn(first, 7), turn(second, 7)
    first = first + jnp.where(sub == 7, up_second, up_first)
    second = second + jnp.where(sub == 7, up_first, up_second)
    down_first, down_second = turn(first, 1), turn(second, 1)
    return (
        first + jnp.where(sub == 0, down_second, down_first),
        second + jnp.where(sub == 0, down_first, down_second),
    )


def along_z_fine(left, right):
    lane = lane_index()
    up_left, up_right = pltpu.roll(left, 127, 1), pltpu.roll(right, 127, 1)
    sum_left = left + jnp.where(lane < 127, up_left, up_right)
    sum_right = right + keep(lane < 127, up_right)
    down_left, down_right = pltpu.roll(sum_left, 1, 1), pltpu.roll(sum_right, 1, 1)
    return (
        sum_left + jnp.where(lane > 0, down_left, left),
        sum_right + jnp.where(lane > 0, down_right, down_left),
    )


def along_z_coarse(tile):
    lane = lane_index()
    summed = tile + keep(lane < 127, pltpu.roll(tile, 127, 1))
    return summed + jnp.where(lane > 0, pltpu.roll(summed, 1, 1), tile)


def along_yz(tiles):
    tiles = list(tiles)
    if len(tiles) == 4:
        for z in range(2):
            tiles[z], tiles[2 + z] = along_y(tiles[z], tiles[2 + z])
        for y in range(2):
            tiles[2 * y], tiles[2 * y + 1] = along_z_fine(tiles[2 * y], tiles[2 * y + 1])
        return tiles
    return [along_z_coarse(tile) for tile in along_y(*tiles)]


def added(first, second):
    return [a + b for a, b in zip(first, second)]


def relax(q, h, planes, parts, count, masks, lo, hi):
    sides = [[mask * factor for mask in masks] for factor in (lo, 1.0, hi)]

    def sweep(k, source):
        def load(x):
            return [source[x, part] for part in range(parts)]

        here = load(k)
        below = added(load(k - 1), here)
        for x in range(k, planes - k):
            after = load(x + 1)
            above = added(here, after)
            summed = along_yz(added(below, above))
            side = sides[0 if x < 4 else 2 if x >= planes - 4 else 1]
            for part in range(parts):
                spread = side[part // (parts // 2)] * summed[part]
                q[x, part] = (KEEP * here[part] + spread) + h[x, part]
            here, below = after, above

    @pl.when(count == 1)
    def _():
        q[...] = h[...]

    for k in range(1, 4):

        @pl.when(count > k)
        def _():
            sweep(k, h if k == 1 else q)


def relax_levels(counts, cycle, h0, q0, h1, q1, h2, q2):
    lo, hi, ylo, yhi, ylo2, yhi2 = [flag * 1.0 for flag in flags()]
    sub, lane = sub_index(), lane_index()
    spread = jnp.full(TILE, SPREAD, F32)
    above = jnp.where(sub < 2, 1.0, jnp.where(sub < 4, yhi, jnp.where(sub < 6, yhi2, 0.0)))
    below = jnp.where(sub < 4, 0.0, jnp.where(sub < 6, ylo2, ylo))
    masks2 = (keep(lane < 64, above * spread), keep(lane < 64, below * spread))
    masks1 = (jnp.where(sub < 4, 1.0, yhi) * spread, jnp.where(sub < 4, 0.0, ylo) * spread)
    masks0 = (spread, jnp.where(sub < 4, yhi, ylo) * spread)
    relax(q2, h2, 12, 2, counts[cycle, 2], masks2, lo, hi)
    relax(q1, h1, 16, 2, counts[cycle, 1], masks1, lo, hi)
    relax(q0, h0, 24, 4, counts[cycle, 0], masks0, lo, hi)


def corrections(q1, iw1, q2, iw2, copies):
    sub = sub_index()
    one, two = (
        [
            jnp.where(sub < 7, q[p + 3, 0] * iw[p, 0], q[p + 3, 1] * iw[p, 1])
            for p in range(planes)
        ]
        for q, iw, planes in ((q1, iw1, 10), (q2, iw2, 6))
    )
    spread = []
    for tile in two:
        inner = jnp.where(sub < 3, turn(tile, 1), turn(tile, 2))
        spread.append(jnp.where((sub == 0) | (sub == 7), tile, inner))
    rows = [jnp.concatenate([one[p], spread[(p + 1) // 2]], axis=1) for p in range(10)]
    return exact_dot(jnp.concatenate(rows, axis=0), copies[...])


def iterate(coarse, q0, w, before, out):
    sub = sub_index()
    for k in range(10):
        for z in range(2):
            tile = coarse[8 * k : 8 * k + 8, 128 * z : 128 * z + 128]
            turned = [tile] + [turn(tile, by) for by in range(1, 5)]
            rows = turned[4]
            for by, last in ((3, 6), (2, 4), (1, 2), (0, 0)):
                rows = jnp.where(sub <= last, turned[by], rows)
            halo = jnp.where(sub < 7, turned[4], tile)
            for p in (2 * k - 1, 2 * k):
                if 0 <= p < 18:
                    for part, value in ((z, rows), (2 + z, halo)):
                        total = q0[p + 3, part] + w[p, part] * value
                        if before is not None:
                            total = before[p, part] + total
                        out[p, part] = total


def defects(pf):
    def load(p):
        return [pf[p, part] for part in range(4)]

    here = load(1)
    below = added(load(0), here)
    for x in range(16):
        after = load(x + 2)
        above = added(here, after)
        summed = along_yz(added(below, above))
        yield here[:2], [SELF_WEIGHT * here[z] - SIDE_CUBE * summed[z] for z in range(2)]
        here, below = after, above


def middle_kernel(
    sweeps, own, coarse, xr, yp, yr, sums, copies,
    xp, pf, w, iw1, iw2, h0_next, h12_next,
    h0_all, q0, h1_all, q1, h2_all, q2, counts, arrived,
):
    counting = pltpu.make_async_copy(sweeps, counts, arrived)
    counting.start()
    lo, hi, ylo, yhi = flags()[:4]
    load = column_fine(lambda x, z: own[z, x], 4, xr, X_FIRST["h0"], lo, hi)
    join_fine(load, 24, yr, Y_FIRST["h0"], ylo, yhi, h0_all)
    load = column_fine(lambda x, z: own[z, OWN["w"] + x], 1, xr, X_FIRST["w"], 1.0, 1.0)
    join_fine(load, 18, yr, Y_FIRST["w"], 1.0, 1.0, w)
    join_h1(yp, yr, Y_FIRST["h1"], h1_all)
    join_w1(yp, yr, iw1)
    join_h2(yp, yr, Y_FIRST, h2_all)
    join_w2(yp, yr, iw2)
    counting.wait()
    relax_levels(counts, 0, h0_all, q0, h1_all, q1, h2_all, q2)
    iterate(corrections(q1, iw1, q2, iw2, copies), q0, w, None, pf)

    rests = [[], []]
    for x, (_, defect) in enumerate(defects(pf)):
        for z in range(2):
            h0 = own[z, x] - LEVEL[0] * defect[z]
            h0_next[x, z] = h0
            rests[z].append(own[z, OWN["w"] + x] * h0)
    summed = [plane_sums(rest) for rest in rests]
    rows = [jnp.concatenate([summed[0][k], summed[1][k]], axis=1) for k in range(5)]
    total = exact_dot(jnp.concatenate(rows, axis=0), sums[...])
    h1 = []
    for k in range(4):
        weight = coarse[COARSE["w1"] + k]
        h1.append(0.5 * LEVEL[1] / LEVEL[0] * total[8 * k : 8 * k + 8, :128] / weight)
        h12_next[k] = h1[k]
    weight = inverse(coarse[COARSE["w2"]])
    h2 = 0.25 * LEVEL[2] / LEVEL[0] * total[32:40, 128:] * weight
    h12_next[4] = h2
    pack_x(lambda x, z: h0_next[x, z], h1, h2, xp, X_SECOND)


def last_kernel(
    sweeps, m, f, h0, xr, yp, yr, pf, w, iw1, iw2, copies,
    solution_out, residual_out,
    h0_all, q0, h1_all, q1, h2_all, q2, counts, arrived, pf_all,
):
    counting = pltpu.make_async_copy(sweeps, counts, arrived)
    counting.start()
    lo, hi, ylo, yhi = flags()[:4]
    load = column_fine(lambda x, z: h0[x, z], 4, xr, X_SECOND["h0"], lo, hi)
    join_fine(load, 24, yr, Y_SECOND["h0"], ylo, yhi, h0_all)
    join_h1(yp, yr, Y_SECOND["h1"], h1_all)
    join_h2(yp, yr, Y_SECOND, h2_all)
    counting.wait()
    relax_levels(counts, 1, h0_all, q0, h1_all, q1, h2_all, q2)
    iterate(corrections(q1, iw1, q2, iw2, copies), q0, w, pf, pf_all)
    first = core() == 0
    for x, (here, defect) in enumerate(defects(pf_all)):
        mine, rest = (jnp.where(first, both[0], both[1]) for both in (here, defect))
        weight = m[x]
        solution_out[x] = mine / weight
        residual_out[x] = f[x] - weight * rest


def call(kernel, outs, scratch, name, *operands, outside=0):
    whole = pl.BlockSpec(memory_space=pltpu.HBM)
    vmem = pl.BlockSpec(memory_space=pltpu.VMEM)
    return pl.pallas_call(
        kernel,
        out_shape=[jax.ShapeDtypeStruct(shape, F32) for shape in outs],
        in_specs=[whole] * outside + [vmem] * (len(operands) - outside),
        out_specs=[vmem] * len(outs),
        scratch_shapes=scratch,
        compiler_params=pltpu.CompilerParams(vmem_limit_bytes=32 * 2**20),
        name=name,
    )(*(pltpu.with_memory_space_constraint(x, pltpu.HBM) for x in operands[:outside]), *operands[outside:])


def space(*dims):
    return pltpu.VMEM(tiles(*dims), F32)


def tiles(*dims):
    return (*dims, *TILE)


def pairs(axis, distance):
    size = lax.axis_size(axis)
    return [[i, size + i + distance] for i in range(size - distance)]


def share(value):
    return lax.all_gather(value, "group", axis=0)


def swap(packed, axis):
    moves = [move for a, b in pairs(axis, 1) for move in ((a, b), (b, a))]
    return lax.ppermute(packed, ("group", axis), moves)


def trade_x(packed):
    return share(swap(packed, "gx"))


def trade_y(packed, packed_far):
    near = swap(packed, "gy")
    size = lax.axis_size("gy")
    groups = [*pairs("gy", 2), [size - 2, size - 1], [size, size + 1]]
    far = lax.all_gather(packed_far, ("group", "gy"), axis=0, tiled=True, axis_index_groups=groups)
    return share(jnp.concatenate([near, far], axis=0))


def on_device(forcing, metric, sweeps):
    sums, copies = (jnp.asarray(matrix, jnp.bfloat16) for matrix in (WHOLE_SUMS, COPIES))
    spaces = [space(24, 4)] * 2 + [space(16, 2)] * 2 + [space(12, 2)] * 2
    spaces += [pltpu.SMEM(sweeps.shape, jnp.int32), pltpu.SemaphoreType.DMA]

    (own,) = call(
        first_kernel,
        [tiles(OWN["size"])],
        [space(16), space(16), pltpu.SemaphoreType.DMA((2,))],
        "block_sums",
        *(metric, forcing),
        outside=2,
    )
    own = share(own)
    xp, coarse = call(
        first_sides_kernel,
        [tiles(X_FIRST["size"]), tiles(COARSE["size"])],
        [],
        "first_sides",
        own,
    )
    xr = trade_x(xp)
    yp, y2p = call(
        first_rows_kernel,
        [tiles(Y_FIRST["size"]), tiles(3)],
        [],
        "first_rows",
        *(own, coarse, xr),
    )
    yr = trade_y(yp, y2p)
    xp, pf, w, iw1, iw2, h0, h12 = call(
        middle_kernel,
        [
            *(tiles(X_SECOND["size"]), tiles(18, 4), tiles(18, 4), tiles(10, 2), tiles(6, 2)),
            *(tiles(16, 2), tiles(5)),
        ],
        spaces,
        "first_cycle",
        *(sweeps, own, coarse, xr, yp, yr, sums, copies),
        outside=1,
    )
    xr = trade_x(xp)
    yp, y2p = call(
        second_rows_kernel,
        [tiles(Y_SECOND["size"]), tiles(3)],
        [],
        "second_rows",
        *(h0, h12, xr),
    )
    yr = trade_y(yp, y2p)
    return call(
        last_kernel,
        [tiles(16), tiles(16)],
        [*spaces, space(18, 4)],
        "second_cycle",
        *(sweeps, metric, forcing, h0, xr, yp, yr, pf, w, iw1, iw2, copies),
        outside=1,
    )


def solution(mesh):
    def program(forcing, metric, sweeps):
        return tuple(on_device(forcing, metric, sweeps))

    return jax.shard_map(
        program,
        mesh=mesh,
        in_specs=(P("gx", "gy", "group"), P("gx", "gy", "group"), P()),
        out_specs=(P("gx", "gy", "group"), P("gx", "gy", "group")),
        check_vma=False,
    )
```

```python
import jax
import jax.numpy as jnp
import numpy as np
from jax import lax
from jax.experimental import pallas as pl
from jax.experimental.pallas import tpu as pltpu
from jax.sharding import PartitionSpec as P

RELAXATION = 0.8
SIDE_WEIGHT = 0.05 ** (1.0 / 3.0)
SELF_WEIGHT = 3.4
SIDE_CUBE = SIDE_WEIGHT**3

KEEP = 1.0 - RELAXATION * SELF_WEIGHT / 3.0
SPREAD = RELAXATION * SIDE_CUBE / 3.0
LEVEL = [RELAXATION / (3.0 * 4.0**-level) for level in range(3)]

F32 = jnp.float32
TILE = (8, 128)

OWN = dict(h0=0, w=16, h1=32, w1=36, h2=40, w2=41, counts=42, size=43)
COARSE = dict(h1=0, w1=4, h2=8, w2=9, size=10)
X_FIRST = dict(h0=0, h1=8, h2=10, w=11, w12=13, size=14)
X_SECOND = dict(h0=0, h1=8, h2=10, size=11)
Y_FIRST = dict(h0=0, h1=24, h2=32, w=35, w1=53, w2=58, size=60, far=60)
Y_SECOND = dict(h0=0, h1=24, h2=32, size=35, far=35)

LANES = np.arange(256)
WHOLE_SUMS = np.concatenate(
    [LANES[:, None] // 2 == LANES[None, :128], LANES[:, None] // 4 == LANES[None, :128]], axis=1
).astype(np.float32)
COPIES = WHOLE_SUMS.T * np.where(LANES[:, None] < 128, 0.5, 0.25).astype(np.float32)


def exact_dot(rows, matrix):
    parts = []
    rest = rows
    for _ in range(3):
        parts.append(rest.astype(jnp.bfloat16))
        rest = rest - parts[-1].astype(F32)
    out = lax.dot_general(
        jnp.concatenate(parts, axis=0),
        matrix,
        (((1,), (0,)), ((), ())),
        preferred_element_type=F32,
    )
    count = rows.shape[0]
    return out[:count] + (out[count : 2 * count] + out[2 * count :])


def sub_index():
    return lax.broadcasted_iota(jnp.int32, TILE, 0)


def lane_index():
    return lax.broadcasted_iota(jnp.int32, TILE, 1)


def turn(tile, by):
    by %= 8
    return pltpu.roll(tile, by, 0) if by else tile


def keep(where, tile):
    return jnp.where(where, tile, 0.0)


def inverse(tile):
    return jnp.where(tile > 0, 1.0 / jnp.where(tile > 0, tile, 1.0), 0.0)


def core():
    return lax.axis_index("group")


def flags():
    gx, gy = lax.axis_index("gx"), lax.axis_index("gy")
    x_last, y_last = lax.axis_size("gx") - 1, lax.axis_size("gy") - 1
    places = [gx > 0, gx < x_last, gy > 0, gy < y_last, gy > 1, gy < y_last - 1]
    return [place.astype(F32) for place in places]


def pair_rows(first, second):
    sub = sub_index()
    first, second = (tile + turn(tile, 7) for tile in (first, second))
    low = jnp.where(sub == 0, first, turn(first, 7))
    low = jnp.where(sub < 2, low, jnp.where(sub == 2, turn(first, 6), turn(first, 5)))
    high = jnp.where(sub == 4, turn(second, 4), turn(second, 3))
    high = jnp.where(sub < 6, high, jnp.where(sub == 6, turn(second, 2), turn(second, 1)))
    return jnp.where(sub < 4, low, high)


def plane_sums(fine):
    sub = sub_index()
    sums = [fine[2 * k] + fine[2 * k + 1] for k in range(8)]
    one = [pair_rows(sums[2 * k], sums[2 * k + 1]) for k in range(4)]
    two = None
    for k in range(4):
        both = one[k] + turn(one[k], 4)
        both = both + turn(both, 7)
        placed = jnp.where(sub == 2 * k, turn(both, 2 * k), turn(both, 2 * k - 1))
        two = placed if k == 0 else jnp.where(sub < 2 * k, two, placed)
    return one + [two]


def half_sums():
    row = lax.broadcasted_iota(jnp.int32, (128, 128), 0)
    column = lax.broadcasted_iota(jnp.int32, (128, 128), 1)
    matrix = jnp.concatenate([row >> 1 == column, row >> 2 == column], axis=1)
    return jnp.where(matrix, 1.0, 0.0).astype(jnp.bfloat16)


def first_kernel(m_whole, f_whole, sweeps_whole, out, m, f, sweeps, arrived):
    moves = ((m_whole, m), (f_whole, f), (sweeps_whole, sweeps))
    copies = [
        pltpu.make_async_copy(source, target, arrived.at[k])
        for k, (source, target) in enumerate(moves)
    ]
    for copy in copies:
        copy.start()
    sums = half_sums()
    for copy in copies:
        copy.wait()
    m_tiles, f_tiles = ([ref[x] for x in range(16)] for ref in (m, f))
    for x in range(16):
        out[OWN["h0"] + x] = LEVEL[0] * f_tiles[x] / m_tiles[x]
        out[OWN["w"] + x] = m_tiles[x]
    rows = jnp.concatenate(plane_sums(m_tiles) + plane_sums(f_tiles), axis=0)
    total = exact_dot(rows, sums)
    out[OWN["counts"]] = jnp.zeros(TILE, F32)
    out[OWN["counts"], : sweeps.shape[0], : sweeps.shape[1]] = sweeps[...].astype(F32)
    upper = core() == 1
    for k in range(5):
        left, width = (0, 64) if k < 4 else (128, 32)
        weight, force = (
            total[row : row + 8, left : left + 128] for row in (8 * k, 40 + 8 * k)
        )
        weight = (0.125 if k < 4 else 0.125 * 0.125) * weight
        force = (0.5 * LEVEL[1] if k < 4 else 0.25 * LEVEL[2]) * force * inverse(weight)
        weight, force = (
            jnp.where(upper, pltpu.roll(tile, width, 1), tile) for tile in (weight, force)
        )
        out[(OWN["w1"] + k) if k < 4 else OWN["w2"]] = weight
        out[(OWN["h1"] + k) if k < 4 else OWN["h2"]] = force


def pack_x(fine, h1, h2, xp, at):
    upward = core() == 0
    start = jnp.where(upward, 12, 0)
    for k in range(4):
        for z in range(2):
            xp[at["h0"] + 2 * k + z] = fine(start + k, z)
    for k in range(2):
        xp[at["h1"] + k] = jnp.where(upward, h1[2 + k], h1[k])
    xp[at["h2"]] = h2


def first_sides_kernel(own, xp, coarse):
    total = [own[0, k] + own[1, k] for k in range(OWN["h1"], OWN["counts"])]
    for k in range(COARSE["size"]):
        coarse[k] = total[k]
    h1, w1 = total[:4], total[4:8]
    h2, w2 = total[8:]
    pack_x(lambda x, z: own[z, x], h1, h2, xp, X_FIRST)
    upward = core() == 0
    edge = OWN["w"] + jnp.where(upward, 15, 0)
    for z in range(2):
        xp[X_FIRST["w"] + z] = own[z, edge]
    sub = sub_index()
    edge_one = jnp.where(upward, turn(w1[3], 4), w1[0])
    edge_two = jnp.where(upward, turn(w2, 6), turn(w2, 4))
    xp[X_FIRST["w12"]] = jnp.where(sub < 4, edge_one, edge_two)


def column_fine(own, planes, xr, at, lo, hi):
    def load(p, z):
        if p < planes:
            return xr[1, at + 2 * p + z] * lo
        if p < 16 + planes:
            return own(p - planes, z)
        return xr[0, at + 2 * (p - 16 - planes) + z] * hi

    return load


def pack_fine(load, planes, mine, yp, at):
    for k in range(planes // 2):
        for z in range(2):
            yp[at + 2 * k + z] = jnp.where(mine, load(2 * k, z), turn(load(2 * k + 1, z), 4))


def pack_y(own, h1, h2, xr, yp, y2p, x_at, at):
    lo, hi = flags()[:2]
    mine = (sub_index() < 4) == (core() == 1)
    pack_fine(column_fine(own, 4, xr, x_at["h0"], lo, hi), 24, mine, yp, at["h0"])
    for k in range(2):
        yp[at["h1"] + k] = xr[1, x_at["h1"] + k] * lo
        yp[at["h1"] + 6 + k] = xr[0, x_at["h1"] + k] * hi
    for k in range(4):
        yp[at["h1"] + 2 + k] = h1(k)
    two = [xr[1, x_at["h2"]] * lo, h2(), xr[0, x_at["h2"]] * hi]
    for k in range(3):
        yp[at["h2"] + k] = two[k]
        y2p[k] = two[k]


def first_rows_kernel(own, coarse, xr, yp, y2p):
    at = Y_FIRST
    pack_y(
        lambda x, z: own[z, x],
        lambda k: coarse[k],
        lambda: coarse[COARSE["h2"]],
        *(xr, yp, y2p, X_FIRST, at),
    )
    sub = sub_index()
    mine = (sub < 4) == (core() == 1)
    weights = column_fine(lambda x, z: own[z, OWN["w"] + x], 1, xr, X_FIRST["w"], 1.0, 1.0)
    pack_fine(weights, 18, mine, yp, at["w"])
    low, high = xr[1, X_FIRST["w12"]], xr[0, X_FIRST["w12"]]
    for k in range(4):
        yp[at["w1"] + k] = coarse[COARSE["w1"] + k]
    yp[at["w1"] + 4] = jnp.where(sub < 4, low, turn(high, 4))
    yp[at["w2"]] = coarse[COARSE["w2"]]
    yp[at["w2"] + 1] = jnp.where(sub < 2, turn(low, 4), turn(high, 6))


def second_rows_kernel(h0, h12, xr, yp, y2p):
    pack_y(
        lambda x, z: h0[x, z],
        lambda k: h12[k],
        lambda: h12[4],
        *(xr, yp, y2p, X_SECOND, Y_SECOND),
    )


def join_fine(load, planes, yr, at, ylo, yhi, *outs):
    sub = sub_index()
    for k in range(planes // 2):
        for z in range(2):
            above, below = yr[0, at + 2 * k + z] * yhi, yr[1, at + 2 * k + z] * ylo
            halos = (
                jnp.where(sub < 4, above, below),
                turn(jnp.where(sub < 4, below, above), 4),
            )
            for i in range(2):
                own = load(2 * k + i, z)
                for out in outs:
                    out[2 * k + i, z] = own
                    out[2 * k + i, 2 + z] = halos[i]


def four_rows(own, above, below, i):
    sub = sub_index()
    turned = 4 * (1 - i)
    first = jnp.where(sub < 4, turn(own, 4 * i), turn(above, turned))
    return first, keep(sub >= 4, turn(below, turned))


def join_h1(yp, yr, at, *outs):
    ylo, yhi = flags()[2:4]
    for k in range(8):
        tile = at + k
        own, above, below = yp[tile], yr[0, tile] * yhi, yr[1, tile] * ylo
        for i in range(2):
            both = four_rows(own, above, below, i)
            for out in outs:
                out[2 * k + i, 0], out[2 * k + i, 1] = both


def join_w1(yp, yr, out):
    for k in range(5):
        tile = Y_FIRST["w1"] + k
        own, above, below = yp[tile], yr[0, tile], yr[1, tile]
        for i in range(2):
            p = 9 * i if k == 4 else 1 + 2 * k + i
            first, second = four_rows(own, above, below, i)
            out[p, 0], out[p, 1] = inverse(first), inverse(second)


def join_h2(yp, yr, at, *outs):
    ylo, yhi, ylo2, yhi2 = flags()[2:]
    sub = sub_index()
    for k in range(3):
        tile, far = at["h2"] + k, at["far"] + k
        own, above, below = yp[tile], yr[0, tile] * yhi, yr[1, tile] * ylo
        above2, below2 = yr[0, far + 3] * yhi2, yr[1, far] * ylo2
        for i in range(4):
            first = jnp.where(sub < 2, turn(own, -2 * i), turn(above, 2 - 2 * i))
            upper = keep(sub < 6, turn(above2, 4 - 2 * i))
            lower = jnp.where(sub < 6, turn(below2, 4 - 2 * i), turn(below, 6 - 2 * i))
            for out in outs:
                out[4 * k + i, 0] = jnp.where(sub < 4, first, upper)
                out[4 * k + i, 1] = keep(sub >= 4, lower)


def join_w2(yp, yr, out):
    sub = sub_index()
    for p in range(6):
        k, i = (1, p // 5) if p in (0, 5) else (0, p - 1)
        tile = Y_FIRST["w2"] + k
        own, above, below = yp[tile], yr[0, tile], yr[1, tile]
        first = jnp.where(sub < 2, turn(own, -2 * i), turn(above, 2 - 2 * i))
        out[p, 0] = inverse(keep(sub < 4, first))
        out[p, 1] = inverse(keep(sub >= 6, turn(below, 6 - 2 * i)))


def along_y(first, second):
    sub = sub_index()
    up_first, up_second = turn(first, 7), turn(second, 7)
    down_first, down_second = turn(first, 1), turn(second, 1)
    sides_first = jnp.where(sub == 7, up_second, up_first) + jnp.where(sub == 0, down_second, down_first)
    sides_second = jnp.where(sub == 7, up_first, up_second) + jnp.where(sub == 0, down_first, down_second)
    return (first + first) + sides_first, (second + second) + sides_second


def along_z_fine(left, right):
    lane = lane_index()
    up_left, up_right = pltpu.roll(left, 127, 1), pltpu.roll(right, 127, 1)
    down_left, down_right = pltpu.roll(left, 1, 1), pltpu.roll(right, 1, 1)
    sides_left = jnp.where(lane < 127, up_left, up_right) + keep(lane > 0, down_left)
    sides_right = keep(lane < 127, up_right) + jnp.where(lane > 0, down_right, down_left)
    return (left + left) + sides_left, (right + right) + sides_right


def along_z_coarse(tile):
    lane = lane_index()
    sides = keep(lane < 127, pltpu.roll(tile, 127, 1)) + keep(lane > 0, pltpu.roll(tile, 1, 1))
    return (tile + tile) + sides


def along_yz(tiles):
    tiles = list(tiles)
    if len(tiles) == 4:
        for z in range(2):
            tiles[z], tiles[2 + z] = along_y(tiles[z], tiles[2 + z])
        for y in range(2):
            tiles[2 * y], tiles[2 * y + 1] = along_z_fine(tiles[2 * y], tiles[2 * y + 1])
        return tiles
    return [along_z_coarse(tile) for tile in along_y(*tiles)]


def added(first, second):
    return [a + b for a, b in zip(first, second)]


def relax_planes(q, h, start, planes, parts, before, masks, factors, active):
    def load(x):
        return [q[x, part] for part in range(parts)]

    kept = KEEP if active is None else 1.0 + active * (KEEP - 1.0)
    here = load(start)
    below = added(before, here)
    for i in range(planes):
        x = start + i
        after = load(x + 1)
        above = added(here, after)
        summed = along_yz(added(below, above))
        for part in range(parts):
            spread = (masks[part // (parts // 2)] * factors[i]) * summed[part]
            source = h[x, part] if active is None else active * h[x, part]
            q[x, part] = (kept * here[part] + spread) + source
        last, here, below = here, after, above
    return last


def relax_levels(counts, h0, q0, h1, q1, h2, q2):
    lo, hi, ylo, yhi, ylo2, yhi2 = flags()
    sub, lane = sub_index(), lane_index()
    spread = jnp.full(TILE, SPREAD, F32)
    above = jnp.where(sub < 2, 1.0, jnp.where(sub < 4, yhi, jnp.where(sub < 6, yhi2, 0.0)))
    below = jnp.where(sub < 4, 0.0, jnp.where(sub < 6, ylo2, ylo))
    masks2 = (keep(lane < 64, above * spread), keep(lane < 64, below * spread))
    masks1 = (jnp.where(sub < 4, 1.0, yhi) * spread, jnp.where(sub < 4, 0.0, ylo) * spread)
    masks0 = (spread, jnp.where(sub < 4, yhi, ylo) * spread)

    def coarse_sweep(k, _):
        for q, h, planes, masks, count in ((q2, h2, 12, masks2, counts[2]), (q1, h1, 16, masks1, counts[1])):
            active = jnp.where(count > k, 1.0, 0.0)
            factors = [active * lo] * 3 + [active] * (planes - 8) + [active * hi] * 3
            before = [q[0, part] for part in range(2)]
            relax_planes(q, h, 1, planes - 2, 2, before, masks, factors, active)
        return 0

    def fine_sweep(_, __):
        def half(j, before):
            start = 1 + 11 * j
            factors = [
                jnp.where(start + i < 4, lo, jnp.where(start + i >= 20, hi, 1.0)) for i in range(11)
            ]
            return tuple(relax_planes(q0, h0, start, 11, 4, list(before), masks0, factors, None))

        lax.fori_loop(0, 2, half, tuple(q0[0, part] for part in range(4)))
        return 0

    lax.fori_loop(1, jnp.maximum(counts[1], counts[2]), coarse_sweep, 0)
    lax.fori_loop(1, counts[0], fine_sweep, 0)


def sweep_counts(own, cycle):
    held, sub, lane = own[0, OWN["counts"]], sub_index(), lane_index()
    return [
        jnp.max(keep((sub == cycle) & (lane == level), held)).astype(jnp.int32) for level in range(3)
    ]


def corrections(q1, iw1, q2, iw2, copies):
    sub = sub_index()
    one, two = (
        [
            jnp.where(sub < 7, q[p + 3, 0] * iw[p, 0], q[p + 3, 1] * iw[p, 1])
            for p in range(planes)
        ]
        for q, iw, planes in ((q1, iw1, 10), (q2, iw2, 6))
    )
    spread = []
    for tile in two:
        inner = jnp.where(sub < 3, turn(tile, 1), turn(tile, 2))
        spread.append(jnp.where((sub == 0) | (sub == 7), tile, inner))
    rows = [jnp.concatenate([one[p], spread[(p + 1) // 2]], axis=1) for p in range(10)]
    return exact_dot(jnp.concatenate(rows, axis=0), copies[...])


def iterate(coarse, q0, w, before, out):
    sub = sub_index()
    for k in range(10):
        for z in range(2):
            tile = coarse[8 * k : 8 * k + 8, 128 * z : 128 * z + 128]
            turned = [tile] + [turn(tile, by) for by in range(1, 5)]
            rows = turned[4]
            for by, last in ((3, 6), (2, 4), (1, 2), (0, 0)):
                rows = jnp.where(sub <= last, turned[by], rows)
            halo = jnp.where(sub < 7, turned[4], tile)
            for p in (2 * k - 1, 2 * k):
                if 0 <= p < 18:
                    for part, value in ((z, rows), (2 + z, halo)):
                        total = q0[p + 3, part] + w[p, part] * value
                        if before is not None:
                            total = before[p, part] + total
                        out[p, part] = total


def defects(pf):
    def load(p):
        return [pf[p, part] for part in range(4)]

    here = load(1)
    below = added(load(0), here)
    for x in range(16):
        after = load(x + 2)
        above = added(here, after)
        summed = along_yz(added(below, above))
        yield here[:2], [SELF_WEIGHT * here[z] - SIDE_CUBE * summed[z] for z in range(2)]
        here, below = after, above


def middle_kernel(
    own, coarse, xr, yp, yr, sums, copies,
    xp, pf, w, iw1, iw2, h0_next, h12_next,
    h0_all, q0, h1_all, q1, h2_all, q2,
):
    counts = sweep_counts(own, 0)
    lo, hi, ylo, yhi = flags()[:4]
    load = column_fine(lambda x, z: own[z, x], 4, xr, X_FIRST["h0"], lo, hi)
    join_fine(load, 24, yr, Y_FIRST["h0"], ylo, yhi, h0_all, q0)
    load = column_fine(lambda x, z: own[z, OWN["w"] + x], 1, xr, X_FIRST["w"], 1.0, 1.0)
    join_fine(load, 18, yr, Y_FIRST["w"], 1.0, 1.0, w)
    join_h1(yp, yr, Y_FIRST["h1"], h1_all, q1)
    join_w1(yp, yr, iw1)
    join_h2(yp, yr, Y_FIRST, h2_all, q2)
    join_w2(yp, yr, iw2)
    relax_levels(counts, h0_all, q0, h1_all, q1, h2_all, q2)
    iterate(corrections(q1, iw1, q2, iw2, copies), q0, w, None, pf)

    rests = [[], []]
    for x, (_, defect) in enumerate(defects(pf)):
        for z in range(2):
            h0 = own[z, x] - LEVEL[0] * defect[z]
            h0_next[x, z] = h0
            rests[z].append(own[z, OWN["w"] + x] * h0)
    summed = [plane_sums(rest) for rest in rests]
    rows = [jnp.concatenate([summed[0][k], summed[1][k]], axis=1) for k in range(5)]
    total = exact_dot(jnp.concatenate(rows, axis=0), sums[...])
    h1 = []
    for k in range(4):
        weight = coarse[COARSE["w1"] + k]
        h1.append(0.5 * LEVEL[1] / LEVEL[0] * total[8 * k : 8 * k + 8, :128] / weight)
        h12_next[k] = h1[k]
    weight = inverse(coarse[COARSE["w2"]])
    h2 = 0.25 * LEVEL[2] / LEVEL[0] * total[32:40, 128:] * weight
    h12_next[4] = h2
    pack_x(lambda x, z: h0_next[x, z], h1, h2, xp, X_SECOND)


def last_kernel(
    own, m, f, h0, xr, yp, yr, pf, w, iw1, iw2, copies,
    solution_out, residual_out,
    h0_all, q0, h1_all, q1, h2_all, q2, pf_all, solved, left, sent,
):
    counts = sweep_counts(own, 1)
    lo, hi, ylo, yhi = flags()[:4]
    load = column_fine(lambda x, z: h0[x, z], 4, xr, X_SECOND["h0"], lo, hi)
    join_fine(load, 24, yr, Y_SECOND["h0"], ylo, yhi, h0_all, q0)
    join_h1(yp, yr, Y_SECOND["h1"], h1_all, q1)
    join_h2(yp, yr, Y_SECOND, h2_all, q2)
    relax_levels(counts, h0_all, q0, h1_all, q1, h2_all, q2)
    iterate(corrections(q1, iw1, q2, iw2, copies), q0, w, pf, pf_all)
    first = core() == 0
    sending = []
    for x, (here, defect) in enumerate(defects(pf_all)):
        mine, rest = (jnp.where(first, both[0], both[1]) for both in (here, defect))
        weight = m[x]
        solved[x] = mine / weight
        left[x] = f[x] - weight * rest
        if x % 4 == 3:
            done = pl.ds(x - 3, 4)
            for k, (source, target) in enumerate(((solved, solution_out), (left, residual_out))):
                copy = pltpu.make_async_copy(
                    source.at[done], target.at[done], sent.at[2 * (x // 4) + k]
                )
                copy.start()
                sending.append(copy)
    for copy in sending:
        copy.wait()


def call(kernel, outs, scratch, name, *operands, outside=0, outs_outside=False):
    whole = pl.BlockSpec(memory_space=pltpu.HBM)
    vmem = pl.BlockSpec(memory_space=pltpu.VMEM)
    return pl.pallas_call(
        kernel,
        out_shape=[jax.ShapeDtypeStruct(shape, F32) for shape in outs],
        in_specs=[whole] * outside + [vmem] * (len(operands) - outside),
        out_specs=[whole if outs_outside else vmem] * len(outs),
        scratch_shapes=scratch,
        compiler_params=pltpu.CompilerParams(vmem_limit_bytes=32 * 2**20),
        name=name,
    )(*(pltpu.with_memory_space_constraint(x, pltpu.HBM) for x in operands[:outside]), *operands[outside:])


def space(*dims):
    return pltpu.VMEM(tiles(*dims), F32)


def tiles(*dims):
    return (*dims, *TILE)


def pairs(axis, distance):
    size = lax.axis_size(axis)
    return [[i, size + i + distance] for i in range(size - distance)]


def share(value):
    return lax.all_gather(value, "group", axis=0)


def swap(packed, axis):
    moves = [move for a, b in pairs(axis, 1) for move in ((a, b), (b, a))]
    return lax.ppermute(packed, ("group", axis), moves)


def trade_x(packed):
    return share(swap(packed, "gx"))


def trade_y(packed, packed_far):
    near = swap(packed, "gy")
    size = lax.axis_size("gy")
    groups = [*pairs("gy", 2), [size - 2, size - 1], [size, size + 1]]
    far = lax.all_gather(packed_far, ("group", "gy"), axis=0, tiled=True, axis_index_groups=groups)
    return share(jnp.concatenate([near, far], axis=0))


def on_device(forcing, metric, sweeps):
    sums, copies = (jnp.asarray(matrix, jnp.bfloat16) for matrix in (WHOLE_SUMS, COPIES))
    spaces = [space(24, 4)] * 2 + [space(16, 2)] * 2 + [space(12, 2)] * 2

    (own,) = call(
        first_kernel,
        [tiles(OWN["size"])],
        [
            *(space(16), space(16), pltpu.VMEM(sweeps.shape, jnp.int32)),
            pltpu.SemaphoreType.DMA((3,)),
        ],
        "block_sums",
        *(metric, forcing, sweeps),
        outside=3,
    )
    own = share(own)
    xp, coarse = call(
        first_sides_kernel,
        [tiles(X_FIRST["size"]), tiles(COARSE["size"])],
        [],
        "first_sides",
        own,
    )
    xr = trade_x(xp)
    yp, y2p = call(
        first_rows_kernel,
        [tiles(Y_FIRST["size"]), tiles(3)],
        [],
        "first_rows",
        *(own, coarse, xr),
    )
    yr = trade_y(yp, y2p)
    xp, pf, w, iw1, iw2, h0, h12 = call(
        middle_kernel,
        [
            *(tiles(X_SECOND["size"]), tiles(18, 4), tiles(18, 4), tiles(10, 2), tiles(6, 2)),
            *(tiles(16, 2), tiles(5)),
        ],
        spaces,
        "first_cycle",
        *(own, coarse, xr, yp, yr, sums, copies),
    )
    xr = trade_x(xp)
    yp, y2p = call(
        second_rows_kernel,
        [tiles(Y_SECOND["size"]), tiles(3)],
        [],
        "second_rows",
        *(h0, h12, xr),
    )
    yr = trade_y(yp, y2p)
    return call(
        last_kernel,
        [tiles(16), tiles(16)],
        [*spaces, space(18, 4), space(16), space(16), pltpu.SemaphoreType.DMA((8,))],
        "second_cycle",
        *(own, metric, forcing, h0, xr, yp, yr, pf, w, iw1, iw2, copies),
        outs_outside=True,
    )


def solution(mesh):
    def program(forcing, metric, sweeps):
        return tuple(on_device(forcing, metric, sweeps))

    return jax.shard_map(
        program,
        mesh=mesh,
        in_specs=(P("gx", "gy", "group"), P("gx", "gy", "group"), P()),
        out_specs=(P("gx", "gy", "group"), P("gx", "gy", "group")),
        check_vma=False,
    )
```

```python
import jax
import jax.numpy as jnp
import numpy as np
from jax import lax
from jax.experimental import pallas as pl
from jax.experimental.pallas import tpu as pltpu
from jax.sharding import PartitionSpec as P

RELAXATION = 0.8
SIDE_WEIGHT = 0.05 ** (1.0 / 3.0)
SELF_WEIGHT = 3.4
SIDE_CUBE = SIDE_WEIGHT**3

KEEP = 1.0 - RELAXATION * SELF_WEIGHT / 3.0
SPREAD = RELAXATION * SIDE_CUBE / 3.0
LEVEL = [RELAXATION / (3.0 * 4.0**-level) for level in range(3)]

F32 = jnp.float32
TILE = (8, 128)

OWN = dict(h0=0, w=16, h1=32, w1=36, h2=40, w2=41, counts=42, size=43)
COARSE = dict(h1=0, w1=4, h2=8, w2=9, size=10)
X_FIRST = dict(h0=0, h1=8, h2=10, w=11, w12=13, size=14)
X_SECOND = dict(h0=0, h1=8, h2=10, size=11)
Y_FIRST = dict(h0=0, h1=24, h2=32, w=35, w1=53, w2=58, size=60, far=60)
Y_SECOND = dict(h0=0, h1=24, h2=32, size=35, far=35)

LANES = np.arange(256)
WHOLE_SUMS = np.concatenate(
    [LANES[:, None] // 2 == LANES[None, :128], LANES[:, None] // 4 == LANES[None, :128]], axis=1
).astype(np.float32)
COPIES = WHOLE_SUMS.T * np.where(LANES[:, None] < 128, 0.5, 0.25).astype(np.float32)


def exact_dot(rows, matrix):
    parts = []
    rest = rows
    for _ in range(3):
        parts.append(rest.astype(jnp.bfloat16))
        rest = rest - parts[-1].astype(F32)
    out = lax.dot_general(
        jnp.concatenate(parts, axis=0),
        matrix,
        (((1,), (0,)), ((), ())),
        preferred_element_type=F32,
    )
    count = rows.shape[0]
    return out[:count] + (out[count : 2 * count] + out[2 * count :])


def sub_index():
    return lax.broadcasted_iota(jnp.int32, TILE, 0)


def lane_index():
    return lax.broadcasted_iota(jnp.int32, TILE, 1)


def turn(tile, by):
    by %= 8
    return pltpu.roll(tile, by, 0) if by else tile


def keep(where, tile):
    return jnp.where(where, tile, 0.0)


def inverse(tile):
    return jnp.where(tile > 0, 1.0 / jnp.where(tile > 0, tile, 1.0), 0.0)


def core():
    return lax.axis_index("group")


def flags():
    gx, gy = lax.axis_index("gx"), lax.axis_index("gy")
    x_last, y_last = lax.axis_size("gx") - 1, lax.axis_size("gy") - 1
    places = [gx > 0, gx < x_last, gy > 0, gy < y_last, gy > 1, gy < y_last - 1]
    return [place.astype(F32) for place in places]


def pair_rows(first, second):
    sub = sub_index()
    first, second = (tile + turn(tile, 7) for tile in (first, second))
    low = jnp.where(sub == 0, first, turn(first, 7))
    low = jnp.where(sub < 2, low, jnp.where(sub == 2, turn(first, 6), turn(first, 5)))
    high = jnp.where(sub == 4, turn(second, 4), turn(second, 3))
    high = jnp.where(sub < 6, high, jnp.where(sub == 6, turn(second, 2), turn(second, 1)))
    return jnp.where(sub < 4, low, high)


def plane_sums(fine):
    sub = sub_index()
    sums = [fine[2 * k] + fine[2 * k + 1] for k in range(8)]
    one = [pair_rows(sums[2 * k], sums[2 * k + 1]) for k in range(4)]
    two = None
    for k in range(4):
        both = one[k] + turn(one[k], 4)
        both = both + turn(both, 7)
        placed = jnp.where(sub == 2 * k, turn(both, 2 * k), turn(both, 2 * k - 1))
        two = placed if k == 0 else jnp.where(sub < 2 * k, two, placed)
    return one + [two]


def half_sums():
    row = lax.broadcasted_iota(jnp.int32, (128, 128), 0)
    column = lax.broadcasted_iota(jnp.int32, (128, 128), 1)
    matrix = jnp.concatenate([row >> 1 == column, row >> 2 == column], axis=1)
    return jnp.where(matrix, 1.0, 0.0).astype(jnp.bfloat16)


def first_kernel(m_whole, f_whole, sweeps_whole, out, m, f, sweeps, arrived):
    moves = ((m_whole, m), (f_whole, f), (sweeps_whole, sweeps))
    copies = [
        pltpu.make_async_copy(source, target, arrived.at[k])
        for k, (source, target) in enumerate(moves)
    ]
    for copy in copies:
        copy.start()
    sums = half_sums()
    for copy in copies:
        copy.wait()
    m_tiles, f_tiles = ([ref[x] for x in range(16)] for ref in (m, f))
    for x in range(16):
        out[OWN["h0"] + x] = LEVEL[0] * f_tiles[x] / m_tiles[x]
        out[OWN["w"] + x] = m_tiles[x]
    rows = jnp.concatenate(plane_sums(m_tiles) + plane_sums(f_tiles), axis=0)
    total = exact_dot(rows, sums)
    out[OWN["counts"]] = jnp.zeros(TILE, F32)
    out[OWN["counts"], : sweeps.shape[0], : sweeps.shape[1]] = sweeps[...].astype(F32)
    upper = core() == 1
    for k in range(5):
        left, width = (0, 64) if k < 4 else (128, 32)
        weight, force = (
            total[row : row + 8, left : left + 128] for row in (8 * k, 40 + 8 * k)
        )
        weight = (0.125 if k < 4 else 0.125 * 0.125) * weight
        force = (0.5 * LEVEL[1] if k < 4 else 0.25 * LEVEL[2]) * force * inverse(weight)
        weight, force = (
            jnp.where(upper, pltpu.roll(tile, width, 1), tile) for tile in (weight, force)
        )
        out[(OWN["w1"] + k) if k < 4 else OWN["w2"]] = weight
        out[(OWN["h1"] + k) if k < 4 else OWN["h2"]] = force


def pack_x(fine, h1, h2, xp, at):
    upward = core() == 0
    start = jnp.where(upward, 12, 0)
    for k in range(4):
        for z in range(2):
            xp[at["h0"] + 2 * k + z] = fine(start + k, z)
    for k in range(2):
        xp[at["h1"] + k] = jnp.where(upward, h1[2 + k], h1[k])
    xp[at["h2"]] = h2


def first_sides_kernel(own, xp, coarse):
    total = [own[0, k] + own[1, k] for k in range(OWN["h1"], OWN["counts"])]
    for k in range(COARSE["size"]):
        coarse[k] = total[k]
    h1, w1 = total[:4], total[4:8]
    h2, w2 = total[8:]
    pack_x(lambda x, z: own[z, x], h1, h2, xp, X_FIRST)
    upward = core() == 0
    edge = OWN["w"] + jnp.where(upward, 15, 0)
    for z in range(2):
        xp[X_FIRST["w"] + z] = own[z, edge]
    sub = sub_index()
    edge_one = jnp.where(upward, turn(w1[3], 4), w1[0])
    edge_two = jnp.where(upward, turn(w2, 6), turn(w2, 4))
    xp[X_FIRST["w12"]] = jnp.where(sub < 4, edge_one, edge_two)


def column_fine(own, planes, xr, at, lo, hi):
    def load(p, z):
        if p < planes:
            return xr[1, 0, at + 2 * p + z] * lo
        if p < 16 + planes:
            return own(p - planes, z)
        return xr[0, 1, at + 2 * (p - 16 - planes) + z] * hi

    return load


def pack_fine(load, planes, mine, yp, at):
    for k in range(planes // 2):
        for z in range(2):
            yp[at + 2 * k + z] = jnp.where(mine, load(2 * k, z), turn(load(2 * k + 1, z), 4))


def pack_y(own, h1, h2, xr, yp, y2p, x_at, at):
    lo, hi = flags()[:2]
    mine = (sub_index() < 4) == (core() == 1)
    pack_fine(column_fine(own, 4, xr, x_at["h0"], lo, hi), 24, mine, yp, at["h0"])
    for k in range(2):
        yp[at["h1"] + k] = xr[1, 0, x_at["h1"] + k] * lo
        yp[at["h1"] + 6 + k] = xr[0, 1, x_at["h1"] + k] * hi
    for k in range(4):
        yp[at["h1"] + 2 + k] = h1(k)
    two = [xr[1, 0, x_at["h2"]] * lo, h2(), xr[0, 1, x_at["h2"]] * hi]
    for k in range(3):
        yp[at["h2"] + k] = two[k]
        y2p[k] = two[k]


def first_rows_kernel(own, coarse, xr, yp, y2p):
    at = Y_FIRST
    pack_y(
        lambda x, z: own[z, x],
        lambda k: coarse[k],
        lambda: coarse[COARSE["h2"]],
        *(xr, yp, y2p, X_FIRST, at),
    )
    sub = sub_index()
    mine = (sub < 4) == (core() == 1)
    weights = column_fine(lambda x, z: own[z, OWN["w"] + x], 1, xr, X_FIRST["w"], 1.0, 1.0)
    pack_fine(weights, 18, mine, yp, at["w"])
    low, high = xr[1, 0, X_FIRST["w12"]], xr[0, 1, X_FIRST["w12"]]
    for k in range(4):
        yp[at["w1"] + k] = coarse[COARSE["w1"] + k]
    yp[at["w1"] + 4] = jnp.where(sub < 4, low, turn(high, 4))
    yp[at["w2"]] = coarse[COARSE["w2"]]
    yp[at["w2"] + 1] = jnp.where(sub < 2, turn(low, 4), turn(high, 6))


def second_rows_kernel(h0, h12, xr, yp, y2p):
    pack_y(
        lambda x, z: h0[x, z],
        lambda k: h12[k],
        lambda: h12[4],
        *(xr, yp, y2p, X_SECOND, Y_SECOND),
    )


def join_fine(load, planes, yr, at, ylo, yhi, *outs):
    sub = sub_index()
    for k in range(planes // 2):
        for z in range(2):
            above, below = yr[0, at + 2 * k + z] * yhi, yr[1, at + 2 * k + z] * ylo
            halos = (
                jnp.where(sub < 4, above, below),
                turn(jnp.where(sub < 4, below, above), 4),
            )
            for i in range(2):
                own = load(2 * k + i, z)
                for out in outs:
                    out[2 * k + i, z] = own
                    out[2 * k + i, 2 + z] = halos[i]


def four_rows(own, above, below, i):
    sub = sub_index()
    turned = 4 * (1 - i)
    first = jnp.where(sub < 4, turn(own, 4 * i), turn(above, turned))
    return first, keep(sub >= 4, turn(below, turned))


def join_h1(yp, yr, at, *outs):
    ylo, yhi = flags()[2:4]
    for k in range(8):
        tile = at + k
        own, above, below = yp[tile], yr[0, tile] * yhi, yr[1, tile] * ylo
        for i in range(2):
            both = four_rows(own, above, below, i)
            for out in outs:
                out[2 * k + i, 0], out[2 * k + i, 1] = both


def join_w1(yp, yr, out):
    for k in range(5):
        tile = Y_FIRST["w1"] + k
        own, above, below = yp[tile], yr[0, tile], yr[1, tile]
        for i in range(2):
            p = 9 * i if k == 4 else 1 + 2 * k + i
            first, second = four_rows(own, above, below, i)
            out[p, 0], out[p, 1] = inverse(first), inverse(second)


def join_h2(yp, yr, at, *outs):
    ylo, yhi, ylo2, yhi2 = flags()[2:]
    sub = sub_index()
    for k in range(3):
        tile, far = at["h2"] + k, at["far"] + k
        own, above, below = yp[tile], yr[0, tile] * yhi, yr[1, tile] * ylo
        above2, below2 = yr[1, far + 3] * yhi2, yr[0, far] * ylo2
        for i in range(4):
            first = jnp.where(sub < 2, turn(own, -2 * i), turn(above, 2 - 2 * i))
            upper = keep(sub < 6, turn(above2, 4 - 2 * i))
            lower = jnp.where(sub < 6, turn(below2, 4 - 2 * i), turn(below, 6 - 2 * i))
            for out in outs:
                out[4 * k + i, 0] = jnp.where(sub < 4, first, upper)
                out[4 * k + i, 1] = keep(sub >= 4, lower)


def join_w2(yp, yr, out):
    sub = sub_index()
    for p in range(6):
        k, i = (1, p // 5) if p in (0, 5) else (0, p - 1)
        tile = Y_FIRST["w2"] + k
        own, above, below = yp[tile], yr[0, tile], yr[1, tile]
        first = jnp.where(sub < 2, turn(own, -2 * i), turn(above, 2 - 2 * i))
        out[p, 0] = inverse(keep(sub < 4, first))
        out[p, 1] = inverse(keep(sub >= 6, turn(below, 6 - 2 * i)))


def along_y(first, second):
    sub = sub_index()
    up_first, up_second = turn(first, 7), turn(second, 7)
    down_first, down_second = turn(first, 1), turn(second, 1)
    sides_first = jnp.where(sub == 7, up_second, up_first) + jnp.where(sub == 0, down_second, down_first)
    sides_second = jnp.where(sub == 7, up_first, up_second) + jnp.where(sub == 0, down_first, down_second)
    return (first + first) + sides_first, (second + second) + sides_second


def along_z_fine(left, right):
    lane = lane_index()
    up_left, up_right = pltpu.roll(left, 127, 1), pltpu.roll(right, 127, 1)
    down_left, down_right = pltpu.roll(left, 1, 1), pltpu.roll(right, 1, 1)
    sides_left = jnp.where(lane < 127, up_left, up_right) + keep(lane > 0, down_left)
    sides_right = keep(lane < 127, up_right) + jnp.where(lane > 0, down_right, down_left)
    return (left + left) + sides_left, (right + right) + sides_right


def along_z_coarse(tile):
    lane = lane_index()
    sides = keep(lane < 127, pltpu.roll(tile, 127, 1)) + keep(lane > 0, pltpu.roll(tile, 1, 1))
    return (tile + tile) + sides


def along_yz(tiles):
    tiles = list(tiles)
    if len(tiles) == 4:
        for z in range(2):
            tiles[z], tiles[2 + z] = along_y(tiles[z], tiles[2 + z])
        for y in range(2):
            tiles[2 * y], tiles[2 * y + 1] = along_z_fine(tiles[2 * y], tiles[2 * y + 1])
        return tiles
    return [along_z_coarse(tile) for tile in along_y(*tiles)]


def added(first, second):
    return [a + b for a, b in zip(first, second)]


def relax_planes(q, h, start, planes, parts, before, masks, factors, active):
    def load(x):
        return [q[x, part] for part in range(parts)]

    kept = KEEP if active is None else 1.0 + active * (KEEP - 1.0)
    here = load(start)
    below = added(before, here)
    for i in range(planes):
        x = start + i
        after = load(x + 1)
        above = added(here, after)
        summed = along_yz(added(below, above))
        for part in range(parts):
            spread = (masks[part // (parts // 2)] * factors[i]) * summed[part]
            source = h[x, part] if active is None else active * h[x, part]
            q[x, part] = (kept * here[part] + spread) + source
        last, here, below = here, after, above
    return last


def relax_levels(counts, h0, q0, h1, q1, h2, q2):
    lo, hi, ylo, yhi, ylo2, yhi2 = flags()
    sub, lane = sub_index(), lane_index()
    spread = jnp.full(TILE, SPREAD, F32)
    above = jnp.where(sub < 2, 1.0, jnp.where(sub < 4, yhi, jnp.where(sub < 6, yhi2, 0.0)))
    below = jnp.where(sub < 4, 0.0, jnp.where(sub < 6, ylo2, ylo))
    masks2 = (keep(lane < 64, above * spread), keep(lane < 64, below * spread))
    masks1 = (jnp.where(sub < 4, 1.0, yhi) * spread, jnp.where(sub < 4, 0.0, ylo) * spread)
    masks0 = (spread, jnp.where(sub < 4, yhi, ylo) * spread)

    def coarse_sweep(k, _):
        for q, h, planes, masks, count in ((q2, h2, 12, masks2, counts[2]), (q1, h1, 16, masks1, counts[1])):
            active = jnp.where(count > k, 1.0, 0.0)
            factors = [active * lo] * 3 + [active] * (planes - 8) + [active * hi] * 3
            before = [q[0, part] for part in range(2)]
            relax_planes(q, h, 1, planes - 2, 2, before, masks, factors, active)
        return 0

    def fine_sweep(_, __):
        def half(j, before):
            start = 1 + 11 * j
            factors = [
                jnp.where(start + i < 4, lo, jnp.where(start + i >= 20, hi, 1.0)) for i in range(11)
            ]
            return tuple(relax_planes(q0, h0, start, 11, 4, list(before), masks0, factors, None))

        lax.fori_loop(0, 2, half, tuple(q0[0, part] for part in range(4)))
        return 0

    lax.fori_loop(1, jnp.maximum(counts[1], counts[2]), coarse_sweep, 0)
    lax.fori_loop(1, counts[0], fine_sweep, 0)


def sweep_counts(own, cycle):
    held, sub, lane = own[0, OWN["counts"]], sub_index(), lane_index()
    return [
        jnp.max(keep((sub == cycle) & (lane == level), held)).astype(jnp.int32) for level in range(3)
    ]


def corrections(q1, iw1, q2, iw2, copies):
    sub = sub_index()
    one, two = (
        [
            jnp.where(sub < 7, q[p + 3, 0] * iw[p, 0], q[p + 3, 1] * iw[p, 1])
            for p in range(planes)
        ]
        for q, iw, planes in ((q1, iw1, 10), (q2, iw2, 6))
    )
    spread = []
    for tile in two:
        inner = jnp.where(sub < 3, turn(tile, 1), turn(tile, 2))
        spread.append(jnp.where((sub == 0) | (sub == 7), tile, inner))
    rows = [jnp.concatenate([one[p], spread[(p + 1) // 2]], axis=1) for p in range(10)]
    return exact_dot(jnp.concatenate(rows, axis=0), copies[...])


def iterate(coarse, q0, w, before, out):
    sub = sub_index()
    for k in range(10):
        for z in range(2):
            tile = coarse[8 * k : 8 * k + 8, 128 * z : 128 * z + 128]
            turned = [tile] + [turn(tile, by) for by in range(1, 5)]
            rows = turned[4]
            for by, last in ((3, 6), (2, 4), (1, 2), (0, 0)):
                rows = jnp.where(sub <= last, turned[by], rows)
            halo = jnp.where(sub < 7, turned[4], tile)
            for p in (2 * k - 1, 2 * k):
                if 0 <= p < 18:
                    for part, value in ((z, rows), (2 + z, halo)):
                        total = q0[p + 3, part] + w[p, part] * value
                        if before is not None:
                            total = before[p, part] + total
                        out[p, part] = total


def defects(pf):
    def load(p):
        return [pf[p, part] for part in range(4)]

    here = load(1)
    below = added(load(0), here)
    for x in range(16):
        after = load(x + 2)
        above = added(here, after)
        summed = along_yz(added(below, above))
        yield here[:2], [SELF_WEIGHT * here[z] - SIDE_CUBE * summed[z] for z in range(2)]
        here, below = after, above


def middle_kernel(
    own, coarse, xr, yp, yr, sums, copies,
    xp, pf, w, iw1, iw2, h0_next, h12_next,
    h0_all, q0, h1_all, q1, h2_all, q2,
):
    counts = sweep_counts(own, 0)
    lo, hi, ylo, yhi = flags()[:4]
    load = column_fine(lambda x, z: own[z, x], 4, xr, X_FIRST["h0"], lo, hi)
    join_fine(load, 24, yr, Y_FIRST["h0"], ylo, yhi, h0_all, q0)
    load = column_fine(lambda x, z: own[z, OWN["w"] + x], 1, xr, X_FIRST["w"], 1.0, 1.0)
    join_fine(load, 18, yr, Y_FIRST["w"], 1.0, 1.0, w)
    join_h1(yp, yr, Y_FIRST["h1"], h1_all, q1)
    join_w1(yp, yr, iw1)
    join_h2(yp, yr, Y_FIRST, h2_all, q2)
    join_w2(yp, yr, iw2)
    relax_levels(counts, h0_all, q0, h1_all, q1, h2_all, q2)
    iterate(corrections(q1, iw1, q2, iw2, copies), q0, w, None, pf)

    rests = [[], []]
    for x, (_, defect) in enumerate(defects(pf)):
        for z in range(2):
            h0 = own[z, x] - LEVEL[0] * defect[z]
            h0_next[x, z] = h0
            rests[z].append(own[z, OWN["w"] + x] * h0)
    summed = [plane_sums(rest) for rest in rests]
    rows = [jnp.concatenate([summed[0][k], summed[1][k]], axis=1) for k in range(5)]
    total = exact_dot(jnp.concatenate(rows, axis=0), sums[...])
    h1 = []
    for k in range(4):
        weight = coarse[COARSE["w1"] + k]
        h1.append(0.5 * LEVEL[1] / LEVEL[0] * total[8 * k : 8 * k + 8, :128] / weight)
        h12_next[k] = h1[k]
    weight = inverse(coarse[COARSE["w2"]])
    h2 = 0.25 * LEVEL[2] / LEVEL[0] * total[32:40, 128:] * weight
    h12_next[4] = h2
    pack_x(lambda x, z: h0_next[x, z], h1, h2, xp, X_SECOND)


def last_kernel(
    own, m, f, h0, xr, yp, yr, pf, w, iw1, iw2, copies,
    solution_out, residual_out,
    h0_all, q0, h1_all, q1, h2_all, q2, pf_all, solved, left, sent,
):
    counts = sweep_counts(own, 1)
    lo, hi, ylo, yhi = flags()[:4]
    load = column_fine(lambda x, z: h0[x, z], 4, xr, X_SECOND["h0"], lo, hi)
    join_fine(load, 24, yr, Y_SECOND["h0"], ylo, yhi, h0_all, q0)
    join_h1(yp, yr, Y_SECOND["h1"], h1_all, q1)
    join_h2(yp, yr, Y_SECOND, h2_all, q2)
    relax_levels(counts, h0_all, q0, h1_all, q1, h2_all, q2)
    iterate(corrections(q1, iw1, q2, iw2, copies), q0, w, pf, pf_all)
    first = core() == 0
    sending = []
    for x, (here, defect) in enumerate(defects(pf_all)):
        mine, rest = (jnp.where(first, both[0], both[1]) for both in (here, defect))
        weight = m[x]
        solved[x] = mine / weight
        left[x] = f[x] - weight * rest
        if x % 4 == 3:
            done = pl.ds(x - 3, 4)
            for k, (source, target) in enumerate(((solved, solution_out), (left, residual_out))):
                copy = pltpu.make_async_copy(
                    source.at[done], target.at[done], sent.at[2 * (x // 4) + k]
                )
                copy.start()
                sending.append(copy)
    for copy in sending:
        copy.wait()


def call(kernel, outs, scratch, name, *operands, outside=0, outs_outside=False):
    whole = pl.BlockSpec(memory_space=pltpu.HBM)
    vmem = pl.BlockSpec(memory_space=pltpu.VMEM)
    return pl.pallas_call(
        kernel,
        out_shape=[jax.ShapeDtypeStruct(shape, F32) for shape in outs],
        in_specs=[whole] * outside + [vmem] * (len(operands) - outside),
        out_specs=[whole if outs_outside else vmem] * len(outs),
        scratch_shapes=scratch,
        compiler_params=pltpu.CompilerParams(vmem_limit_bytes=32 * 2**20),
        name=name,
    )(*(pltpu.with_memory_space_constraint(x, pltpu.HBM) for x in operands[:outside]), *operands[outside:])


def space(*dims):
    return pltpu.VMEM(tiles(*dims), F32)


def tiles(*dims):
    return (*dims, *TILE)


def share(value):
    return lax.all_gather(value, "group", axis=0)


def trade_x(packed):
    names = ("group", "gx", "gy")
    sizes = [lax.axis_size(name) for name in names]
    index = np.arange(np.prod(sizes)).reshape(sizes)
    inner = np.stack([index[0, :-1], index[1, 1:]], axis=-1).reshape(-1, 2)
    ends = np.concatenate([index[0, -1], index[1, 0]]).reshape(-1, 2)
    groups = np.concatenate([inner, ends]).tolist()
    return share(lax.all_gather(packed, names, axis=0, axis_index_groups=groups))


def trade_y(packed, packed_far):
    size = lax.axis_size("gy")
    moves = []
    for i in range(size - 1):
        moves += [(i, size + i + 1), (size + i + 1, i)]
    near = lax.ppermute(packed, ("group", "gy"), moves)
    groups = [[size + i, i + 2] for i in range(size - 2)]
    groups += [[0, 1], [2 * size - 2, 2 * size - 1]]
    far = lax.all_gather(packed_far, ("group", "gy"), axis=0, tiled=True, axis_index_groups=groups)
    return share(jnp.concatenate([near, far], axis=0))


def on_device(forcing, metric, sweeps):
    sums, copies = (jnp.asarray(matrix, jnp.bfloat16) for matrix in (WHOLE_SUMS, COPIES))
    spaces = [space(24, 4)] * 2 + [space(16, 2)] * 2 + [space(12, 2)] * 2

    (own,) = call(
        first_kernel,
        [tiles(OWN["size"])],
        [
            *(space(16), space(16), pltpu.VMEM(sweeps.shape, jnp.int32)),
            pltpu.SemaphoreType.DMA((3,)),
        ],
        "block_sums",
        *(metric, forcing, sweeps),
        outside=3,
    )
    own = share(own)
    xp, coarse = call(
        first_sides_kernel,
        [tiles(X_FIRST["size"]), tiles(COARSE["size"])],
        [],
        "first_sides",
        own,
    )
    xr = trade_x(xp)
    yp, y2p = call(
        first_rows_kernel,
        [tiles(Y_FIRST["size"]), tiles(3)],
        [],
        "first_rows",
        *(own, coarse, xr),
    )
    yr = trade_y(yp, y2p)
    xp, pf, w, iw1, iw2, h0, h12 = call(
        middle_kernel,
        [
            *(tiles(X_SECOND["size"]), tiles(18, 4), tiles(18, 4), tiles(10, 2), tiles(6, 2)),
            *(tiles(16, 2), tiles(5)),
        ],
        spaces,
        "first_cycle",
        *(own, coarse, xr, yp, yr, sums, copies),
    )
    xr = trade_x(xp)
    yp, y2p = call(
        second_rows_kernel,
        [tiles(Y_SECOND["size"]), tiles(3)],
        [],
        "second_rows",
        *(h0, h12, xr),
    )
    yr = trade_y(yp, y2p)
    return call(
        last_kernel,
        [tiles(16), tiles(16)],
        [*spaces, space(18, 4), space(16), space(16), pltpu.SemaphoreType.DMA((8,))],
        "second_cycle",
        *(own, metric, forcing, h0, xr, yp, yr, pf, w, iw1, iw2, copies),
        outs_outside=True,
    )


def solution(mesh):
    def program(forcing, metric, sweeps):
        return tuple(on_device(forcing, metric, sweeps))

    return jax.shard_map(
        program,
        mesh=mesh,
        in_specs=(P("gx", "gy", "group"), P("gx", "gy", "group"), P()),
        out_specs=(P("gx", "gy", "group"), P("gx", "gy", "group")),
        check_vma=False,
    )
```

```python
import jax
import jax.numpy as jnp
import numpy as np
from jax import lax
from jax.experimental import pallas as pl
from jax.experimental.pallas import tpu as pltpu
from jax.sharding import PartitionSpec as P

RELAXATION = 0.8
SIDE_WEIGHT = 0.05 ** (1.0 / 3.0)
SELF_WEIGHT = 3.4
SIDE_CUBE = SIDE_WEIGHT**3

KEEP = 1.0 - RELAXATION * SELF_WEIGHT / 3.0
SPREAD = RELAXATION * SIDE_CUBE / 3.0
LEVEL = [RELAXATION / (3.0 * 4.0**-level) for level in range(3)]

F32 = jnp.float32
TILE = (8, 128)

OWN = dict(h0=0, w=16, h1=32, w1=36, h2=40, w2=41, counts=42, size=43)
COARSE = dict(h1=0, w1=4, h2=8, w2=9, size=10)
X_FIRST = dict(h0=0, h1=8, h2=10, w=11, w12=13, size=14)
X_SECOND = dict(h0=0, h1=8, h2=10, size=11)
Y_FIRST = dict(h0=0, h1=24, h2=32, w=35, w1=41, w2=46, size=48, far=48)
Y_SECOND = dict(h0=0, h1=24, h2=32, size=35, far=35)

LANES = np.arange(256)
WHOLE_SUMS = np.concatenate(
    [LANES[:, None] // 2 == LANES[None, :128], LANES[:, None] // 4 == LANES[None, :128]], axis=1
).astype(np.float32)
COPIES = WHOLE_SUMS.T * np.where(LANES[:, None] < 128, 0.5, 0.25).astype(np.float32)


def exact_dot(rows, matrix):
    parts = []
    rest = rows
    for _ in range(3):
        parts.append(rest.astype(jnp.bfloat16))
        rest = rest - parts[-1].astype(F32)
    out = lax.dot_general(
        jnp.concatenate(parts, axis=0),
        matrix,
        (((1,), (0,)), ((), ())),
        preferred_element_type=F32,
    )
    count = rows.shape[0]
    return out[:count] + (out[count : 2 * count] + out[2 * count :])


def sub_index():
    return lax.broadcasted_iota(jnp.int32, TILE, 0)


def lane_index():
    return lax.broadcasted_iota(jnp.int32, TILE, 1)


def turn(tile, by):
    by %= 8
    return pltpu.roll(tile, by, 0) if by else tile


def keep(where, tile):
    return jnp.where(where, tile, 0.0)


def inverse(tile):
    return jnp.where(tile > 0, 1.0 / jnp.where(tile > 0, tile, 1.0), 0.0)


def core():
    return lax.axis_index("group")


def flags():
    gx, gy = lax.axis_index("gx"), lax.axis_index("gy")
    x_last, y_last = lax.axis_size("gx") - 1, lax.axis_size("gy") - 1
    places = [gx > 0, gx < x_last, gy > 0, gy < y_last, gy > 1, gy < y_last - 1]
    return [place.astype(F32) for place in places]


def pair_rows(first, second):
    sub = sub_index()
    first, second = (tile + turn(tile, 7) for tile in (first, second))
    low = jnp.where(sub == 0, first, turn(first, 7))
    low = jnp.where(sub < 2, low, jnp.where(sub == 2, turn(first, 6), turn(first, 5)))
    high = jnp.where(sub == 4, turn(second, 4), turn(second, 3))
    high = jnp.where(sub < 6, high, jnp.where(sub == 6, turn(second, 2), turn(second, 1)))
    return jnp.where(sub < 4, low, high)


def plane_sums(fine):
    sub = sub_index()
    sums = [fine[2 * k] + fine[2 * k + 1] for k in range(8)]
    one = [pair_rows(sums[2 * k], sums[2 * k + 1]) for k in range(4)]
    two = None
    for k in range(4):
        both = one[k] + turn(one[k], 4)
        both = both + turn(both, 7)
        placed = jnp.where(sub == 2 * k, turn(both, 2 * k), turn(both, 2 * k - 1))
        two = placed if k == 0 else jnp.where(sub < 2 * k, two, placed)
    return one + [two]


def half_sums():
    row = lax.broadcasted_iota(jnp.int32, (128, 128), 0)
    column = lax.broadcasted_iota(jnp.int32, (128, 128), 1)
    matrix = jnp.concatenate([row >> 1 == column, row >> 2 == column], axis=1)
    return jnp.where(matrix, 1.0, 0.0).astype(jnp.bfloat16)


def first_kernel(m_whole, f_whole, sweeps_whole, out, m, f, sweeps, arrived):
    moves = ((m_whole, m), (f_whole, f), (sweeps_whole, sweeps))
    copies = [
        pltpu.make_async_copy(source, target, arrived.at[k])
        for k, (source, target) in enumerate(moves)
    ]
    for copy in copies:
        copy.start()
    sums = half_sums()
    copies[0].wait()
    m_tiles = [m[x] for x in range(16)]
    m_sums = plane_sums(m_tiles)
    for x in range(16):
        out[OWN["w"] + x] = m_tiles[x]
    for copy in copies[1:]:
        copy.wait()
    f_tiles = [f[x] for x in range(16)]
    for x in range(16):
        out[OWN["h0"] + x] = LEVEL[0] * f_tiles[x] / m_tiles[x]
    rows = jnp.concatenate(m_sums + plane_sums(f_tiles), axis=0)
    total = exact_dot(rows, sums)
    out[OWN["counts"]] = jnp.zeros(TILE, F32)
    out[OWN["counts"], : sweeps.shape[0], : sweeps.shape[1]] = sweeps[...].astype(F32)
    upper = core() == 1
    for k in range(5):
        left, width = (0, 64) if k < 4 else (128, 32)
        weight, force = (
            total[row : row + 8, left : left + 128] for row in (8 * k, 40 + 8 * k)
        )
        weight = (0.125 if k < 4 else 0.125 * 0.125) * weight
        force = (0.5 * LEVEL[1] if k < 4 else 0.25 * LEVEL[2]) * force * inverse(weight)
        weight, force = (
            jnp.where(upper, pltpu.roll(tile, width, 1), tile) for tile in (weight, force)
        )
        out[(OWN["w1"] + k) if k < 4 else OWN["w2"]] = weight
        out[(OWN["h1"] + k) if k < 4 else OWN["h2"]] = force


def pack_x(fine, h1, h2, xp, at):
    upward = core() == 0
    start = jnp.where(upward, 12, 0)
    for k in range(4):
        for z in range(2):
            xp[at["h0"] + 2 * k + z] = fine(start + k, z)
    for k in range(2):
        xp[at["h1"] + k] = jnp.where(upward, h1[2 + k], h1[k])
    xp[at["h2"]] = h2


def first_sides_kernel(own, xp, coarse):
    total = [own[0, k] + own[1, k] for k in range(OWN["h1"], OWN["counts"])]
    for k in range(COARSE["size"]):
        coarse[k] = total[k]
    h1, w1 = total[:4], total[4:8]
    h2, w2 = total[8:]
    pack_x(lambda x, z: own[z, x], h1, h2, xp, X_FIRST)
    upward = core() == 0
    edge = OWN["w"] + jnp.where(upward, 15, 0)
    for z in range(2):
        xp[X_FIRST["w"] + z] = own[z, edge]
    sub = sub_index()
    edge_one = jnp.where(upward, turn(w1[3], 4), w1[0])
    edge_two = jnp.where(upward, turn(w2, 6), turn(w2, 4))
    xp[X_FIRST["w12"]] = jnp.where(sub < 4, edge_one, edge_two)


def column_fine(own, planes, xr, at, lo, hi):
    def load(p, z):
        if p < planes:
            return xr[1, 0, at + 2 * p + z] * lo
        if p < 16 + planes:
            return own(p - planes, z)
        return xr[0, 1, at + 2 * (p - 16 - planes) + z] * hi

    return load


def pack_fine(load, planes, mine, yp, at):
    for k in range(planes // 2):
        for z in range(2):
            yp[at + 2 * k + z] = jnp.where(mine, load(2 * k, z), turn(load(2 * k + 1, z), 4))


def pack_y(own, h1, h2, xr, yp, y2p, x_at, at):
    lo, hi = flags()[:2]
    mine = (sub_index() < 4) == (core() == 1)
    pack_fine(column_fine(own, 4, xr, x_at["h0"], lo, hi), 24, mine, yp, at["h0"])
    for k in range(2):
        yp[at["h1"] + k] = xr[1, 0, x_at["h1"] + k] * lo
        yp[at["h1"] + 6 + k] = xr[0, 1, x_at["h1"] + k] * hi
    for k in range(4):
        yp[at["h1"] + 2 + k] = h1(k)
    two = [xr[1, 0, x_at["h2"]] * lo, h2(), xr[0, 1, x_at["h2"]] * hi]
    for k in range(3):
        yp[at["h2"] + k] = two[k]
        y2p[k] = two[k]


def first_rows_kernel(own, coarse, xr, yp, y2p):
    at = Y_FIRST
    pack_y(
        lambda x, z: own[z, x],
        lambda k: coarse[k],
        lambda: coarse[COARSE["h2"]],
        *(xr, yp, y2p, X_FIRST, at),
    )
    sub = sub_index()
    weights = column_fine(lambda x, z: own[z, OWN["w"] + x], 1, xr, X_FIRST["w"], 1.0, 1.0)
    upward = core() == 0
    for k in range(3):
        for z in range(2):
            packed = None
            for i in range(min(8, 18 - 8 * k)):
                tile = weights(8 * k + i, z)
                row = turn(jnp.where(upward, turn(tile, 1), tile), i)
                packed = row if i == 0 else jnp.where(sub < i, packed, row)
            yp[at["w"] + 2 * k + z] = packed
    low, high = xr[1, 0, X_FIRST["w12"]], xr[0, 1, X_FIRST["w12"]]
    for k in range(4):
        yp[at["w1"] + k] = coarse[COARSE["w1"] + k]
    yp[at["w1"] + 4] = jnp.where(sub < 4, low, turn(high, 4))
    yp[at["w2"]] = coarse[COARSE["w2"]]
    yp[at["w2"] + 1] = jnp.where(sub < 2, turn(low, 4), turn(high, 6))


def second_rows_kernel(h0, h12, xr, yp, y2p):
    pack_y(
        lambda x, z: h0[x, z],
        lambda k: h12[k],
        lambda: h12[4],
        *(xr, yp, y2p, X_SECOND, Y_SECOND),
    )


def join_fine(load, planes, yr, at, ylo, yhi, *outs):
    sub = sub_index()
    for k in range(planes // 2):
        for z in range(2):
            above, below = yr[0, at + 2 * k + z] * yhi, yr[1, at + 2 * k + z] * ylo
            halos = (
                jnp.where(sub < 4, above, below),
                turn(jnp.where(sub < 4, below, above), 4),
            )
            for i in range(2):
                own = load(2 * k + i, z)
                for out in outs:
                    out[2 * k + i, z] = own
                    out[2 * k + i, 2 + z] = halos[i]


def join_weights(load, yr, at, out):
    sub = sub_index()
    for p in range(18):
        for z in range(2):
            tile, i = at + 2 * (p // 8) + z, p % 8
            above, below = turn(yr[0, tile], -i), turn(yr[1, tile], 7 - i)
            out[p, z] = load(p, z)
            out[p, 2 + z] = jnp.where(sub < 7, above, below)


def four_rows(own, above, below, i):
    sub = sub_index()
    turned = 4 * (1 - i)
    first = jnp.where(sub < 4, turn(own, 4 * i), turn(above, turned))
    return first, keep(sub >= 4, turn(below, turned))


def join_h1(yp, yr, at, *outs):
    ylo, yhi = flags()[2:4]
    for k in range(8):
        tile = at + k
        own, above, below = yp[tile], yr[0, tile] * yhi, yr[1, tile] * ylo
        for i in range(2):
            both = four_rows(own, above, below, i)
            for out in outs:
                out[2 * k + i, 0], out[2 * k + i, 1] = both


def join_w1(yp, yr, out):
    for k in range(5):
        tile = Y_FIRST["w1"] + k
        own, above, below = yp[tile], yr[0, tile], yr[1, tile]
        for i in range(2):
            p = 9 * i if k == 4 else 1 + 2 * k + i
            first, second = four_rows(own, above, below, i)
            out[p, 0], out[p, 1] = inverse(first), inverse(second)


def join_h2(yp, yr, at, *outs):
    ylo, yhi, ylo2, yhi2 = flags()[2:]
    sub = sub_index()
    for k in range(3):
        tile, far = at["h2"] + k, at["far"] + k
        own, above, below = yp[tile], yr[0, tile] * yhi, yr[1, tile] * ylo
        above2, below2 = yr[1, far + 3] * yhi2, yr[0, far] * ylo2
        for i in range(4):
            first = jnp.where(sub < 2, turn(own, -2 * i), turn(above, 2 - 2 * i))
            upper = keep(sub < 6, turn(above2, 4 - 2 * i))
            lower = jnp.where(sub < 6, turn(below2, 4 - 2 * i), turn(below, 6 - 2 * i))
            for out in outs:
                out[4 * k + i, 0] = jnp.where(sub < 4, first, upper)
                out[4 * k + i, 1] = keep(sub >= 4, lower)


def join_w2(yp, yr, out):
    sub = sub_index()
    for p in range(6):
        k, i = (1, p // 5) if p in (0, 5) else (0, p - 1)
        tile = Y_FIRST["w2"] + k
        own, above, below = yp[tile], yr[0, tile], yr[1, tile]
        first = jnp.where(sub < 2, turn(own, -2 * i), turn(above, 2 - 2 * i))
        out[p, 0] = inverse(keep(sub < 4, first))
        out[p, 1] = inverse(keep(sub >= 6, turn(below, 6 - 2 * i)))


def along_y(first, second):
    sub = sub_index()
    up_first, up_second = turn(first, 7), turn(second, 7)
    down_first, down_second = turn(first, 1), turn(second, 1)
    sides_first = jnp.where(sub == 7, up_second, up_first) + jnp.where(sub == 0, down_second, down_first)
    sides_second = jnp.where(sub == 7, up_first, up_second) + jnp.where(sub == 0, down_first, down_second)
    return (first + first) + sides_first, (second + second) + sides_second


def along_z_fine(left, right):
    lane = lane_index()
    up_left, up_right = pltpu.roll(left, 127, 1), pltpu.roll(right, 127, 1)
    down_left, down_right = pltpu.roll(left, 1, 1), pltpu.roll(right, 1, 1)
    sides_left = jnp.where(lane < 127, up_left, up_right) + keep(lane > 0, down_left)
    sides_right = keep(lane < 127, up_right) + jnp.where(lane > 0, down_right, down_left)
    return (left + left) + sides_left, (right + right) + sides_right


def along_z_coarse(tile):
    lane = lane_index()
    sides = keep(lane < 127, pltpu.roll(tile, 127, 1)) + keep(lane > 0, pltpu.roll(tile, 1, 1))
    return (tile + tile) + sides


def along_yz(tiles):
    tiles = list(tiles)
    if len(tiles) == 4:
        for z in range(2):
            tiles[z], tiles[2 + z] = along_y(tiles[z], tiles[2 + z])
        for y in range(2):
            tiles[2 * y], tiles[2 * y + 1] = along_z_fine(tiles[2 * y], tiles[2 * y + 1])
        return tiles
    return [along_z_coarse(tile) for tile in along_y(*tiles)]


def added(first, second):
    return [a + b for a, b in zip(first, second)]


def relax_planes(q, h, start, planes, parts, before, masks, factors, active):
    def load(x):
        return [q[x, part] for part in range(parts)]

    kept = KEEP if active is None else 1.0 + active * (KEEP - 1.0)
    here = load(start)
    below = added(before, here)
    for i in range(planes):
        x = start + i
        after = load(x + 1)
        above = added(here, after)
        summed = along_yz(added(below, above))
        for part in range(parts):
            spread = (masks[part // (parts // 2)] * factors[i]) * summed[part]
            source = h[x, part] if active is None else active * h[x, part]
            q[x, part] = (kept * here[part] + spread) + source
        last, here, below = here, after, above
    return last


def relax_levels(counts, h0, q0, h1, q1, h2, q2):
    lo, hi, ylo, yhi, ylo2, yhi2 = flags()
    sub, lane = sub_index(), lane_index()
    spread = jnp.full(TILE, SPREAD, F32)
    above = jnp.where(sub < 2, 1.0, jnp.where(sub < 4, yhi, jnp.where(sub < 6, yhi2, 0.0)))
    below = jnp.where(sub < 4, 0.0, jnp.where(sub < 6, ylo2, ylo))
    masks2 = (keep(lane < 64, above * spread), keep(lane < 64, below * spread))
    masks1 = (jnp.where(sub < 4, 1.0, yhi) * spread, jnp.where(sub < 4, 0.0, ylo) * spread)
    masks0 = (spread, jnp.where(sub < 4, yhi, ylo) * spread)

    def coarse_sweep(k, _):
        for q, h, planes, masks, count in ((q2, h2, 12, masks2, counts[2]), (q1, h1, 16, masks1, counts[1])):
            active = jnp.where(count > k, 1.0, 0.0)
            factors = [active * lo] * 3 + [active] * (planes - 8) + [active * hi] * 3
            before = [q[0, part] for part in range(2)]
            relax_planes(q, h, 1, planes - 2, 2, before, masks, factors, active)
        return 0

    def fine_sweep(_, __):
        def half(j, before):
            start = 1 + 11 * j
            factors = [
                jnp.where(start + i < 4, lo, jnp.where(start + i >= 20, hi, 1.0)) for i in range(11)
            ]
            return tuple(relax_planes(q0, h0, start, 11, 4, list(before), masks0, factors, None))

        lax.fori_loop(0, 2, half, tuple(q0[0, part] for part in range(4)))
        return 0

    lax.fori_loop(1, jnp.maximum(counts[1], counts[2]), coarse_sweep, 0)
    lax.fori_loop(1, counts[0], fine_sweep, 0)


def sweep_counts(own, cycle):
    held, sub, lane = own[0, OWN["counts"]], sub_index(), lane_index()
    return [
        jnp.max(keep((sub == cycle) & (lane == level), held)).astype(jnp.int32) for level in range(3)
    ]


def corrections(q1, iw1, q2, iw2, copies):
    sub = sub_index()
    one, two = (
        [
            jnp.where(sub < 7, q[p + 3, 0] * iw[p, 0], q[p + 3, 1] * iw[p, 1])
            for p in range(planes)
        ]
        for q, iw, planes in ((q1, iw1, 10), (q2, iw2, 6))
    )
    spread = []
    for tile in two:
        inner = jnp.where(sub < 3, turn(tile, 1), turn(tile, 2))
        spread.append(jnp.where((sub == 0) | (sub == 7), tile, inner))
    rows = [jnp.concatenate([one[p], spread[(p + 1) // 2]], axis=1) for p in range(10)]
    return exact_dot(jnp.concatenate(rows, axis=0), copies[...])


def iterate(coarse, q0, w, before, out):
    sub = sub_index()
    for k in range(10):
        for z in range(2):
            tile = coarse[8 * k : 8 * k + 8, 128 * z : 128 * z + 128]
            turned = [tile] + [turn(tile, by) for by in range(1, 5)]
            rows = turned[4]
            for by, last in ((3, 6), (2, 4), (1, 2), (0, 0)):
                rows = jnp.where(sub <= last, turned[by], rows)
            halo = jnp.where(sub < 7, turned[4], tile)
            for p in (2 * k - 1, 2 * k):
                if 0 <= p < 18:
                    for part, value in ((z, rows), (2 + z, halo)):
                        total = q0[p + 3, part] + w[p, part] * value
                        if before is not None:
                            total = before[p, part] + total
                        out[p, part] = total


def defects(pf):
    def load(p):
        return [pf[p, part] for part in range(4)]

    here = load(1)
    below = added(load(0), here)
    for x in range(16):
        after = load(x + 2)
        above = added(here, after)
        summed = along_yz(added(below, above))
        yield here[:2], [SELF_WEIGHT * here[z] - SIDE_CUBE * summed[z] for z in range(2)]
        here, below = after, above


def middle_kernel(
    own, coarse, xr, yp, yr, sums, copies,
    xp, pf, w, iw1, iw2, h0_next, h12_next,
    h0_all, q0, h1_all, q1, h2_all, q2,
):
    counts = sweep_counts(own, 0)
    lo, hi, ylo, yhi = flags()[:4]
    load = column_fine(lambda x, z: own[z, x], 4, xr, X_FIRST["h0"], lo, hi)
    join_fine(load, 24, yr, Y_FIRST["h0"], ylo, yhi, h0_all, q0)
    load = column_fine(lambda x, z: own[z, OWN["w"] + x], 1, xr, X_FIRST["w"], 1.0, 1.0)
    join_weights(load, yr, Y_FIRST["w"], w)
    join_h1(yp, yr, Y_FIRST["h1"], h1_all, q1)
    join_w1(yp, yr, iw1)
    join_h2(yp, yr, Y_FIRST, h2_all, q2)
    join_w2(yp, yr, iw2)
    relax_levels(counts, h0_all, q0, h1_all, q1, h2_all, q2)
    iterate(corrections(q1, iw1, q2, iw2, copies), q0, w, None, pf)

    rests = [[], []]
    for x, (_, defect) in enumerate(defects(pf)):
        for z in range(2):
            h0 = own[z, x] - LEVEL[0] * defect[z]
            h0_next[x, z] = h0
            rests[z].append(own[z, OWN["w"] + x] * h0)
    summed = [plane_sums(rest) for rest in rests]
    rows = [jnp.concatenate([summed[0][k], summed[1][k]], axis=1) for k in range(5)]
    total = exact_dot(jnp.concatenate(rows, axis=0), sums[...])
    h1 = []
    for k in range(4):
        weight = coarse[COARSE["w1"] + k]
        h1.append(0.5 * LEVEL[1] / LEVEL[0] * total[8 * k : 8 * k + 8, :128] / weight)
        h12_next[k] = h1[k]
    weight = inverse(coarse[COARSE["w2"]])
    h2 = 0.25 * LEVEL[2] / LEVEL[0] * total[32:40, 128:] * weight
    h12_next[4] = h2
    pack_x(lambda x, z: h0_next[x, z], h1, h2, xp, X_SECOND)


def last_kernel(
    own, m, f, h0, xr, yp, yr, pf, w, iw1, iw2, copies,
    solution_out, residual_out,
    h0_all, q0, h1_all, q1, h2_all, q2, pf_all, solved, left, sent,
):
    counts = sweep_counts(own, 1)
    lo, hi, ylo, yhi = flags()[:4]
    load = column_fine(lambda x, z: h0[x, z], 4, xr, X_SECOND["h0"], lo, hi)
    join_fine(load, 24, yr, Y_SECOND["h0"], ylo, yhi, h0_all, q0)
    join_h1(yp, yr, Y_SECOND["h1"], h1_all, q1)
    join_h2(yp, yr, Y_SECOND, h2_all, q2)
    relax_levels(counts, h0_all, q0, h1_all, q1, h2_all, q2)
    iterate(corrections(q1, iw1, q2, iw2, copies), q0, w, pf, pf_all)
    first = core() == 0
    sending = []
    for x, (here, defect) in enumerate(defects(pf_all)):
        mine, rest = (jnp.where(first, both[0], both[1]) for both in (here, defect))
        weight = m[x]
        solved[x] = mine / weight
        left[x] = f[x] - weight * rest
        if x % 4 == 3:
            done = pl.ds(x - 3, 4)
            for k, (source, target) in enumerate(((solved, solution_out), (left, residual_out))):
                copy = pltpu.make_async_copy(
                    source.at[done], target.at[done], sent.at[2 * (x // 4) + k]
                )
                copy.start()
                sending.append(copy)
    for copy in sending:
        copy.wait()


def call(kernel, outs, scratch, name, *operands, outside=0, outs_outside=False):
    whole = pl.BlockSpec(memory_space=pltpu.HBM)
    vmem = pl.BlockSpec(memory_space=pltpu.VMEM)
    return pl.pallas_call(
        kernel,
        out_shape=[jax.ShapeDtypeStruct(shape, F32) for shape in outs],
        in_specs=[whole] * outside + [vmem] * (len(operands) - outside),
        out_specs=[whole if outs_outside else vmem] * len(outs),
        scratch_shapes=scratch,
        compiler_params=pltpu.CompilerParams(vmem_limit_bytes=32 * 2**20),
        name=name,
    )(*(pltpu.with_memory_space_constraint(x, pltpu.HBM) for x in operands[:outside]), *operands[outside:])


def space(*dims):
    return pltpu.VMEM(tiles(*dims), F32)


def tiles(*dims):
    return (*dims, *TILE)


def share(value):
    return lax.all_gather(value, "group", axis=0)


def trade_x(packed):
    names = ("group", "gx", "gy")
    sizes = [lax.axis_size(name) for name in names]
    index = np.arange(np.prod(sizes)).reshape(sizes)
    inner = np.stack([index[0, :-1], index[1, 1:]], axis=-1).reshape(-1, 2)
    ends = np.concatenate([index[0, -1], index[1, 0]]).reshape(-1, 2)
    groups = np.concatenate([inner, ends]).tolist()
    return share(lax.all_gather(packed, names, axis=0, axis_index_groups=groups))


def trade_y(packed, packed_far):
    size = lax.axis_size("gy")
    moves = []
    for i in range(size - 1):
        moves += [(i, size + i + 1), (size + i + 1, i)]
    near = lax.ppermute(packed, ("group", "gy"), moves)
    groups = [[size + i, i + 2] for i in range(size - 2)]
    groups += [[0, 1], [2 * size - 2, 2 * size - 1]]
    far = lax.all_gather(packed_far, ("group", "gy"), axis=0, tiled=True, axis_index_groups=groups)
    return share(jnp.concatenate([near, far], axis=0))


def on_device(forcing, metric, sweeps):
    sums, copies = (jnp.asarray(matrix, jnp.bfloat16) for matrix in (WHOLE_SUMS, COPIES))
    spaces = [space(24, 4)] * 2 + [space(16, 2)] * 2 + [space(12, 2)] * 2

    (own,) = call(
        first_kernel,
        [tiles(OWN["size"])],
        [
            *(space(16), space(16), pltpu.VMEM(sweeps.shape, jnp.int32)),
            pltpu.SemaphoreType.DMA((3,)),
        ],
        "block_sums",
        *(metric, forcing, sweeps),
        outside=3,
    )
    own = share(own)
    xp, coarse = call(
        first_sides_kernel,
        [tiles(X_FIRST["size"]), tiles(COARSE["size"])],
        [],
        "first_sides",
        own,
    )
    xr = trade_x(xp)
    yp, y2p = call(
        first_rows_kernel,
        [tiles(Y_FIRST["size"]), tiles(3)],
        [],
        "first_rows",
        *(own, coarse, xr),
    )
    yr = trade_y(yp, y2p)
    xp, pf, w, iw1, iw2, h0, h12 = call(
        middle_kernel,
        [
            *(tiles(X_SECOND["size"]), tiles(18, 4), tiles(18, 4), tiles(10, 2), tiles(6, 2)),
            *(tiles(16, 2), tiles(5)),
        ],
        spaces,
        "first_cycle",
        *(own, coarse, xr, yp, yr, sums, copies),
    )
    xr = trade_x(xp)
    yp, y2p = call(
        second_rows_kernel,
        [tiles(Y_SECOND["size"]), tiles(3)],
        [],
        "second_rows",
        *(h0, h12, xr),
    )
    yr = trade_y(yp, y2p)
    return call(
        last_kernel,
        [tiles(16), tiles(16)],
        [*spaces, space(18, 4), space(16), space(16), pltpu.SemaphoreType.DMA((8,))],
        "second_cycle",
        *(own, metric, forcing, h0, xr, yp, yr, pf, w, iw1, iw2, copies),
        outs_outside=True,
    )


def solution(mesh):
    def program(forcing, metric, sweeps):
        return tuple(on_device(forcing, metric, sweeps))

    return jax.shard_map(
        program,
        mesh=mesh,
        in_specs=(P("gx", "gy", "group"), P("gx", "gy", "group"), P()),
        out_specs=(P("gx", "gy", "group"), P("gx", "gy", "group")),
        check_vma=False,
    )
```

```python
import jax
import jax.numpy as jnp
import numpy as np
from jax import lax
from jax.experimental import pallas as pl
from jax.experimental.pallas import tpu as pltpu
from jax.sharding import PartitionSpec as P

RELAXATION = 0.8
SIDE_WEIGHT = 0.05 ** (1.0 / 3.0)
SELF_WEIGHT = 3.4
SIDE_CUBE = SIDE_WEIGHT**3

KEEP = 1.0 - RELAXATION * SELF_WEIGHT / 3.0
SPREAD = RELAXATION * SIDE_CUBE / 3.0
LEVEL = [RELAXATION / (3.0 * 4.0**-level) for level in range(3)]

F32 = jnp.float32
TILE = (8, 128)

OWN = dict(h0=0, w=16, h1=32, w1=36, h2=40, w2=41, counts=42, size=43)
COARSE = dict(h1=0, w1=4, h2=8, w2=9, size=10)
X_FIRST = dict(h0=0, h1=8, h2=10, w=11, w12=13, size=14)
X_SECOND = dict(h0=0, h1=8, h2=10, size=11)
Y_FIRST = dict(h0=0, h1=24, h2=32, w=35, w12=41, size=43, far=43)
Y_SECOND = dict(h0=0, h1=24, h2=32, size=35, far=35)

LANES = np.arange(256)
WHOLE_SUMS = np.concatenate(
    [LANES[:, None] // 2 == LANES[None, :128], LANES[:, None] // 4 == LANES[None, :128]], axis=1
).astype(np.float32)
COPIES = WHOLE_SUMS.T * np.where(LANES[:, None] < 128, 0.5, 0.25).astype(np.float32)


def exact_dot(rows, matrix):
    parts = []
    rest = rows
    for _ in range(3):
        parts.append(rest.astype(jnp.bfloat16))
        rest = rest - parts[-1].astype(F32)
    out = lax.dot_general(
        jnp.concatenate(parts, axis=0),
        matrix,
        (((1,), (0,)), ((), ())),
        preferred_element_type=F32,
    )
    count = rows.shape[0]
    return out[:count] + (out[count : 2 * count] + out[2 * count :])


def sub_index():
    return lax.broadcasted_iota(jnp.int32, TILE, 0)


def lane_index():
    return lax.broadcasted_iota(jnp.int32, TILE, 1)


def turn(tile, by):
    by %= 8
    return pltpu.roll(tile, by, 0) if by else tile


def keep(where, tile):
    return jnp.where(where, tile, 0.0)


def inverse(tile):
    return jnp.where(tile > 0, 1.0 / jnp.where(tile > 0, tile, 1.0), 0.0)


def core():
    return lax.axis_index("group")


def flags():
    gx, gy = lax.axis_index("gx"), lax.axis_index("gy")
    x_last, y_last = lax.axis_size("gx") - 1, lax.axis_size("gy") - 1
    places = [gx > 0, gx < x_last, gy > 0, gy < y_last, gy > 1, gy < y_last - 1]
    return [place.astype(F32) for place in places]


def pair_rows(first, second):
    sub = sub_index()
    first, second = (tile + turn(tile, 7) for tile in (first, second))
    low = jnp.where(sub == 0, first, turn(first, 7))
    low = jnp.where(sub < 2, low, jnp.where(sub == 2, turn(first, 6), turn(first, 5)))
    high = jnp.where(sub == 4, turn(second, 4), turn(second, 3))
    high = jnp.where(sub < 6, high, jnp.where(sub == 6, turn(second, 2), turn(second, 1)))
    return jnp.where(sub < 4, low, high)


def plane_sums(fine):
    sub = sub_index()
    sums = [fine[2 * k] + fine[2 * k + 1] for k in range(8)]
    one = [pair_rows(sums[2 * k], sums[2 * k + 1]) for k in range(4)]
    two = None
    for k in range(4):
        both = one[k] + turn(one[k], 4)
        both = both + turn(both, 7)
        placed = jnp.where(sub == 2 * k, turn(both, 2 * k), turn(both, 2 * k - 1))
        two = placed if k == 0 else jnp.where(sub < 2 * k, two, placed)
    return one + [two]


def half_sums():
    row = lax.broadcasted_iota(jnp.int32, (128, 128), 0)
    column = lax.broadcasted_iota(jnp.int32, (128, 128), 1)
    matrix = jnp.concatenate([row >> 1 == column, row >> 2 == column], axis=1)
    return jnp.where(matrix, 1.0, 0.0).astype(jnp.bfloat16)


def first_kernel(m_whole, f_whole, sweeps_whole, out, m, f, sweeps, arrived):
    moves = ((m_whole, m), (f_whole, f), (sweeps_whole, sweeps))
    copies = [
        pltpu.make_async_copy(source, target, arrived.at[k])
        for k, (source, target) in enumerate(moves)
    ]
    for copy in copies:
        copy.start()
    sums = half_sums()
    copies[0].wait()
    m_tiles = [m[x] for x in range(16)]
    m_sums = plane_sums(m_tiles)
    for x in range(16):
        out[OWN["w"] + x] = m_tiles[x]
    for copy in copies[1:]:
        copy.wait()
    f_tiles = [f[x] for x in range(16)]
    for x in range(16):
        out[OWN["h0"] + x] = LEVEL[0] * f_tiles[x] / m_tiles[x]
    rows = jnp.concatenate(m_sums + plane_sums(f_tiles), axis=0)
    total = exact_dot(rows, sums)
    out[OWN["counts"]] = jnp.zeros(TILE, F32)
    out[OWN["counts"], : sweeps.shape[0], : sweeps.shape[1]] = sweeps[...].astype(F32)
    upper = core() == 1
    for k in range(5):
        left, width = (0, 64) if k < 4 else (128, 32)
        weight, force = (
            total[row : row + 8, left : left + 128] for row in (8 * k, 40 + 8 * k)
        )
        weight = (0.125 if k < 4 else 0.125 * 0.125) * weight
        force = (0.5 * LEVEL[1] if k < 4 else 0.25 * LEVEL[2]) * force * inverse(weight)
        weight, force = (
            jnp.where(upper, pltpu.roll(tile, width, 1), tile) for tile in (weight, force)
        )
        out[(OWN["w1"] + k) if k < 4 else OWN["w2"]] = weight
        out[(OWN["h1"] + k) if k < 4 else OWN["h2"]] = force


def pack_x(fine, h1, h2, xp, at):
    upward = core() == 0
    start = jnp.where(upward, 12, 0)
    for k in range(4):
        for z in range(2):
            xp[at["h0"] + 2 * k + z] = fine(start + k, z)
    for k in range(2):
        xp[at["h1"] + k] = jnp.where(upward, h1[2 + k], h1[k])
    xp[at["h2"]] = h2


def first_sides_kernel(own, xp, coarse):
    total = [own[0, k] + own[1, k] for k in range(OWN["h1"], OWN["counts"])]
    for k in range(COARSE["size"]):
        coarse[k] = total[k]
    h1, w1 = total[:4], total[4:8]
    h2, w2 = total[8:]
    pack_x(lambda x, z: own[z, x], h1, h2, xp, X_FIRST)
    upward = core() == 0
    edge = OWN["w"] + jnp.where(upward, 15, 0)
    for z in range(2):
        xp[X_FIRST["w"] + z] = own[z, edge]
    sub = sub_index()
    edge_one = jnp.where(upward, turn(w1[3], 4), w1[0])
    edge_two = jnp.where(upward, turn(w2, 6), turn(w2, 4))
    xp[X_FIRST["w12"]] = jnp.where(sub < 4, edge_one, edge_two)


def column_fine(own, planes, xr, at, lo, hi):
    def load(p, z):
        if p < planes:
            return xr[1, 0, at + 2 * p + z] * lo
        if p < 16 + planes:
            return own(p - planes, z)
        return xr[0, 1, at + 2 * (p - 16 - planes) + z] * hi

    return load


def pack_fine(load, planes, mine, yp, at):
    for k in range(planes // 2):
        for z in range(2):
            yp[at + 2 * k + z] = jnp.where(mine, load(2 * k, z), turn(load(2 * k + 1, z), 4))


def pack_y(own, h1, h2, xr, yp, y2p, x_at, at):
    lo, hi = flags()[:2]
    mine = (sub_index() < 4) == (core() == 1)
    pack_fine(column_fine(own, 4, xr, x_at["h0"], lo, hi), 24, mine, yp, at["h0"])
    for k in range(2):
        yp[at["h1"] + k] = xr[1, 0, x_at["h1"] + k] * lo
        yp[at["h1"] + 6 + k] = xr[0, 1, x_at["h1"] + k] * hi
    for k in range(4):
        yp[at["h1"] + 2 + k] = h1(k)
    two = [xr[1, 0, x_at["h2"]] * lo, h2(), xr[0, 1, x_at["h2"]] * hi]
    for k in range(3):
        yp[at["h2"] + k] = two[k]
        y2p[k] = two[k]


def column_w1(p, coarse, xr):
    if p in (0, 9):
        return (xr[1, 0, X_FIRST["w12"]] if p == 0 else xr[0, 1, X_FIRST["w12"]]), 0
    return coarse[COARSE["w1"] + (p - 1) // 2], 4 * ((p - 1) % 2)


def column_w2(p, coarse, xr):
    if p in (0, 5):
        return (xr[1, 0, X_FIRST["w12"]] if p == 0 else xr[0, 1, X_FIRST["w12"]]), 4
    return coarse[COARSE["w2"]], 2 * (p - 1)


def first_rows_kernel(own, coarse, xr, yp, y2p):
    at = Y_FIRST
    pack_y(
        lambda x, z: own[z, x],
        lambda k: coarse[k],
        lambda: coarse[COARSE["h2"]],
        *(xr, yp, y2p, X_FIRST, at),
    )
    sub = sub_index()
    weights = column_fine(lambda x, z: own[z, OWN["w"] + x], 1, xr, X_FIRST["w"], 1.0, 1.0)
    upward = core() == 0
    for k in range(3):
        for z in range(2):
            packed = None
            for i in range(min(8, 18 - 8 * k)):
                tile = weights(8 * k + i, z)
                row = turn(jnp.where(upward, turn(tile, 1), tile), i)
                packed = row if i == 0 else jnp.where(sub < i, packed, row)
            yp[at["w"] + 2 * k + z] = packed
    for k in range(2):
        packed = None
        for i in range(8):
            p = 8 * k + i
            if p < 10:
                (tile, start), last = column_w1(p, coarse, xr), 3
            else:
                (tile, start), last = column_w2(p - 10, coarse, xr), 1
            row = turn(jnp.where(upward, turn(tile, -start - last), turn(tile, -start)), i)
            packed = row if i == 0 else jnp.where(sub < i, packed, row)
        yp[at["w12"] + k] = packed


def second_rows_kernel(h0, h12, xr, yp, y2p):
    pack_y(
        lambda x, z: h0[x, z],
        lambda k: h12[k],
        lambda: h12[4],
        *(xr, yp, y2p, X_SECOND, Y_SECOND),
    )


def join_fine(load, planes, yr, at, ylo, yhi, *outs):
    sub = sub_index()
    for k in range(planes // 2):
        for z in range(2):
            above, below = yr[0, at + 2 * k + z] * yhi, yr[1, at + 2 * k + z] * ylo
            halos = (
                jnp.where(sub < 4, above, below),
                turn(jnp.where(sub < 4, below, above), 4),
            )
            for i in range(2):
                own = load(2 * k + i, z)
                for out in outs:
                    out[2 * k + i, z] = own
                    out[2 * k + i, 2 + z] = halos[i]


def join_weights(load, yr, at, out):
    sub = sub_index()
    for p in range(18):
        for z in range(2):
            tile, i = at + 2 * (p // 8) + z, p % 8
            above, below = turn(yr[0, tile], -i), turn(yr[1, tile], 7 - i)
            out[p, z] = load(p, z)
            out[p, 2 + z] = jnp.where(sub < 7, above, below)


def four_rows(own, above, below, i):
    sub = sub_index()
    turned = 4 * (1 - i)
    first = jnp.where(sub < 4, turn(own, 4 * i), turn(above, turned))
    return first, keep(sub >= 4, turn(below, turned))


def join_h1(yp, yr, at, *outs):
    ylo, yhi = flags()[2:4]
    for k in range(8):
        tile = at + k
        own, above, below = yp[tile], yr[0, tile] * yhi, yr[1, tile] * ylo
        for i in range(2):
            both = four_rows(own, above, below, i)
            for out in outs:
                out[2 * k + i, 0], out[2 * k + i, 1] = both


def join_coarse_weights(coarse, xr, yr, iw1, iw2):
    sub = sub_index()
    for p in range(16):
        packed, i = Y_FIRST["w12"] + p // 8, p % 8
        above, below = yr[0, packed], yr[1, packed]
        if p < 10:
            (tile, start), rows, out, plane = column_w1(p, coarse, xr), 4, iw1, p
        else:
            (tile, start), rows, out, plane = column_w2(p - 10, coarse, xr), 2, iw2, p - 10
        own = turn(tile, -start)
        out[plane, 0] = inverse(jnp.where(sub < rows, own, keep(sub == rows, turn(above, rows - i))))
        out[plane, 1] = inverse(keep(sub == 7, turn(below, 7 - i)))


def join_h2(yp, yr, at, *outs):
    ylo, yhi, ylo2, yhi2 = flags()[2:]
    sub = sub_index()
    for k in range(3):
        tile, far = at["h2"] + k, at["far"] + k
        own, above, below = yp[tile], yr[0, tile] * yhi, yr[1, tile] * ylo
        above2, below2 = yr[1, far + 3] * yhi2, yr[0, far] * ylo2
        for i in range(4):
            first = jnp.where(sub < 2, turn(own, -2 * i), turn(above, 2 - 2 * i))
            upper = keep(sub < 6, turn(above2, 4 - 2 * i))
            lower = jnp.where(sub < 6, turn(below2, 4 - 2 * i), turn(below, 6 - 2 * i))
            for out in outs:
                out[4 * k + i, 0] = jnp.where(sub < 4, first, upper)
                out[4 * k + i, 1] = keep(sub >= 4, lower)


def along_y(first, second):
    sub = sub_index()
    up_first, up_second = turn(first, 7), turn(second, 7)
    down_first, down_second = turn(first, 1), turn(second, 1)
    sides_first = jnp.where(sub == 7, up_second, up_first) + jnp.where(sub == 0, down_second, down_first)
    sides_second = jnp.where(sub == 7, up_first, up_second) + jnp.where(sub == 0, down_first, down_second)
    return (first + first) + sides_first, (second + second) + sides_second


def along_z_fine(left, right):
    lane = lane_index()
    up_left, up_right = pltpu.roll(left, 127, 1), pltpu.roll(right, 127, 1)
    down_left, down_right = pltpu.roll(left, 1, 1), pltpu.roll(right, 1, 1)
    sides_left = jnp.where(lane < 127, up_left, up_right) + keep(lane > 0, down_left)
    sides_right = keep(lane < 127, up_right) + jnp.where(lane > 0, down_right, down_left)
    return (left + left) + sides_left, (right + right) + sides_right


def along_z_coarse(tile):
    lane = lane_index()
    sides = keep(lane < 127, pltpu.roll(tile, 127, 1)) + keep(lane > 0, pltpu.roll(tile, 1, 1))
    return (tile + tile) + sides


def along_yz(tiles):
    tiles = list(tiles)
    if len(tiles) == 4:
        for z in range(2):
            tiles[z], tiles[2 + z] = along_y(tiles[z], tiles[2 + z])
        for y in range(2):
            tiles[2 * y], tiles[2 * y + 1] = along_z_fine(tiles[2 * y], tiles[2 * y + 1])
        return tiles
    return [along_z_coarse(tile) for tile in along_y(*tiles)]


def added(first, second):
    return [a + b for a, b in zip(first, second)]


def relax_planes(q, h, start, planes, parts, before, masks, factors, active):
    def load(x):
        return [q[x, part] for part in range(parts)]

    kept = KEEP if active is None else 1.0 + active * (KEEP - 1.0)
    here = load(start)
    below = added(before, here)
    for i in range(planes):
        x = start + i
        after = load(x + 1)
        above = added(here, after)
        summed = along_yz(added(below, above))
        for part in range(parts):
            mask = masks[part // (parts // 2)]
            spread = (mask if factors[i] is None else mask * factors[i]) * summed[part]
            source = h[x, part] if active is None else active * h[x, part]
            q[x, part] = (kept * here[part] + spread) + source
        here, below = after, above


def relax_levels(counts, h0, q0, h1, q1, h2, q2):
    lo, hi, ylo, yhi, ylo2, yhi2 = flags()
    sub, lane = sub_index(), lane_index()
    spread = jnp.full(TILE, SPREAD, F32)
    above = jnp.where(sub < 2, 1.0, jnp.where(sub < 4, yhi, jnp.where(sub < 6, yhi2, 0.0)))
    below = jnp.where(sub < 4, 0.0, jnp.where(sub < 6, ylo2, ylo))
    masks2 = (keep(lane < 64, above * spread), keep(lane < 64, below * spread))
    masks1 = (jnp.where(sub < 4, 1.0, yhi) * spread, jnp.where(sub < 4, 0.0, ylo) * spread)
    masks0 = (spread, jnp.where(sub < 4, yhi, ylo) * spread)

    def coarse_sweep(k, _):
        for q, h, planes, masks, count in ((q2, h2, 12, masks2, counts[2]), (q1, h1, 16, masks1, counts[1])):
            active = jnp.where(count > k, 1.0, 0.0)
            factors = [active * lo] * 3 + [active] * (planes - 8) + [active * hi] * 3
            before = [q[0, part] for part in range(2)]
            relax_planes(q, h, 1, planes - 2, 2, before, masks, factors, active)
        return 0

    def fine_sweep(_, __):
        factors = [lo] * 3 + [None] * 16 + [hi] * 3
        before = [q0[0, part] for part in range(4)]
        relax_planes(q0, h0, 1, 22, 4, before, masks0, factors, None)
        return 0

    lax.fori_loop(1, jnp.maximum(counts[1], counts[2]), coarse_sweep, 0)
    lax.fori_loop(1, counts[0], fine_sweep, 0)


def sweep_counts(own, cycle):
    held, sub, lane = own[0, OWN["counts"]], sub_index(), lane_index()
    return [
        jnp.max(keep((sub == cycle) & (lane == level), held)).astype(jnp.int32) for level in range(3)
    ]


def corrections(q1, iw1, q2, iw2, copies):
    sub = sub_index()
    one, two = (
        [
            jnp.where(sub < 7, q[p + 3, 0] * iw[p, 0], q[p + 3, 1] * iw[p, 1])
            for p in range(planes)
        ]
        for q, iw, planes in ((q1, iw1, 10), (q2, iw2, 6))
    )
    spread = []
    for tile in two:
        inner = jnp.where(sub < 3, turn(tile, 1), turn(tile, 2))
        spread.append(jnp.where((sub == 0) | (sub == 7), tile, inner))
    rows = [jnp.concatenate([one[p], spread[(p + 1) // 2]], axis=1) for p in range(10)]
    return exact_dot(jnp.concatenate(rows, axis=0), copies[...])


def iterate(coarse, q0, w, before, out):
    sub = sub_index()
    for k in range(10):
        for z in range(2):
            tile = coarse[8 * k : 8 * k + 8, 128 * z : 128 * z + 128]
            turned = [tile] + [turn(tile, by) for by in range(1, 5)]
            rows = turned[4]
            for by, last in ((3, 6), (2, 4), (1, 2), (0, 0)):
                rows = jnp.where(sub <= last, turned[by], rows)
            halo = jnp.where(sub < 7, turned[4], tile)
            for p in (2 * k - 1, 2 * k):
                if 0 <= p < 18:
                    for part, value in ((z, rows), (2 + z, halo)):
                        total = q0[p + 3, part] + w[p, part] * value
                        if before is not None:
                            total = before[p, part] + total
                        out[p, part] = total


def defects(pf):
    def load(p):
        return [pf[p, part] for part in range(4)]

    here = load(1)
    below = added(load(0), here)
    for x in range(16):
        after = load(x + 2)
        above = added(here, after)
        summed = along_yz(added(below, above))
        yield here[:2], [SELF_WEIGHT * here[z] - SIDE_CUBE * summed[z] for z in range(2)]
        here, below = after, above


def middle_kernel(
    own, coarse, xr, yp, yr, sums, copies,
    xp, pf, w, iw1, iw2, h0_next, h12_next,
    h0_all, q0, h1_all, q1, h2_all, q2,
):
    counts = sweep_counts(own, 0)
    lo, hi, ylo, yhi = flags()[:4]
    load = column_fine(lambda x, z: own[z, x], 4, xr, X_FIRST["h0"], lo, hi)
    join_fine(load, 24, yr, Y_FIRST["h0"], ylo, yhi, h0_all, q0)
    load = column_fine(lambda x, z: own[z, OWN["w"] + x], 1, xr, X_FIRST["w"], 1.0, 1.0)
    join_weights(load, yr, Y_FIRST["w"], w)
    join_h1(yp, yr, Y_FIRST["h1"], h1_all, q1)
    join_h2(yp, yr, Y_FIRST, h2_all, q2)
    join_coarse_weights(coarse, xr, yr, iw1, iw2)
    relax_levels(counts, h0_all, q0, h1_all, q1, h2_all, q2)
    iterate(corrections(q1, iw1, q2, iw2, copies), q0, w, None, pf)

    rests = [[], []]
    for x, (_, defect) in enumerate(defects(pf)):
        for z in range(2):
            h0 = own[z, x] - LEVEL[0] * defect[z]
            h0_next[x, z] = h0
            rests[z].append(own[z, OWN["w"] + x] * h0)
    summed = [plane_sums(rest) for rest in rests]
    rows = [jnp.concatenate([summed[0][k], summed[1][k]], axis=1) for k in range(5)]
    total = exact_dot(jnp.concatenate(rows, axis=0), sums[...])
    h1 = []
    for k in range(4):
        weight = coarse[COARSE["w1"] + k]
        h1.append(0.5 * LEVEL[1] / LEVEL[0] * total[8 * k : 8 * k + 8, :128] / weight)
        h12_next[k] = h1[k]
    weight = inverse(coarse[COARSE["w2"]])
    h2 = 0.25 * LEVEL[2] / LEVEL[0] * total[32:40, 128:] * weight
    h12_next[4] = h2
    pack_x(lambda x, z: h0_next[x, z], h1, h2, xp, X_SECOND)


def last_kernel(
    own, m, f, h0, xr, yp, yr, pf, w, iw1, iw2, copies,
    solution_out, residual_out,
    h0_all, q0, h1_all, q1, h2_all, q2, pf_all, solved, left, sent,
):
    counts = sweep_counts(own, 1)
    lo, hi, ylo, yhi = flags()[:4]
    load = column_fine(lambda x, z: h0[x, z], 4, xr, X_SECOND["h0"], lo, hi)
    join_fine(load, 24, yr, Y_SECOND["h0"], ylo, yhi, h0_all, q0)
    join_h1(yp, yr, Y_SECOND["h1"], h1_all, q1)
    join_h2(yp, yr, Y_SECOND, h2_all, q2)
    relax_levels(counts, h0_all, q0, h1_all, q1, h2_all, q2)
    iterate(corrections(q1, iw1, q2, iw2, copies), q0, w, pf, pf_all)
    first = core() == 0
    for x, (here, defect) in enumerate(defects(pf_all)):
        mine, rest = (jnp.where(first, both[0], both[1]) for both in (here, defect))
        weight = m[x]
        solved[x] = mine / weight
        left[x] = f[x] - weight * rest
    sends = [
        pltpu.make_async_copy(source, target, sent.at[k])
        for k, (source, target) in enumerate(((solved, solution_out), (left, residual_out)))
    ]
    for send in sends:
        send.start()
    for send in sends:
        send.wait()


def call(kernel, outs, scratch, name, *operands, outside=0, outs_outside=False):
    whole = pl.BlockSpec(memory_space=pltpu.HBM)
    vmem = pl.BlockSpec(memory_space=pltpu.VMEM)
    return pl.pallas_call(
        kernel,
        out_shape=[jax.ShapeDtypeStruct(shape, F32) for shape in outs],
        in_specs=[whole] * outside + [vmem] * (len(operands) - outside),
        out_specs=[whole if outs_outside else vmem] * len(outs),
        scratch_shapes=scratch,
        compiler_params=pltpu.CompilerParams(vmem_limit_bytes=32 * 2**20),
        name=name,
    )(*(pltpu.with_memory_space_constraint(x, pltpu.HBM) for x in operands[:outside]), *operands[outside:])


def space(*dims):
    return pltpu.VMEM(tiles(*dims), F32)


def tiles(*dims):
    return (*dims, *TILE)


def share(value):
    return lax.all_gather(value, "group", axis=0)


def trade_x(packed):
    names = ("group", "gx", "gy")
    sizes = [lax.axis_size(name) for name in names]
    index = np.arange(np.prod(sizes)).reshape(sizes)
    inner = np.stack([index[0, :-1], index[1, 1:]], axis=-1).reshape(-1, 2)
    ends = np.concatenate([index[0, -1], index[1, 0]]).reshape(-1, 2)
    groups = np.concatenate([inner, ends]).tolist()
    return share(lax.all_gather(packed, names, axis=0, axis_index_groups=groups))


def trade_y(packed, packed_far):
    size = lax.axis_size("gy")
    moves = []
    for i in range(size - 1):
        moves += [(i, size + i + 1), (size + i + 1, i)]
    near = lax.ppermute(packed, ("group", "gy"), moves)
    groups = [[size + i, i + 2] for i in range(size - 2)]
    groups += [[0, 1], [2 * size - 2, 2 * size - 1]]
    far = lax.all_gather(packed_far, ("group", "gy"), axis=0, tiled=True, axis_index_groups=groups)
    return share(jnp.concatenate([near, far], axis=0))


def on_device(forcing, metric, sweeps):
    sums, copies = (jnp.asarray(matrix, jnp.bfloat16) for matrix in (WHOLE_SUMS, COPIES))
    spaces = [space(24, 4)] * 2 + [space(16, 2)] * 2 + [space(12, 2)] * 2

    (own,) = call(
        first_kernel,
        [tiles(OWN["size"])],
        [
            *(space(16), space(16), pltpu.VMEM(sweeps.shape, jnp.int32)),
            pltpu.SemaphoreType.DMA((3,)),
        ],
        "block_sums",
        *(metric, forcing, sweeps),
        outside=3,
    )
    own = share(own)
    xp, coarse = call(
        first_sides_kernel,
        [tiles(X_FIRST["size"]), tiles(COARSE["size"])],
        [],
        "first_sides",
        own,
    )
    xr = trade_x(xp)
    yp, y2p = call(
        first_rows_kernel,
        [tiles(Y_FIRST["size"]), tiles(3)],
        [],
        "first_rows",
        *(own, coarse, xr),
    )
    yr = trade_y(yp, y2p)
    xp, pf, w, iw1, iw2, h0, h12 = call(
        middle_kernel,
        [
            *(tiles(X_SECOND["size"]), tiles(18, 4), tiles(18, 4), tiles(10, 2), tiles(6, 2)),
            *(tiles(16, 2), tiles(5)),
        ],
        spaces,
        "first_cycle",
        *(own, coarse, xr, yp, yr, sums, copies),
    )
    xr = trade_x(xp)
    yp, y2p = call(
        second_rows_kernel,
        [tiles(Y_SECOND["size"]), tiles(3)],
        [],
        "second_rows",
        *(h0, h12, xr),
    )
    yr = trade_y(yp, y2p)
    return call(
        last_kernel,
        [tiles(16), tiles(16)],
        [*spaces, space(18, 4), space(16), space(16), pltpu.SemaphoreType.DMA((2,))],
        "second_cycle",
        *(own, metric, forcing, h0, xr, yp, yr, pf, w, iw1, iw2, copies),
        outs_outside=True,
    )


def solution(mesh):
    def program(forcing, metric, sweeps):
        return tuple(on_device(forcing, metric, sweeps))

    return jax.shard_map(
        program,
        mesh=mesh,
        in_specs=(P("gx", "gy", "group"), P("gx", "gy", "group"), P()),
        out_specs=(P("gx", "gy", "group"), P("gx", "gy", "group")),
        check_vma=False,
    )
```

```python
import jax
import jax.numpy as jnp
import numpy as np
from jax import lax
from jax.experimental import pallas as pl
from jax.experimental.pallas import tpu as pltpu
from jax.sharding import PartitionSpec as P

RELAXATION = 0.8
SIDE_WEIGHT = 0.05 ** (1.0 / 3.0)
SELF_WEIGHT = 3.4
SIDE_CUBE = SIDE_WEIGHT**3

KEEP = 1.0 - RELAXATION * SELF_WEIGHT / 3.0
SPREAD = RELAXATION * SIDE_CUBE / 3.0
LEVEL = [RELAXATION / (3.0 * 4.0**-level) for level in range(3)]

F32 = jnp.float32
TILE = (8, 128)

OWN = dict(h0=0, w=16, h1=32, w1=36, h2=40, w2=41, counts=42, size=43)
COARSE = dict(h1=0, w1=4, h2=8, w2=9, size=10)
X_FIRST = dict(h0=0, h1=8, h2=10, w=11, w12=13, size=14)
X_SECOND = dict(h0=0, h1=8, h2=10, size=11)
Y_FIRST = dict(h0=0, h1=24, h2=32, w=35, w12=41, size=43, far=43)
Y_SECOND = dict(h0=0, h1=24, h2=32, size=35, far=35)

LANES = np.arange(256)
WHOLE_SUMS = np.concatenate(
    [LANES[:, None] // 2 == LANES[None, :128], LANES[:, None] // 4 == LANES[None, :128]], axis=1
).astype(np.float32)
COPIES = WHOLE_SUMS.T * np.where(LANES[:, None] < 128, 0.5, 0.25).astype(np.float32)


def exact_dot(rows, matrix):
    parts = []
    rest = rows
    for _ in range(3):
        parts.append(rest.astype(jnp.bfloat16))
        rest = rest - parts[-1].astype(F32)
    out = lax.dot_general(
        jnp.concatenate(parts, axis=0),
        matrix,
        (((1,), (0,)), ((), ())),
        preferred_element_type=F32,
    )
    count = rows.shape[0]
    return out[:count] + (out[count : 2 * count] + out[2 * count :])


def sub_index():
    return lax.broadcasted_iota(jnp.int32, TILE, 0)


def lane_index():
    return lax.broadcasted_iota(jnp.int32, TILE, 1)


def turn(tile, by):
    by %= 8
    return pltpu.roll(tile, by, 0) if by else tile


def keep(where, tile):
    return jnp.where(where, tile, 0.0)


def inverse(tile):
    return jnp.where(tile > 0, 1.0 / jnp.where(tile > 0, tile, 1.0), 0.0)


def core():
    return lax.axis_index("group")


def flags():
    gx, gy = lax.axis_index("gx"), lax.axis_index("gy")
    x_last, y_last = lax.axis_size("gx") - 1, lax.axis_size("gy") - 1
    places = [gx > 0, gx < x_last, gy > 0, gy < y_last, gy > 1, gy < y_last - 1]
    return [place.astype(F32) for place in places]


def pair_rows(first, second):
    sub = sub_index()
    first, second = (tile + turn(tile, 7) for tile in (first, second))
    low = jnp.where(sub == 0, first, turn(first, 7))
    low = jnp.where(sub < 2, low, jnp.where(sub == 2, turn(first, 6), turn(first, 5)))
    high = jnp.where(sub == 4, turn(second, 4), turn(second, 3))
    high = jnp.where(sub < 6, high, jnp.where(sub == 6, turn(second, 2), turn(second, 1)))
    return jnp.where(sub < 4, low, high)


def plane_sums(fine):
    sub = sub_index()
    sums = [fine[2 * k] + fine[2 * k + 1] for k in range(8)]
    one = [pair_rows(sums[2 * k], sums[2 * k + 1]) for k in range(4)]
    two = None
    for k in range(4):
        both = one[k] + turn(one[k], 4)
        both = both + turn(both, 7)
        placed = jnp.where(sub == 2 * k, turn(both, 2 * k), turn(both, 2 * k - 1))
        two = placed if k == 0 else jnp.where(sub < 2 * k, two, placed)
    return one + [two]


def half_sums():
    row = lax.broadcasted_iota(jnp.int32, (128, 128), 0)
    column = lax.broadcasted_iota(jnp.int32, (128, 128), 1)
    matrix = jnp.concatenate([row >> 1 == column, row >> 2 == column], axis=1)
    return jnp.where(matrix, 1.0, 0.0).astype(jnp.bfloat16)


def first_kernel(m_whole, f_whole, sweeps_whole, out, m, f, sweeps, arrived):
    moves = ((m_whole, m), (f_whole, f), (sweeps_whole, sweeps))
    copies = [
        pltpu.make_async_copy(source, target, arrived.at[k])
        for k, (source, target) in enumerate(moves)
    ]
    for copy in copies:
        copy.start()
    sums = half_sums()
    copies[0].wait()
    m_tiles = [m[x] for x in range(16)]
    m_sums = plane_sums(m_tiles)
    for x in range(16):
        out[OWN["w"] + x] = m_tiles[x]
    for copy in copies[1:]:
        copy.wait()
    f_tiles = [f[x] for x in range(16)]
    for x in range(16):
        out[OWN["h0"] + x] = LEVEL[0] * f_tiles[x] / m_tiles[x]
    rows = jnp.concatenate(m_sums + plane_sums(f_tiles), axis=0)
    total = exact_dot(rows, sums)
    out[OWN["counts"]] = jnp.zeros(TILE, F32)
    out[OWN["counts"], : sweeps.shape[0], : sweeps.shape[1]] = sweeps[...].astype(F32)
    upper = core() == 1
    for k in range(5):
        left, width = (0, 64) if k < 4 else (128, 32)
        weight, force = (
            total[row : row + 8, left : left + 128] for row in (8 * k, 40 + 8 * k)
        )
        weight = (0.125 if k < 4 else 0.125 * 0.125) * weight
        force = (0.5 * LEVEL[1] if k < 4 else 0.25 * LEVEL[2]) * force * inverse(weight)
        weight, force = (
            jnp.where(upper, pltpu.roll(tile, width, 1), tile) for tile in (weight, force)
        )
        out[(OWN["w1"] + k) if k < 4 else OWN["w2"]] = weight
        out[(OWN["h1"] + k) if k < 4 else OWN["h2"]] = force


def pack_x(fine, h1, h2, xp, at):
    upward = core() == 0
    start = jnp.where(upward, 12, 0)
    for k in range(4):
        for z in range(2):
            xp[at["h0"] + 2 * k + z] = fine(start + k, z)
    for k in range(2):
        xp[at["h1"] + k] = jnp.where(upward, h1[2 + k], h1[k])
    xp[at["h2"]] = h2


def first_sides_kernel(own, xp, coarse):
    total = [own[0, k] + own[1, k] for k in range(OWN["h1"], OWN["counts"])]
    for k in range(COARSE["size"]):
        coarse[k] = total[k]
    h1, w1 = total[:4], total[4:8]
    h2, w2 = total[8:]
    pack_x(lambda x, z: own[z, x], h1, h2, xp, X_FIRST)
    upward = core() == 0
    edge = OWN["w"] + jnp.where(upward, 15, 0)
    for z in range(2):
        xp[X_FIRST["w"] + z] = own[z, edge]
    sub = sub_index()
    edge_one = jnp.where(upward, turn(w1[3], 4), w1[0])
    edge_two = jnp.where(upward, turn(w2, 6), turn(w2, 4))
    xp[X_FIRST["w12"]] = jnp.where(sub < 4, edge_one, edge_two)


def column_fine(own, planes, xr, at, lo, hi):
    def load(p, z):
        if p < planes:
            return xr[1, 0, at + 2 * p + z] * lo
        if p < 16 + planes:
            return own(p - planes, z)
        return xr[0, 1, at + 2 * (p - 16 - planes) + z] * hi

    return load


def pack_fine(load, planes, mine, yp, at):
    for k in range(planes // 2):
        for z in range(2):
            yp[at + 2 * k + z] = jnp.where(mine, load(2 * k, z), turn(load(2 * k + 1, z), 4))


def pack_y(own, h1, h2, xr, yp, y2p, x_at, at):
    lo, hi = flags()[:2]
    mine = (sub_index() < 4) == (core() == 1)
    pack_fine(column_fine(own, 4, xr, x_at["h0"], lo, hi), 24, mine, yp, at["h0"])
    for k in range(2):
        yp[at["h1"] + k] = xr[1, 0, x_at["h1"] + k] * lo
        yp[at["h1"] + 6 + k] = xr[0, 1, x_at["h1"] + k] * hi
    for k in range(4):
        yp[at["h1"] + 2 + k] = h1(k)
    two = [xr[1, 0, x_at["h2"]] * lo, h2(), xr[0, 1, x_at["h2"]] * hi]
    for k in range(3):
        yp[at["h2"] + k] = two[k]
        y2p[k] = two[k]


def column_w1(p, coarse, xr):
    if p in (0, 9):
        return (xr[1, 0, X_FIRST["w12"]] if p == 0 else xr[0, 1, X_FIRST["w12"]]), 0
    return coarse[COARSE["w1"] + (p - 1) // 2], 4 * ((p - 1) % 2)


def column_w2(p, coarse, xr):
    if p in (0, 5):
        return (xr[1, 0, X_FIRST["w12"]] if p == 0 else xr[0, 1, X_FIRST["w12"]]), 4
    return coarse[COARSE["w2"]], 2 * (p - 1)


def first_rows_kernel(own, coarse, xr, yp, y2p):
    at = Y_FIRST
    pack_y(
        lambda x, z: own[z, x],
        lambda k: coarse[k],
        lambda: coarse[COARSE["h2"]],
        *(xr, yp, y2p, X_FIRST, at),
    )
    sub = sub_index()
    weights = column_fine(lambda x, z: own[z, OWN["w"] + x], 1, xr, X_FIRST["w"], 1.0, 1.0)
    upward = core() == 0
    for k in range(3):
        for z in range(2):
            packed = None
            for i in range(min(8, 18 - 8 * k)):
                tile = weights(8 * k + i, z)
                row = turn(jnp.where(upward, turn(tile, 1), tile), i)
                packed = row if i == 0 else jnp.where(sub < i, packed, row)
            yp[at["w"] + 2 * k + z] = packed
    for k in range(2):
        packed = None
        for i in range(8):
            p = 8 * k + i
            if p < 10:
                (tile, start), last = column_w1(p, coarse, xr), 3
            else:
                (tile, start), last = column_w2(p - 10, coarse, xr), 1
            row = turn(jnp.where(upward, turn(tile, -start - last), turn(tile, -start)), i)
            packed = row if i == 0 else jnp.where(sub < i, packed, row)
        yp[at["w12"] + k] = packed


def second_rows_kernel(h0, h12, xr, yp, y2p):
    pack_y(
        lambda x, z: h0[x, z],
        lambda k: h12[k],
        lambda: h12[4],
        *(xr, yp, y2p, X_SECOND, Y_SECOND),
    )


def join_fine(load, planes, yr, at, ylo, yhi, *outs):
    sub = sub_index()
    for k in range(planes // 2):
        for z in range(2):
            above, below = yr[0, at + 2 * k + z] * yhi, yr[1, at + 2 * k + z] * ylo
            halos = (
                jnp.where(sub < 4, above, below),
                turn(jnp.where(sub < 4, below, above), 4),
            )
            for i in range(2):
                own = load(2 * k + i, z)
                for out in outs:
                    out[2 * k + i, z] = own
                    out[2 * k + i, 2 + z] = halos[i]


def join_weights(load, yr, at, out):
    sub = sub_index()
    for p in range(18):
        for z in range(2):
            tile, i = at + 2 * (p // 8) + z, p % 8
            above, below = turn(yr[0, tile], -i), turn(yr[1, tile], 7 - i)
            out[p, z] = load(p, z)
            out[p, 2 + z] = jnp.where(sub < 7, above, below)


def four_rows(own, above, below, i):
    sub = sub_index()
    turned = 4 * (1 - i)
    first = jnp.where(sub < 4, turn(own, 4 * i), turn(above, turned))
    return first, keep(sub >= 4, turn(below, turned))


def join_h1(yp, yr, at, *outs):
    ylo, yhi = flags()[2:4]
    for k in range(8):
        tile = at + k
        own, above, below = yp[tile], yr[0, tile] * yhi, yr[1, tile] * ylo
        for i in range(2):
            both = four_rows(own, above, below, i)
            for out in outs:
                out[2 * k + i, 0], out[2 * k + i, 1] = both


def join_coarse_weights(coarse, xr, yr, iw1, iw2):
    sub = sub_index()
    for p in range(16):
        packed, i = Y_FIRST["w12"] + p // 8, p % 8
        above, below = yr[0, packed], yr[1, packed]
        if p < 10:
            (tile, start), rows, out, plane = column_w1(p, coarse, xr), 4, iw1, p
        else:
            (tile, start), rows, out, plane = column_w2(p - 10, coarse, xr), 2, iw2, p - 10
        own = turn(tile, -start)
        out[plane, 0] = inverse(jnp.where(sub < rows, own, keep(sub == rows, turn(above, rows - i))))
        out[plane, 1] = inverse(keep(sub == 7, turn(below, 7 - i)))


def join_h2(yp, yr, at, *outs):
    ylo, yhi, ylo2, yhi2 = flags()[2:]
    sub = sub_index()
    for k in range(3):
        tile, far = at["h2"] + k, at["far"] + k
        own, above, below = yp[tile], yr[0, tile] * yhi, yr[1, tile] * ylo
        above2, below2 = yr[1, far + 3] * yhi2, yr[0, far] * ylo2
        for i in range(4):
            first = jnp.where(sub < 2, turn(own, -2 * i), turn(above, 2 - 2 * i))
            upper = keep(sub < 6, turn(above2, 4 - 2 * i))
            lower = jnp.where(sub < 6, turn(below2, 4 - 2 * i), turn(below, 6 - 2 * i))
            for out in outs:
                out[4 * k + i, 0] = jnp.where(sub < 4, first, upper)
                out[4 * k + i, 1] = keep(sub >= 4, lower)


def along_y(first, second):
    sub = sub_index()
    up_first, up_second = turn(first, 7), turn(second, 7)
    down_first, down_second = turn(first, 1), turn(second, 1)
    sides_first = jnp.where(sub == 7, up_second, up_first) + jnp.where(sub == 0, down_second, down_first)
    sides_second = jnp.where(sub == 7, up_first, up_second) + jnp.where(sub == 0, down_first, down_second)
    return (first + first) + sides_first, (second + second) + sides_second


def along_z_fine(left, right):
    lane = lane_index()
    up_left, up_right = pltpu.roll(left, 127, 1), pltpu.roll(right, 127, 1)
    down_left, down_right = pltpu.roll(left, 1, 1), pltpu.roll(right, 1, 1)
    sides_left = jnp.where(lane < 127, up_left, up_right) + keep(lane > 0, down_left)
    sides_right = keep(lane < 127, up_right) + jnp.where(lane > 0, down_right, down_left)
    return (left + left) + sides_left, (right + right) + sides_right


def along_z_coarse(tile):
    lane = lane_index()
    sides = keep(lane < 127, pltpu.roll(tile, 127, 1)) + keep(lane > 0, pltpu.roll(tile, 1, 1))
    return (tile + tile) + sides


def along_yz(tiles):
    tiles = list(tiles)
    if len(tiles) == 4:
        for z in range(2):
            tiles[z], tiles[2 + z] = along_y(tiles[z], tiles[2 + z])
        for y in range(2):
            tiles[2 * y], tiles[2 * y + 1] = along_z_fine(tiles[2 * y], tiles[2 * y + 1])
        return tiles
    return [along_z_coarse(tile) for tile in along_y(*tiles)]


def added(first, second):
    return [a + b for a, b in zip(first, second)]


def relax_planes(q, h, start, planes, parts, before, masks, factors, active):
    def load(x):
        return [q[x, part] for part in range(parts)]

    kept = KEEP if active is None else 1.0 + active * (KEEP - 1.0)
    here = load(start)
    below = added(before, here)
    for i in range(planes):
        x = start + i
        after = load(x + 1)
        above = added(here, after)
        summed = along_yz(added(below, above))
        for part in range(parts):
            mask = masks[part // (parts // 2)]
            spread = (mask if factors[i] is None else mask * factors[i]) * summed[part]
            source = h[x, part] if active is None else active * h[x, part]
            q[x, part] = (kept * here[part] + spread) + source
        here, below = after, above


def relax_levels(counts, h0, q0, h1, q1, h2, q2):
    lo, hi, ylo, yhi, ylo2, yhi2 = flags()
    sub, lane = sub_index(), lane_index()
    spread = jnp.full(TILE, SPREAD, F32)
    above = jnp.where(sub < 2, 1.0, jnp.where(sub < 4, yhi, jnp.where(sub < 6, yhi2, 0.0)))
    below = jnp.where(sub < 4, 0.0, jnp.where(sub < 6, ylo2, ylo))
    masks2 = (keep(lane < 64, above * spread), keep(lane < 64, below * spread))
    masks1 = (jnp.where(sub < 4, 1.0, yhi) * spread, jnp.where(sub < 4, 0.0, ylo) * spread)
    masks0 = (spread, jnp.where(sub < 4, yhi, ylo) * spread)

    def coarse_sweep(k, _):
        for q, h, planes, masks, count in ((q2, h2, 12, masks2, counts[2]), (q1, h1, 16, masks1, counts[1])):
            active = jnp.where(count > k, 1.0, 0.0)
            factors = [active * lo] * 3 + [active] * (planes - 8) + [active * hi] * 3
            before = [q[0, part] for part in range(2)]
            relax_planes(q, h, 1, planes - 2, 2, before, masks, factors, active)
        return 0

    def fine_sweep(_, __):
        factors = [lo] * 3 + [None] * 16 + [hi] * 3
        before = [q0[0, part] for part in range(4)]
        relax_planes(q0, h0, 1, 22, 4, before, masks0, factors, None)
        return 0

    def both_sweeps(k, _):
        coarse_sweep(k, 0)
        return fine_sweep(k, 0)

    coarse_count = jnp.maximum(counts[1], counts[2])
    shared = jnp.minimum(counts[0], coarse_count)
    lax.fori_loop(1, shared, both_sweeps, 0)
    lax.fori_loop(shared, coarse_count, coarse_sweep, 0)
    lax.fori_loop(shared, counts[0], fine_sweep, 0)


def sweep_counts(own, cycle):
    held, sub, lane = own[0, OWN["counts"]], sub_index(), lane_index()
    return [
        jnp.max(keep((sub == cycle) & (lane == level), held)).astype(jnp.int32) for level in range(3)
    ]


def corrections(q1, iw1, q2, iw2, copies):
    sub = sub_index()
    one, two = (
        [
            jnp.where(sub < 7, q[p + 3, 0] * iw[p, 0], q[p + 3, 1] * iw[p, 1])
            for p in range(planes)
        ]
        for q, iw, planes in ((q1, iw1, 10), (q2, iw2, 6))
    )
    spread = []
    for tile in two:
        inner = jnp.where(sub < 3, turn(tile, 1), turn(tile, 2))
        spread.append(jnp.where((sub == 0) | (sub == 7), tile, inner))
    rows = [jnp.concatenate([one[p], spread[(p + 1) // 2]], axis=1) for p in range(10)]
    return exact_dot(jnp.concatenate(rows, axis=0), copies[...])


def iterate(coarse, q0, w, before, out):
    sub = sub_index()
    for k in range(10):
        for z in range(2):
            tile = coarse[8 * k : 8 * k + 8, 128 * z : 128 * z + 128]
            turned = [tile] + [turn(tile, by) for by in range(1, 5)]
            rows = turned[4]
            for by, last in ((3, 6), (2, 4), (1, 2), (0, 0)):
                rows = jnp.where(sub <= last, turned[by], rows)
            halo = jnp.where(sub < 7, turned[4], tile)
            for p in (2 * k - 1, 2 * k):
                if 0 <= p < 18:
                    for part, value in ((z, rows), (2 + z, halo)):
                        total = q0[p + 3, part] + w[p, part] * value
                        if before is not None:
                            total = before[p, part] + total
                        out[p, part] = total


def defects(pf):
    def load(p):
        return [pf[p, part] for part in range(4)]

    here = load(1)
    below = added(load(0), here)
    for x in range(16):
        after = load(x + 2)
        above = added(here, after)
        summed = along_yz(added(below, above))
        yield here[:2], [SELF_WEIGHT * here[z] - SIDE_CUBE * summed[z] for z in range(2)]
        here, below = after, above


def middle_kernel(
    own, coarse, xr, yp, yr, sums, copies,
    xp, pf, w, iw1, iw2, h0_next, h12_next,
    h0_all, q0, h1_all, q1, h2_all, q2,
):
    counts = sweep_counts(own, 0)
    lo, hi, ylo, yhi = flags()[:4]
    load = column_fine(lambda x, z: own[z, x], 4, xr, X_FIRST["h0"], lo, hi)
    join_fine(load, 24, yr, Y_FIRST["h0"], ylo, yhi, h0_all, q0)
    load = column_fine(lambda x, z: own[z, OWN["w"] + x], 1, xr, X_FIRST["w"], 1.0, 1.0)
    join_weights(load, yr, Y_FIRST["w"], w)
    join_h1(yp, yr, Y_FIRST["h1"], h1_all, q1)
    join_h2(yp, yr, Y_FIRST, h2_all, q2)
    join_coarse_weights(coarse, xr, yr, iw1, iw2)
    relax_levels(counts, h0_all, q0, h1_all, q1, h2_all, q2)
    iterate(corrections(q1, iw1, q2, iw2, copies), q0, w, None, pf)

    rests = [[], []]
    for x, (_, defect) in enumerate(defects(pf)):
        for z in range(2):
            h0 = own[z, x] - LEVEL[0] * defect[z]
            h0_next[x, z] = h0
            rests[z].append(own[z, OWN["w"] + x] * h0)
    summed = [plane_sums(rest) for rest in rests]
    rows = [jnp.concatenate([summed[0][k], summed[1][k]], axis=1) for k in range(5)]
    total = exact_dot(jnp.concatenate(rows, axis=0), sums[...])
    h1 = []
    for k in range(4):
        weight = coarse[COARSE["w1"] + k]
        h1.append(0.5 * LEVEL[1] / LEVEL[0] * total[8 * k : 8 * k + 8, :128] / weight)
        h12_next[k] = h1[k]
    weight = inverse(coarse[COARSE["w2"]])
    h2 = 0.25 * LEVEL[2] / LEVEL[0] * total[32:40, 128:] * weight
    h12_next[4] = h2
    pack_x(lambda x, z: h0_next[x, z], h1, h2, xp, X_SECOND)


def last_kernel(
    own, m, f, h0, xr, yp, yr, pf, w, iw1, iw2, copies,
    solution_out, residual_out,
    h0_all, q0, h1_all, q1, h2_all, q2, pf_all, solved, left, sent,
):
    counts = sweep_counts(own, 1)
    lo, hi, ylo, yhi = flags()[:4]
    load = column_fine(lambda x, z: h0[x, z], 4, xr, X_SECOND["h0"], lo, hi)
    join_fine(load, 24, yr, Y_SECOND["h0"], ylo, yhi, h0_all, q0)
    join_h1(yp, yr, Y_SECOND["h1"], h1_all, q1)
    join_h2(yp, yr, Y_SECOND, h2_all, q2)
    relax_levels(counts, h0_all, q0, h1_all, q1, h2_all, q2)
    iterate(corrections(q1, iw1, q2, iw2, copies), q0, w, pf, pf_all)
    first = core() == 0
    for x, (here, defect) in enumerate(defects(pf_all)):
        mine, rest = (jnp.where(first, both[0], both[1]) for both in (here, defect))
        weight = m[x]
        solved[x] = mine / weight
        left[x] = f[x] - weight * rest
    sends = [
        pltpu.make_async_copy(source, target, sent.at[k])
        for k, (source, target) in enumerate(((solved, solution_out), (left, residual_out)))
    ]
    for send in sends:
        send.start()
    for send in sends:
        send.wait()


def call(kernel, outs, scratch, name, *operands, outside=0, outs_outside=False):
    whole = pl.BlockSpec(memory_space=pltpu.HBM)
    vmem = pl.BlockSpec(memory_space=pltpu.VMEM)
    return pl.pallas_call(
        kernel,
        out_shape=[jax.ShapeDtypeStruct(shape, F32) for shape in outs],
        in_specs=[whole] * outside + [vmem] * (len(operands) - outside),
        out_specs=[whole if outs_outside else vmem] * len(outs),
        scratch_shapes=scratch,
        compiler_params=pltpu.CompilerParams(vmem_limit_bytes=32 * 2**20),
        name=name,
    )(*(pltpu.with_memory_space_constraint(x, pltpu.HBM) for x in operands[:outside]), *operands[outside:])


def space(*dims):
    return pltpu.VMEM(tiles(*dims), F32)


def tiles(*dims):
    return (*dims, *TILE)


def share(value):
    return lax.all_gather(value, "group", axis=0)


def trade_x(packed):
    names = ("group", "gx", "gy")
    sizes = [lax.axis_size(name) for name in names]
    index = np.arange(np.prod(sizes)).reshape(sizes)
    inner = np.stack([index[0, :-1], index[1, 1:]], axis=-1).reshape(-1, 2)
    ends = np.concatenate([index[0, -1], index[1, 0]]).reshape(-1, 2)
    groups = np.concatenate([inner, ends]).tolist()
    return share(lax.all_gather(packed, names, axis=0, axis_index_groups=groups))


def trade_y(packed, packed_far):
    size = lax.axis_size("gy")
    moves = []
    for i in range(size - 1):
        moves += [(i, size + i + 1), (size + i + 1, i)]
    near = lax.ppermute(packed, ("group", "gy"), moves)
    groups = [[size + i, i + 2] for i in range(size - 2)]
    groups += [[0, 1], [2 * size - 2, 2 * size - 1]]
    far = lax.all_gather(packed_far, ("group", "gy"), axis=0, tiled=True, axis_index_groups=groups)
    return share(jnp.concatenate([near, far], axis=0))


def on_device(forcing, metric, sweeps):
    sums, copies = (jnp.asarray(matrix, jnp.bfloat16) for matrix in (WHOLE_SUMS, COPIES))
    spaces = [space(24, 4)] * 2 + [space(16, 2)] * 2 + [space(12, 2)] * 2

    (own,) = call(
        first_kernel,
        [tiles(OWN["size"])],
        [
            *(space(16), space(16), pltpu.VMEM(sweeps.shape, jnp.int32)),
            pltpu.SemaphoreType.DMA((3,)),
        ],
        "block_sums",
        *(metric, forcing, sweeps),
        outside=3,
    )
    own = share(own)
    xp, coarse = call(
        first_sides_kernel,
        [tiles(X_FIRST["size"]), tiles(COARSE["size"])],
        [],
        "first_sides",
        own,
    )
    xr = trade_x(xp)
    yp, y2p = call(
        first_rows_kernel,
        [tiles(Y_FIRST["size"]), tiles(3)],
        [],
        "first_rows",
        *(own, coarse, xr),
    )
    yr = trade_y(yp, y2p)
    xp, pf, w, iw1, iw2, h0, h12 = call(
        middle_kernel,
        [
            *(tiles(X_SECOND["size"]), tiles(18, 4), tiles(18, 4), tiles(10, 2), tiles(6, 2)),
            *(tiles(16, 2), tiles(5)),
        ],
        spaces,
        "first_cycle",
        *(own, coarse, xr, yp, yr, sums, copies),
    )
    xr = trade_x(xp)
    yp, y2p = call(
        second_rows_kernel,
        [tiles(Y_SECOND["size"]), tiles(3)],
        [],
        "second_rows",
        *(h0, h12, xr),
    )
    yr = trade_y(yp, y2p)
    return call(
        last_kernel,
        [tiles(16), tiles(16)],
        [*spaces, space(18, 4), space(16), space(16), pltpu.SemaphoreType.DMA((2,))],
        "second_cycle",
        *(own, metric, forcing, h0, xr, yp, yr, pf, w, iw1, iw2, copies),
        outs_outside=True,
    )


def solution(mesh):
    def program(forcing, metric, sweeps):
        return tuple(on_device(forcing, metric, sweeps))

    return jax.shard_map(
        program,
        mesh=mesh,
        in_specs=(P("gx", "gy", "group"), P("gx", "gy", "group"), P()),
        out_specs=(P("gx", "gy", "group"), P("gx", "gy", "group")),
        check_vma=False,
    )
```

```python
import jax
import jax.numpy as jnp
import numpy as np
from jax import lax
from jax.experimental import pallas as pl
from jax.experimental.pallas import tpu as pltpu
from jax.sharding import PartitionSpec as P

RELAXATION = 0.8
SIDE_WEIGHT = 0.05 ** (1.0 / 3.0)
SELF_WEIGHT = 3.4
SIDE_CUBE = SIDE_WEIGHT**3

KEEP = 1.0 - RELAXATION * SELF_WEIGHT / 3.0
SPREAD = RELAXATION * SIDE_CUBE / 3.0
LEVEL = [RELAXATION / (3.0 * 4.0**-level) for level in range(3)]

F32 = jnp.float32
TILE = (8, 128)

OWN = dict(h0=0, w=16, h1=32, w1=36, h2=40, w2=41, counts=42, size=43)
COARSE = dict(h1=0, w1=4, h2=8, w2=9, size=10)
X_FIRST = dict(h0=0, h1=8, h2=10, w=11, w12=13, size=14)
X_SECOND = dict(h0=0, h1=8, h2=10, size=11)
Y_FIRST = dict(h0=0, h1=24, h2=32, w=35, w12=41, size=43, far=43)
Y_SECOND = dict(h0=0, h1=24, h2=32, size=35, far=35)

LANES = np.arange(256)
WHOLE_SUMS = np.concatenate(
    [LANES[:, None] // 2 == LANES[None, :128], LANES[:, None] // 4 == LANES[None, :128]], axis=1
).astype(np.float32)
COPIES = WHOLE_SUMS.T * np.where(LANES[:, None] < 128, 0.5, 0.25).astype(np.float32)


def exact_dot(rows, matrix):
    parts = []
    rest = rows
    for _ in range(3):
        parts.append(rest.astype(jnp.bfloat16))
        rest = rest - parts[-1].astype(F32)
    out = lax.dot_general(
        jnp.concatenate(parts, axis=0),
        matrix,
        (((1,), (0,)), ((), ())),
        preferred_element_type=F32,
    )
    count = rows.shape[0]
    return out[:count] + (out[count : 2 * count] + out[2 * count :])


def sub_index():
    return lax.broadcasted_iota(jnp.int32, TILE, 0)


def lane_index():
    return lax.broadcasted_iota(jnp.int32, TILE, 1)


def turn(tile, by):
    by %= 8
    return pltpu.roll(tile, by, 0) if by else tile


def keep(where, tile):
    return jnp.where(where, tile, 0.0)


def inverse(tile):
    return jnp.where(tile > 0, 1.0 / jnp.where(tile > 0, tile, 1.0), 0.0)


def core():
    return lax.axis_index("group")


def odd_x():
    return lax.rem(lax.axis_index("gx"), 2)


def upward_x():
    return core() == odd_x()


def flags():
    gx, gy = lax.axis_index("gx"), lax.axis_index("gy")
    x_last, y_last = lax.axis_size("gx") - 1, lax.axis_size("gy") - 1
    places = [gx > 0, gx < x_last, gy > 0, gy < y_last, gy > 1, gy < y_last - 1]
    return [place.astype(F32) for place in places]


def pair_rows(first, second):
    sub = sub_index()
    first, second = (tile + turn(tile, 7) for tile in (first, second))
    low = jnp.where(sub == 0, first, turn(first, 7))
    low = jnp.where(sub < 2, low, jnp.where(sub == 2, turn(first, 6), turn(first, 5)))
    high = jnp.where(sub == 4, turn(second, 4), turn(second, 3))
    high = jnp.where(sub < 6, high, jnp.where(sub == 6, turn(second, 2), turn(second, 1)))
    return jnp.where(sub < 4, low, high)


def plane_sums(fine):
    sub = sub_index()
    sums = [fine[2 * k] + fine[2 * k + 1] for k in range(8)]
    one = [pair_rows(sums[2 * k], sums[2 * k + 1]) for k in range(4)]
    two = None
    for k in range(4):
        both = one[k] + turn(one[k], 4)
        both = both + turn(both, 7)
        placed = jnp.where(sub == 2 * k, turn(both, 2 * k), turn(both, 2 * k - 1))
        two = placed if k == 0 else jnp.where(sub < 2 * k, two, placed)
    return one + [two]


def half_sums():
    row = lax.broadcasted_iota(jnp.int32, (128, 128), 0)
    column = lax.broadcasted_iota(jnp.int32, (128, 128), 1)
    matrix = jnp.concatenate([row >> 1 == column, row >> 2 == column], axis=1)
    return jnp.where(matrix, 1.0, 0.0).astype(jnp.bfloat16)


def first_kernel(m_whole, f_whole, sweeps_whole, out, m, f, sweeps, arrived):
    moves = ((m_whole, m), (f_whole, f), (sweeps_whole, sweeps))
    copies = [
        pltpu.make_async_copy(source, target, arrived.at[k])
        for k, (source, target) in enumerate(moves)
    ]
    for copy in copies:
        copy.start()
    sums = half_sums()
    copies[0].wait()
    m_tiles = [m[x] for x in range(16)]
    m_sums = plane_sums(m_tiles)
    for x in range(16):
        out[OWN["w"] + x] = m_tiles[x]
    for copy in copies[1:]:
        copy.wait()
    f_tiles = [f[x] for x in range(16)]
    for x in range(16):
        out[OWN["h0"] + x] = LEVEL[0] * f_tiles[x] / m_tiles[x]
    rows = jnp.concatenate(m_sums + plane_sums(f_tiles), axis=0)
    total = exact_dot(rows, sums)
    out[OWN["counts"]] = jnp.zeros(TILE, F32)
    out[OWN["counts"], : sweeps.shape[0], : sweeps.shape[1]] = sweeps[...].astype(F32)
    upper = core() == 1
    for k in range(5):
        left, width = (0, 64) if k < 4 else (128, 32)
        weight, force = (
            total[row : row + 8, left : left + 128] for row in (8 * k, 40 + 8 * k)
        )
        weight = (0.125 if k < 4 else 0.125 * 0.125) * weight
        force = (0.5 * LEVEL[1] if k < 4 else 0.25 * LEVEL[2]) * force * inverse(weight)
        weight, force = (
            jnp.where(upper, pltpu.roll(tile, width, 1), tile) for tile in (weight, force)
        )
        out[(OWN["w1"] + k) if k < 4 else OWN["w2"]] = weight
        out[(OWN["h1"] + k) if k < 4 else OWN["h2"]] = force


def pack_x(fine, h1, h2, xp, at):
    upward = upward_x()
    start = jnp.where(upward, 12, 0)
    for k in range(4):
        for z in range(2):
            xp[at["h0"] + 2 * k + z] = fine(start + k, z)
    for k in range(2):
        xp[at["h1"] + k] = jnp.where(upward, h1[2 + k], h1[k])
    xp[at["h2"]] = h2


def first_sides_kernel(own, xp, coarse):
    total = [own[0, k] + own[1, k] for k in range(OWN["h1"], OWN["counts"])]
    for k in range(COARSE["size"]):
        coarse[k] = total[k]
    h1, w1 = total[:4], total[4:8]
    h2, w2 = total[8:]
    pack_x(lambda x, z: own[z, x], h1, h2, xp, X_FIRST)
    upward = upward_x()
    edge = OWN["w"] + jnp.where(upward, 15, 0)
    for z in range(2):
        xp[X_FIRST["w"] + z] = own[z, edge]
    sub = sub_index()
    edge_one = jnp.where(upward, turn(w1[3], 4), w1[0])
    edge_two = jnp.where(upward, turn(w2, 6), turn(w2, 4))
    xp[X_FIRST["w12"]] = jnp.where(sub < 4, edge_one, edge_two)


def column_fine(own, planes, xr, at, lo, hi):
    def load(p, z):
        if p < planes:
            return xr[1 - odd_x(), 0, at + 2 * p + z] * lo
        if p < 16 + planes:
            return own(p - planes, z)
        return xr[odd_x(), 1, at + 2 * (p - 16 - planes) + z] * hi

    return load


def pack_fine(load, planes, mine, yp, at):
    for k in range(planes // 2):
        for z in range(2):
            yp[at + 2 * k + z] = jnp.where(mine, load(2 * k, z), turn(load(2 * k + 1, z), 4))


def pack_y(own, h1, h2, xr, yp, y2p, x_at, at):
    lo, hi = flags()[:2]
    mine = (sub_index() < 4) == (core() == 1)
    pack_fine(column_fine(own, 4, xr, x_at["h0"], lo, hi), 24, mine, yp, at["h0"])
    for k in range(2):
        yp[at["h1"] + k] = xr[1 - odd_x(), 0, x_at["h1"] + k] * lo
        yp[at["h1"] + 6 + k] = xr[odd_x(), 1, x_at["h1"] + k] * hi
    for k in range(4):
        yp[at["h1"] + 2 + k] = h1(k)
    two = [xr[1 - odd_x(), 0, x_at["h2"]] * lo, h2(), xr[odd_x(), 1, x_at["h2"]] * hi]
    for k in range(3):
        yp[at["h2"] + k] = two[k]
        y2p[k] = two[k]


def column_w1(p, coarse, xr):
    if p in (0, 9):
        return (xr[1 - odd_x(), 0, X_FIRST["w12"]] if p == 0 else xr[odd_x(), 1, X_FIRST["w12"]]), 0
    return coarse[COARSE["w1"] + (p - 1) // 2], 4 * ((p - 1) % 2)


def column_w2(p, coarse, xr):
    if p in (0, 5):
        return (xr[1 - odd_x(), 0, X_FIRST["w12"]] if p == 0 else xr[odd_x(), 1, X_FIRST["w12"]]), 4
    return coarse[COARSE["w2"]], 2 * (p - 1)


def first_rows_kernel(own, coarse, xr, yp, y2p):
    at = Y_FIRST
    pack_y(
        lambda x, z: own[z, x],
        lambda k: coarse[k],
        lambda: coarse[COARSE["h2"]],
        *(xr, yp, y2p, X_FIRST, at),
    )
    sub = sub_index()
    weights = column_fine(lambda x, z: own[z, OWN["w"] + x], 1, xr, X_FIRST["w"], 1.0, 1.0)
    upward = core() == 0
    for k in range(3):
        for z in range(2):
            packed = None
            for i in range(min(8, 18 - 8 * k)):
                tile = weights(8 * k + i, z)
                row = turn(jnp.where(upward, turn(tile, 1), tile), i)
                packed = row if i == 0 else jnp.where(sub < i, packed, row)
            yp[at["w"] + 2 * k + z] = packed
    for k in range(2):
        packed = None
        for i in range(8):
            p = 8 * k + i
            if p < 10:
                (tile, start), last = column_w1(p, coarse, xr), 3
            else:
                (tile, start), last = column_w2(p - 10, coarse, xr), 1
            row = turn(jnp.where(upward, turn(tile, -start - last), turn(tile, -start)), i)
            packed = row if i == 0 else jnp.where(sub < i, packed, row)
        yp[at["w12"] + k] = packed


def second_rows_kernel(h0, h12, xr, yp, y2p):
    pack_y(
        lambda x, z: h0[x, z],
        lambda k: h12[k],
        lambda: h12[4],
        *(xr, yp, y2p, X_SECOND, Y_SECOND),
    )


def join_fine(load, planes, yr, at, ylo, yhi, *outs):
    sub = sub_index()
    for k in range(planes // 2):
        for z in range(2):
            above, below = yr[0, at + 2 * k + z] * yhi, yr[1, at + 2 * k + z] * ylo
            halos = (
                jnp.where(sub < 4, above, below),
                turn(jnp.where(sub < 4, below, above), 4),
            )
            for i in range(2):
                own = load(2 * k + i, z)
                for out in outs:
                    out[2 * k + i, z] = own
                    out[2 * k + i, 2 + z] = halos[i]


def join_weights(load, yr, at, out):
    sub = sub_index()
    for p in range(18):
        for z in range(2):
            tile, i = at + 2 * (p // 8) + z, p % 8
            above, below = turn(yr[0, tile], -i), turn(yr[1, tile], 7 - i)
            out[p, z] = load(p, z)
            out[p, 2 + z] = jnp.where(sub < 7, above, below)


def four_rows(own, above, below, i):
    sub = sub_index()
    turned = 4 * (1 - i)
    first = jnp.where(sub < 4, turn(own, 4 * i), turn(above, turned))
    return first, keep(sub >= 4, turn(below, turned))


def join_h1(yp, yr, at, *outs):
    ylo, yhi = flags()[2:4]
    for k in range(8):
        tile = at + k
        own, above, below = yp[tile], yr[0, tile] * yhi, yr[1, tile] * ylo
        for i in range(2):
            both = four_rows(own, above, below, i)
            for out in outs:
                out[2 * k + i, 0], out[2 * k + i, 1] = both


def join_coarse_weights(coarse, xr, yr, iw1, iw2):
    sub = sub_index()
    for p in range(16):
        packed, i = Y_FIRST["w12"] + p // 8, p % 8
        above, below = yr[0, packed], yr[1, packed]
        if p < 10:
            (tile, start), rows, out, plane = column_w1(p, coarse, xr), 4, iw1, p
        else:
            (tile, start), rows, out, plane = column_w2(p - 10, coarse, xr), 2, iw2, p - 10
        own = turn(tile, -start)
        out[plane, 0] = inverse(jnp.where(sub < rows, own, keep(sub == rows, turn(above, rows - i))))
        out[plane, 1] = inverse(keep(sub == 7, turn(below, 7 - i)))


def join_h2(yp, yr, at, *outs):
    ylo, yhi, ylo2, yhi2 = flags()[2:]
    sub = sub_index()
    for k in range(3):
        tile, far = at["h2"] + k, at["far"] + k
        own, above, below = yp[tile], yr[0, tile] * yhi, yr[1, tile] * ylo
        above2, below2 = yr[1, far + 3] * yhi2, yr[0, far] * ylo2
        for i in range(4):
            first = jnp.where(sub < 2, turn(own, -2 * i), turn(above, 2 - 2 * i))
            upper = keep(sub < 6, turn(above2, 4 - 2 * i))
            lower = jnp.where(sub < 6, turn(below2, 4 - 2 * i), turn(below, 6 - 2 * i))
            for out in outs:
                out[4 * k + i, 0] = jnp.where(sub < 4, first, upper)
                out[4 * k + i, 1] = keep(sub >= 4, lower)


def along_y(first, second):
    sub = sub_index()
    up_first, up_second = turn(first, 7), turn(second, 7)
    down_first, down_second = turn(first, 1), turn(second, 1)
    sides_first = jnp.where(sub == 7, up_second, up_first) + jnp.where(sub == 0, down_second, down_first)
    sides_second = jnp.where(sub == 7, up_first, up_second) + jnp.where(sub == 0, down_first, down_second)
    return (first + first) + sides_first, (second + second) + sides_second


def along_z_fine(left, right):
    lane = lane_index()
    up_left, up_right = pltpu.roll(left, 127, 1), pltpu.roll(right, 127, 1)
    down_left, down_right = pltpu.roll(left, 1, 1), pltpu.roll(right, 1, 1)
    sides_left = jnp.where(lane < 127, up_left, up_right) + keep(lane > 0, down_left)
    sides_right = keep(lane < 127, up_right) + jnp.where(lane > 0, down_right, down_left)
    return (left + left) + sides_left, (right + right) + sides_right


def along_z_coarse(tile):
    lane = lane_index()
    sides = keep(lane < 127, pltpu.roll(tile, 127, 1)) + keep(lane > 0, pltpu.roll(tile, 1, 1))
    return (tile + tile) + sides


def along_yz(tiles):
    tiles = list(tiles)
    if len(tiles) == 4:
        for z in range(2):
            tiles[z], tiles[2 + z] = along_y(tiles[z], tiles[2 + z])
        for y in range(2):
            tiles[2 * y], tiles[2 * y + 1] = along_z_fine(tiles[2 * y], tiles[2 * y + 1])
        return tiles
    return [along_z_coarse(tile) for tile in along_y(*tiles)]


def added(first, second):
    return [a + b for a, b in zip(first, second)]


def relax_planes(q, h, start, planes, parts, before, masks, factors, active):
    def load(x):
        return [q[x, part] for part in range(parts)]

    kept = KEEP if active is None else 1.0 + active * (KEEP - 1.0)
    here = load(start)
    below = added(before, here)
    for i in range(planes):
        x = start + i
        after = load(x + 1)
        above = added(here, after)
        summed = along_yz(added(below, above))
        for part in range(parts):
            mask = masks[part // (parts // 2)]
            spread = (mask if factors[i] is None else mask * factors[i]) * summed[part]
            source = h[x, part] if active is None else active * h[x, part]
            q[x, part] = (kept * here[part] + spread) + source
        here, below = after, above


def relax_levels(counts, h0, q0, h1, q1, h2, q2):
    lo, hi, ylo, yhi, ylo2, yhi2 = flags()
    sub, lane = sub_index(), lane_index()
    spread = jnp.full(TILE, SPREAD, F32)
    above = jnp.where(sub < 2, 1.0, jnp.where(sub < 4, yhi, jnp.where(sub < 6, yhi2, 0.0)))
    below = jnp.where(sub < 4, 0.0, jnp.where(sub < 6, ylo2, ylo))
    masks2 = (keep(lane < 64, above * spread), keep(lane < 64, below * spread))
    masks1 = (jnp.where(sub < 4, 1.0, yhi) * spread, jnp.where(sub < 4, 0.0, ylo) * spread)
    masks0 = (spread, jnp.where(sub < 4, yhi, ylo) * spread)

    def coarse_sweep(k, _):
        for q, h, planes, masks, count in ((q2, h2, 12, masks2, counts[2]), (q1, h1, 16, masks1, counts[1])):
            active = jnp.where(count > k, 1.0, 0.0)
            factors = [active * lo] * 3 + [active] * (planes - 8) + [active * hi] * 3
            before = [q[0, part] for part in range(2)]
            relax_planes(q, h, 1, planes - 2, 2, before, masks, factors, active)
        return 0

    def fine_sweep(_, __):
        factors = [lo] * 3 + [None] * 16 + [hi] * 3
        before = [q0[0, part] for part in range(4)]
        relax_planes(q0, h0, 1, 22, 4, before, masks0, factors, None)
        return 0

    def both_sweeps(k, _):
        coarse_sweep(k, 0)
        return fine_sweep(k, 0)

    coarse_count = jnp.maximum(counts[1], counts[2])
    shared = jnp.minimum(counts[0], coarse_count)
    lax.fori_loop(1, shared, both_sweeps, 0)
    lax.fori_loop(shared, coarse_count, coarse_sweep, 0)
    lax.fori_loop(shared, counts[0], fine_sweep, 0)


def sweep_counts(own, cycle):
    held, sub, lane = own[0, OWN["counts"]], sub_index(), lane_index()
    return [
        jnp.max(keep((sub == cycle) & (lane == level), held)).astype(jnp.int32) for level in range(3)
    ]


def corrections(q1, iw1, q2, iw2, copies):
    sub = sub_index()
    one, two = (
        [
            jnp.where(sub < 7, q[p + 3, 0] * iw[p, 0], q[p + 3, 1] * iw[p, 1])
            for p in range(planes)
        ]
        for q, iw, planes in ((q1, iw1, 10), (q2, iw2, 6))
    )
    spread = []
    for tile in two:
        inner = jnp.where(sub < 3, turn(tile, 1), turn(tile, 2))
        spread.append(jnp.where((sub == 0) | (sub == 7), tile, inner))
    rows = [jnp.concatenate([one[p], spread[(p + 1) // 2]], axis=1) for p in range(10)]
    return exact_dot(jnp.concatenate(rows, axis=0), copies[...])


def iterate(coarse, q0, w, before, out):
    sub = sub_index()
    for k in range(10):
        for z in range(2):
            tile = coarse[8 * k : 8 * k + 8, 128 * z : 128 * z + 128]
            turned = [tile] + [turn(tile, by) for by in range(1, 5)]
            rows = turned[4]
            for by, last in ((3, 6), (2, 4), (1, 2), (0, 0)):
                rows = jnp.where(sub <= last, turned[by], rows)
            halo = jnp.where(sub < 7, turned[4], tile)
            for p in (2 * k - 1, 2 * k):
                if 0 <= p < 18:
                    for part, value in ((z, rows), (2 + z, halo)):
                        total = q0[p + 3, part] + w[p, part] * value
                        if before is not None:
                            total = before[p, part] + total
                        out[p, part] = total


def defects(pf):
    def load(p):
        return [pf[p, part] for part in range(4)]

    here = load(1)
    below = added(load(0), here)
    for x in range(16):
        after = load(x + 2)
        above = added(here, after)
        summed = along_yz(added(below, above))
        yield here[:2], [SELF_WEIGHT * here[z] - SIDE_CUBE * summed[z] for z in range(2)]
        here, below = after, above


def middle_kernel(
    own, coarse, xr, yp, yr, sums, copies,
    xp, pf, w, iw1, iw2, h0_next, h12_next,
    h0_all, q0, h1_all, q1, h2_all, q2,
):
    counts = sweep_counts(own, 0)
    lo, hi, ylo, yhi = flags()[:4]
    load = column_fine(lambda x, z: own[z, x], 4, xr, X_FIRST["h0"], lo, hi)
    join_fine(load, 24, yr, Y_FIRST["h0"], ylo, yhi, h0_all, q0)
    load = column_fine(lambda x, z: own[z, OWN["w"] + x], 1, xr, X_FIRST["w"], 1.0, 1.0)
    join_weights(load, yr, Y_FIRST["w"], w)
    join_h1(yp, yr, Y_FIRST["h1"], h1_all, q1)
    join_h2(yp, yr, Y_FIRST, h2_all, q2)
    join_coarse_weights(coarse, xr, yr, iw1, iw2)
    relax_levels(counts, h0_all, q0, h1_all, q1, h2_all, q2)
    iterate(corrections(q1, iw1, q2, iw2, copies), q0, w, None, pf)

    rests = [[], []]
    for x, (_, defect) in enumerate(defects(pf)):
        for z in range(2):
            h0 = own[z, x] - LEVEL[0] * defect[z]
            h0_next[x, z] = h0
            rests[z].append(own[z, OWN["w"] + x] * h0)
    summed = [plane_sums(rest) for rest in rests]
    rows = [jnp.concatenate([summed[0][k], summed[1][k]], axis=1) for k in range(5)]
    total = exact_dot(jnp.concatenate(rows, axis=0), sums[...])
    h1 = []
    for k in range(4):
        weight = coarse[COARSE["w1"] + k]
        h1.append(0.5 * LEVEL[1] / LEVEL[0] * total[8 * k : 8 * k + 8, :128] / weight)
        h12_next[k] = h1[k]
    weight = inverse(coarse[COARSE["w2"]])
    h2 = 0.25 * LEVEL[2] / LEVEL[0] * total[32:40, 128:] * weight
    h12_next[4] = h2
    pack_x(lambda x, z: h0_next[x, z], h1, h2, xp, X_SECOND)


def last_kernel(
    own, m, f, h0, xr, yp, yr, pf, w, iw1, iw2, copies,
    solution_out, residual_out,
    h0_all, q0, h1_all, q1, h2_all, q2, pf_all, solved, left, sent,
):
    counts = sweep_counts(own, 1)
    lo, hi, ylo, yhi = flags()[:4]
    load = column_fine(lambda x, z: h0[x, z], 4, xr, X_SECOND["h0"], lo, hi)
    join_fine(load, 24, yr, Y_SECOND["h0"], ylo, yhi, h0_all, q0)
    join_h1(yp, yr, Y_SECOND["h1"], h1_all, q1)
    join_h2(yp, yr, Y_SECOND, h2_all, q2)
    relax_levels(counts, h0_all, q0, h1_all, q1, h2_all, q2)
    iterate(corrections(q1, iw1, q2, iw2, copies), q0, w, pf, pf_all)
    first = core() == 0
    for x, (here, defect) in enumerate(defects(pf_all)):
        mine, rest = (jnp.where(first, both[0], both[1]) for both in (here, defect))
        weight = m[x]
        solved[x] = mine / weight
        left[x] = f[x] - weight * rest
    sends = [
        pltpu.make_async_copy(source, target, sent.at[k])
        for k, (source, target) in enumerate(((solved, solution_out), (left, residual_out)))
    ]
    for send in sends:
        send.start()
    for send in sends:
        send.wait()


def call(kernel, outs, scratch, name, *operands, outside=0, outs_outside=False):
    whole = pl.BlockSpec(memory_space=pltpu.HBM)
    vmem = pl.BlockSpec(memory_space=pltpu.VMEM)
    return pl.pallas_call(
        kernel,
        out_shape=[jax.ShapeDtypeStruct(shape, F32) for shape in outs],
        in_specs=[whole] * outside + [vmem] * (len(operands) - outside),
        out_specs=[whole if outs_outside else vmem] * len(outs),
        scratch_shapes=scratch,
        compiler_params=pltpu.CompilerParams(vmem_limit_bytes=32 * 2**20),
        name=name,
    )(*(pltpu.with_memory_space_constraint(x, pltpu.HBM) for x in operands[:outside]), *operands[outside:])


def space(*dims):
    return pltpu.VMEM(tiles(*dims), F32)


def tiles(*dims):
    return (*dims, *TILE)


def share(value):
    return lax.all_gather(value, "group", axis=0)


def trade_x(packed):
    names = ("group", "gx", "gy")
    sizes = [lax.axis_size(name) for name in names]
    index = np.arange(np.prod(sizes)).reshape(sizes)
    inner = [
        np.stack([index[k, k:-1:2], index[k, k + 1 :: 2]], axis=-1)
        for k in range(2)
    ]
    ends = [index[1, 0], index[1, -1]]
    groups = np.concatenate([pair.reshape(-1, 2) for pair in [*inner, *ends]]).tolist()
    return share(lax.all_gather(packed, names, axis=0, axis_index_groups=groups))


def trade_y(packed, packed_far):
    size = lax.axis_size("gy")
    moves = []
    for i in range(size - 1):
        moves += [(i, size + i + 1), (size + i + 1, i)]
    near = lax.ppermute(packed, ("group", "gy"), moves)
    groups = [[size + i, i + 2] for i in range(size - 2)]
    groups += [[0, 1], [2 * size - 2, 2 * size - 1]]
    far = lax.all_gather(packed_far, ("group", "gy"), axis=0, tiled=True, axis_index_groups=groups)
    return share(jnp.concatenate([near, far], axis=0))


def on_device(forcing, metric, sweeps):
    sums, copies = (jnp.asarray(matrix, jnp.bfloat16) for matrix in (WHOLE_SUMS, COPIES))
    spaces = [space(24, 4)] * 2 + [space(16, 2)] * 2 + [space(12, 2)] * 2

    (own,) = call(
        first_kernel,
        [tiles(OWN["size"])],
        [
            *(space(16), space(16), pltpu.VMEM(sweeps.shape, jnp.int32)),
            pltpu.SemaphoreType.DMA((3,)),
        ],
        "block_sums",
        *(metric, forcing, sweeps),
        outside=3,
    )
    own = share(own)
    xp, coarse = call(
        first_sides_kernel,
        [tiles(X_FIRST["size"]), tiles(COARSE["size"])],
        [],
        "first_sides",
        own,
    )
    xr = trade_x(xp)
    yp, y2p = call(
        first_rows_kernel,
        [tiles(Y_FIRST["size"]), tiles(3)],
        [],
        "first_rows",
        *(own, coarse, xr),
    )
    yr = trade_y(yp, y2p)
    xp, pf, w, iw1, iw2, h0, h12 = call(
        middle_kernel,
        [
            *(tiles(X_SECOND["size"]), tiles(18, 4), tiles(18, 4), tiles(10, 2), tiles(6, 2)),
            *(tiles(16, 2), tiles(5)),
        ],
        spaces,
        "first_cycle",
        *(own, coarse, xr, yp, yr, sums, copies),
    )
    xr = trade_x(xp)
    yp, y2p = call(
        second_rows_kernel,
        [tiles(Y_SECOND["size"]), tiles(3)],
        [],
        "second_rows",
        *(h0, h12, xr),
    )
    yr = trade_y(yp, y2p)
    return call(
        last_kernel,
        [tiles(16), tiles(16)],
        [*spaces, space(18, 4), space(16), space(16), pltpu.SemaphoreType.DMA((2,))],
        "second_cycle",
        *(own, metric, forcing, h0, xr, yp, yr, pf, w, iw1, iw2, copies),
        outs_outside=True,
    )


def solution(mesh):
    def program(forcing, metric, sweeps):
        return tuple(on_device(forcing, metric, sweeps))

    return jax.shard_map(
        program,
        mesh=mesh,
        in_specs=(P("gx", "gy", "group"), P("gx", "gy", "group"), P()),
        out_specs=(P("gx", "gy", "group"), P("gx", "gy", "group")),
        check_vma=False,
    )
```

```python
import jax
import jax.numpy as jnp
import numpy as np
from jax import lax
from jax.experimental import pallas as pl
from jax.experimental.pallas import tpu as pltpu
from jax.sharding import PartitionSpec as P

RELAXATION = 0.8
SIDE_WEIGHT = 0.05 ** (1.0 / 3.0)
SELF_WEIGHT = 3.4
SIDE_CUBE = SIDE_WEIGHT**3

KEEP = 1.0 - RELAXATION * SELF_WEIGHT / 3.0
SPREAD = RELAXATION * SIDE_CUBE / 3.0
LEVEL = [RELAXATION / (3.0 * 4.0**-level) for level in range(3)]

F32 = jnp.float32
TILE = (8, 128)

OWN = dict(h0=0, w=16, h1=32, w1=36, h2=40, w2=41, counts=42, size=43)
COARSE = dict(h1=0, w1=4, h2=8, w2=9, size=10)
X_FIRST = dict(h0=0, h1=8, h2=10, w=11, w12=13, size=14)
X_SECOND = dict(h0=0, h1=8, h2=10, size=11)
Y_FIRST = dict(h0=0, h1=24, h2=32, w=35, w12=41, size=43, far=43)
Y_SECOND = dict(h0=0, h1=24, h2=32, size=35, far=35)

LANES = np.arange(256)
WHOLE_SUMS = np.concatenate(
    [LANES[:, None] // 2 == LANES[None, :128], LANES[:, None] // 4 == LANES[None, :128]], axis=1
).astype(np.float32)
COPIES = WHOLE_SUMS.T * np.where(LANES[:, None] < 128, 0.5, 0.25).astype(np.float32)


def exact_dot(rows, matrix):
    parts = []
    rest = rows
    for _ in range(3):
        parts.append(rest.astype(jnp.bfloat16))
        rest = rest - parts[-1].astype(F32)
    out = lax.dot_general(
        jnp.concatenate(parts, axis=0),
        matrix,
        (((1,), (0,)), ((), ())),
        preferred_element_type=F32,
    )
    count = rows.shape[0]
    return out[:count] + (out[count : 2 * count] + out[2 * count :])


def sub_index():
    return lax.broadcasted_iota(jnp.int32, TILE, 0)


def lane_index():
    return lax.broadcasted_iota(jnp.int32, TILE, 1)


def turn(tile, by):
    by %= 8
    return pltpu.roll(tile, by, 0) if by else tile


def keep(where, tile):
    return jnp.where(where, tile, 0.0)


def inverse(tile):
    return jnp.where(tile > 0, 1.0 / jnp.where(tile > 0, tile, 1.0), 0.0)


def core():
    return lax.axis_index("group")


def odd_x():
    return lax.rem(lax.axis_index("gx"), 2)


def upward_x():
    return core() == odd_x()


def flags():
    gx, gy = lax.axis_index("gx"), lax.axis_index("gy")
    x_last, y_last = lax.axis_size("gx") - 1, lax.axis_size("gy") - 1
    places = [gx > 0, gx < x_last, gy > 0, gy < y_last, gy > 1, gy < y_last - 1]
    return [place.astype(F32) for place in places]


def pair_rows(first, second):
    sub = sub_index()
    first, second = (tile + turn(tile, 7) for tile in (first, second))
    low = jnp.where(sub == 0, first, turn(first, 7))
    low = jnp.where(sub < 2, low, jnp.where(sub == 2, turn(first, 6), turn(first, 5)))
    high = jnp.where(sub == 4, turn(second, 4), turn(second, 3))
    high = jnp.where(sub < 6, high, jnp.where(sub == 6, turn(second, 2), turn(second, 1)))
    return jnp.where(sub < 4, low, high)


def plane_sums(fine):
    sub = sub_index()
    sums = [fine[2 * k] + fine[2 * k + 1] for k in range(8)]
    one = [pair_rows(sums[2 * k], sums[2 * k + 1]) for k in range(4)]
    two = None
    for k in range(4):
        both = one[k] + turn(one[k], 4)
        both = both + turn(both, 7)
        placed = jnp.where(sub == 2 * k, turn(both, 2 * k), turn(both, 2 * k - 1))
        two = placed if k == 0 else jnp.where(sub < 2 * k, two, placed)
    return one + [two]


def half_sums():
    row = lax.broadcasted_iota(jnp.int32, (128, 128), 0)
    column = lax.broadcasted_iota(jnp.int32, (128, 128), 1)
    matrix = jnp.concatenate([row >> 1 == column, row >> 2 == column], axis=1)
    return jnp.where(matrix, 1.0, 0.0).astype(jnp.bfloat16)


def first_kernel(m_whole, f_whole, sweeps_whole, out, m, f, sweeps, arrived):
    moves = ((m_whole, m), (f_whole, f), (sweeps_whole, sweeps))
    copies = [
        pltpu.make_async_copy(source, target, arrived.at[k])
        for k, (source, target) in enumerate(moves)
    ]
    for copy in copies:
        copy.start()
    sums = half_sums()
    copies[0].wait()
    m_tiles = [m[x] for x in range(16)]
    m_sums = plane_sums(m_tiles)
    for x in range(16):
        out[OWN["w"] + x] = m_tiles[x]
    for copy in copies[1:]:
        copy.wait()
    f_tiles = [f[x] for x in range(16)]
    for x in range(16):
        out[OWN["h0"] + x] = LEVEL[0] * f_tiles[x] / m_tiles[x]
    rows = jnp.concatenate(m_sums + plane_sums(f_tiles), axis=0)
    total = exact_dot(rows, sums)
    out[OWN["counts"]] = jnp.zeros(TILE, F32)
    out[OWN["counts"], : sweeps.shape[0], : sweeps.shape[1]] = sweeps[...].astype(F32)
    upper = core() == 1
    for k in range(5):
        left, width = (0, 64) if k < 4 else (128, 32)
        weight, force = (
            total[row : row + 8, left : left + 128] for row in (8 * k, 40 + 8 * k)
        )
        weight = (0.125 if k < 4 else 0.125 * 0.125) * weight
        force = (0.5 * LEVEL[1] if k < 4 else 0.25 * LEVEL[2]) * force * inverse(weight)
        weight, force = (
            jnp.where(upper, pltpu.roll(tile, width, 1), tile) for tile in (weight, force)
        )
        out[(OWN["w1"] + k) if k < 4 else OWN["w2"]] = weight
        out[(OWN["h1"] + k) if k < 4 else OWN["h2"]] = force


def pack_x(fine, h1, h2, xp, at):
    upward = upward_x()
    start = jnp.where(upward, 12, 0)
    for k in range(4):
        for z in range(2):
            xp[at["h0"] + 2 * k + z] = fine(start + k, z)
    for k in range(2):
        xp[at["h1"] + k] = jnp.where(upward, h1[2 + k], h1[k])
    xp[at["h2"]] = h2


def first_sides_kernel(own, xp, coarse):
    total = [own[0, k] + own[1, k] for k in range(OWN["h1"], OWN["counts"])]
    for k in range(COARSE["size"]):
        coarse[k] = total[k]
    h1, w1 = total[:4], total[4:8]
    h2, w2 = total[8:]
    pack_x(lambda x, z: own[z, x], h1, h2, xp, X_FIRST)
    upward = upward_x()
    edge = OWN["w"] + jnp.where(upward, 15, 0)
    for z in range(2):
        xp[X_FIRST["w"] + z] = own[z, edge]
    sub = sub_index()
    edge_one = jnp.where(upward, turn(w1[3], 4), w1[0])
    edge_two = jnp.where(upward, turn(w2, 6), turn(w2, 4))
    xp[X_FIRST["w12"]] = jnp.where(sub < 4, edge_one, edge_two)


def column_fine(own, planes, xr, at, lo, hi):
    def load(p, z):
        if p < planes:
            return xr[1 - odd_x(), 0, at + 2 * p + z] * lo
        if p < 16 + planes:
            return own(p - planes, z)
        return xr[odd_x(), 1, at + 2 * (p - 16 - planes) + z] * hi

    return load


def pack_fine(load, planes, mine, yp, at):
    for k in range(planes // 2):
        for z in range(2):
            yp[at + 2 * k + z] = jnp.where(mine, load(2 * k, z), turn(load(2 * k + 1, z), 4))


def pack_y(own, h1, h2, xr, yp, y2p, x_at, at):
    lo, hi = flags()[:2]
    mine = (sub_index() < 4) == (core() == 0)
    pack_fine(column_fine(own, 4, xr, x_at["h0"], lo, hi), 24, mine, yp, at["h0"])
    for k in range(2):
        yp[at["h1"] + k] = xr[1 - odd_x(), 0, x_at["h1"] + k] * lo
        yp[at["h1"] + 6 + k] = xr[odd_x(), 1, x_at["h1"] + k] * hi
    for k in range(4):
        yp[at["h1"] + 2 + k] = h1(k)
    two = [xr[1 - odd_x(), 0, x_at["h2"]] * lo, h2(), xr[odd_x(), 1, x_at["h2"]] * hi]
    for k in range(3):
        yp[at["h2"] + k] = two[k]
        y2p[k] = two[k]


def column_w1(p, coarse, xr):
    if p in (0, 9):
        return (xr[1 - odd_x(), 0, X_FIRST["w12"]] if p == 0 else xr[odd_x(), 1, X_FIRST["w12"]]), 0
    return coarse[COARSE["w1"] + (p - 1) // 2], 4 * ((p - 1) % 2)


def column_w2(p, coarse, xr):
    if p in (0, 5):
        return (xr[1 - odd_x(), 0, X_FIRST["w12"]] if p == 0 else xr[odd_x(), 1, X_FIRST["w12"]]), 4
    return coarse[COARSE["w2"]], 2 * (p - 1)


def first_rows_kernel(own, coarse, xr, yp, y2p):
    at = Y_FIRST
    pack_y(
        lambda x, z: own[z, x],
        lambda k: coarse[k],
        lambda: coarse[COARSE["h2"]],
        *(xr, yp, y2p, X_FIRST, at),
    )
    sub = sub_index()
    weights = column_fine(lambda x, z: own[z, OWN["w"] + x], 1, xr, X_FIRST["w"], 1.0, 1.0)
    upward = core() == 1
    for k in range(3):
        for z in range(2):
            packed = None
            for i in range(min(8, 18 - 8 * k)):
                tile = weights(8 * k + i, z)
                row = turn(jnp.where(upward, turn(tile, 1), tile), i)
                packed = row if i == 0 else jnp.where(sub < i, packed, row)
            yp[at["w"] + 2 * k + z] = packed
    for k in range(2):
        packed = None
        for i in range(8):
            p = 8 * k + i
            if p < 10:
                (tile, start), last = column_w1(p, coarse, xr), 3
            else:
                (tile, start), last = column_w2(p - 10, coarse, xr), 1
            row = turn(jnp.where(upward, turn(tile, -start - last), turn(tile, -start)), i)
            packed = row if i == 0 else jnp.where(sub < i, packed, row)
        yp[at["w12"] + k] = packed


def second_rows_kernel(h0, h12, xr, yp, y2p):
    pack_y(
        lambda x, z: h0[x, z],
        lambda k: h12[k],
        lambda: h12[4],
        *(xr, yp, y2p, X_SECOND, Y_SECOND),
    )


def join_fine(load, planes, yr, at, ylo, yhi, *outs):
    sub = sub_index()
    for k in range(planes // 2):
        for z in range(2):
            above, below = yr[1, at + 2 * k + z] * yhi, yr[0, at + 2 * k + z] * ylo
            halos = (
                jnp.where(sub < 4, above, below),
                turn(jnp.where(sub < 4, below, above), 4),
            )
            for i in range(2):
                own = load(2 * k + i, z)
                for out in outs:
                    out[2 * k + i, z] = own
                    out[2 * k + i, 2 + z] = halos[i]


def join_weights(load, yr, at, out):
    sub = sub_index()
    for p in range(18):
        for z in range(2):
            tile, i = at + 2 * (p // 8) + z, p % 8
            above, below = turn(yr[1, tile], -i), turn(yr[0, tile], 7 - i)
            out[p, z] = load(p, z)
            out[p, 2 + z] = jnp.where(sub < 7, above, below)


def four_rows(own, above, below, i):
    sub = sub_index()
    turned = 4 * (1 - i)
    first = jnp.where(sub < 4, turn(own, 4 * i), turn(above, turned))
    return first, keep(sub >= 4, turn(below, turned))


def join_h1(yp, yr, at, *outs):
    ylo, yhi = flags()[2:4]
    for k in range(8):
        tile = at + k
        own, above, below = yp[tile], yr[1, tile] * yhi, yr[0, tile] * ylo
        for i in range(2):
            both = four_rows(own, above, below, i)
            for out in outs:
                out[2 * k + i, 0], out[2 * k + i, 1] = both


def join_coarse_weights(coarse, xr, yr, iw1, iw2):
    sub = sub_index()
    for p in range(16):
        packed, i = Y_FIRST["w12"] + p // 8, p % 8
        above, below = yr[1, packed], yr[0, packed]
        if p < 10:
            (tile, start), rows, out, plane = column_w1(p, coarse, xr), 4, iw1, p
        else:
            (tile, start), rows, out, plane = column_w2(p - 10, coarse, xr), 2, iw2, p - 10
        own = turn(tile, -start)
        out[plane, 0] = inverse(jnp.where(sub < rows, own, keep(sub == rows, turn(above, rows - i))))
        out[plane, 1] = inverse(keep(sub == 7, turn(below, 7 - i)))


def join_h2(yp, yr, at, *outs):
    ylo, yhi, ylo2, yhi2 = flags()[2:]
    sub = sub_index()
    for k in range(3):
        tile, far = at["h2"] + k, at["far"] + k
        own, above, below = yp[tile], yr[1, tile] * yhi, yr[0, tile] * ylo
        above2, below2 = yr[0, far + 3] * yhi2, yr[1, far] * ylo2
        for i in range(4):
            first = jnp.where(sub < 2, turn(own, -2 * i), turn(above, 2 - 2 * i))
            upper = keep(sub < 6, turn(above2, 4 - 2 * i))
            lower = jnp.where(sub < 6, turn(below2, 4 - 2 * i), turn(below, 6 - 2 * i))
            for out in outs:
                out[4 * k + i, 0] = jnp.where(sub < 4, first, upper)
                out[4 * k + i, 1] = keep(sub >= 4, lower)


def along_y(first, second):
    sub = sub_index()
    up_first, up_second = turn(first, 7), turn(second, 7)
    down_first, down_second = turn(first, 1), turn(second, 1)
    sides_first = jnp.where(sub == 7, up_second, up_first) + jnp.where(sub == 0, down_second, down_first)
    sides_second = jnp.where(sub == 7, up_first, up_second) + jnp.where(sub == 0, down_first, down_second)
    return (first + first) + sides_first, (second + second) + sides_second


def along_z_fine(left, right):
    lane = lane_index()
    up_left, up_right = pltpu.roll(left, 127, 1), pltpu.roll(right, 127, 1)
    down_left, down_right = pltpu.roll(left, 1, 1), pltpu.roll(right, 1, 1)
    sides_left = jnp.where(lane < 127, up_left, up_right) + keep(lane > 0, down_left)
    sides_right = keep(lane < 127, up_right) + jnp.where(lane > 0, down_right, down_left)
    return (left + left) + sides_left, (right + right) + sides_right


def along_z_coarse(tile):
    lane = lane_index()
    sides = keep(lane < 127, pltpu.roll(tile, 127, 1)) + keep(lane > 0, pltpu.roll(tile, 1, 1))
    return (tile + tile) + sides


def along_yz(tiles):
    tiles = list(tiles)
    if len(tiles) == 4:
        for z in range(2):
            tiles[z], tiles[2 + z] = along_y(tiles[z], tiles[2 + z])
        for y in range(2):
            tiles[2 * y], tiles[2 * y + 1] = along_z_fine(tiles[2 * y], tiles[2 * y + 1])
        return tiles
    return [along_z_coarse(tile) for tile in along_y(*tiles)]


def added(first, second):
    return [a + b for a, b in zip(first, second)]


def relax_planes(q, h, start, planes, parts, before, masks, factors, active):
    def load(x):
        return [q[x, part] for part in range(parts)]

    kept = KEEP if active is None else 1.0 + active * (KEEP - 1.0)
    here = load(start)
    below = added(before, here)
    for i in range(planes):
        x = start + i
        after = load(x + 1)
        above = added(here, after)
        summed = along_yz(added(below, above))
        for part in range(parts):
            mask = masks[part // (parts // 2)]
            spread = (mask if factors[i] is None else mask * factors[i]) * summed[part]
            source = h[x, part] if active is None else active * h[x, part]
            q[x, part] = (kept * here[part] + spread) + source
        here, below = after, above


def relax_levels(counts, h0, q0, h1, q1, h2, q2):
    lo, hi, ylo, yhi, ylo2, yhi2 = flags()
    sub, lane = sub_index(), lane_index()
    spread = jnp.full(TILE, SPREAD, F32)
    above = jnp.where(sub < 2, 1.0, jnp.where(sub < 4, yhi, jnp.where(sub < 6, yhi2, 0.0)))
    below = jnp.where(sub < 4, 0.0, jnp.where(sub < 6, ylo2, ylo))
    masks2 = (keep(lane < 64, above * spread), keep(lane < 64, below * spread))
    masks1 = (jnp.where(sub < 4, 1.0, yhi) * spread, jnp.where(sub < 4, 0.0, ylo) * spread)
    masks0 = (spread, jnp.where(sub < 4, yhi, ylo) * spread)

    def coarse_sweep(k, _):
        for q, h, planes, masks, count in ((q2, h2, 12, masks2, counts[2]), (q1, h1, 16, masks1, counts[1])):
            active = jnp.where(count > k, 1.0, 0.0)
            factors = [active * lo] * 3 + [active] * (planes - 8) + [active * hi] * 3
            before = [q[0, part] for part in range(2)]
            relax_planes(q, h, 1, planes - 2, 2, before, masks, factors, active)
        return 0

    def fine_sweep(_, __):
        factors = [lo] * 3 + [None] * 16 + [hi] * 3
        before = [q0[0, part] for part in range(4)]
        relax_planes(q0, h0, 1, 22, 4, before, masks0, factors, None)
        return 0

    def both_sweeps(k, _):
        coarse_sweep(k, 0)
        return fine_sweep(k, 0)

    coarse_count = jnp.maximum(counts[1], counts[2])
    shared = jnp.minimum(counts[0], coarse_count)
    lax.fori_loop(1, shared, both_sweeps, 0)
    lax.fori_loop(shared, coarse_count, coarse_sweep, 0)
    lax.fori_loop(shared, counts[0], fine_sweep, 0)


def sweep_counts(own, cycle):
    held, sub, lane = own[0, OWN["counts"]], sub_index(), lane_index()
    return [
        jnp.max(keep((sub == cycle) & (lane == level), held)).astype(jnp.int32) for level in range(3)
    ]


def corrections(q1, iw1, q2, iw2, copies):
    sub = sub_index()
    one, two = (
        [
            jnp.where(sub < 7, q[p + 3, 0] * iw[p, 0], q[p + 3, 1] * iw[p, 1])
            for p in range(planes)
        ]
        for q, iw, planes in ((q1, iw1, 10), (q2, iw2, 6))
    )
    spread = []
    for tile in two:
        inner = jnp.where(sub < 3, turn(tile, 1), turn(tile, 2))
        spread.append(jnp.where((sub == 0) | (sub == 7), tile, inner))
    rows = [jnp.concatenate([one[p], spread[(p + 1) // 2]], axis=1) for p in range(10)]
    return exact_dot(jnp.concatenate(rows, axis=0), copies[...])


def iterate(coarse, q0, w, before, out):
    sub = sub_index()
    for k in range(10):
        for z in range(2):
            tile = coarse[8 * k : 8 * k + 8, 128 * z : 128 * z + 128]
            turned = [tile] + [turn(tile, by) for by in range(1, 5)]
            rows = turned[4]
            for by, last in ((3, 6), (2, 4), (1, 2), (0, 0)):
                rows = jnp.where(sub <= last, turned[by], rows)
            halo = jnp.where(sub < 7, turned[4], tile)
            for p in (2 * k - 1, 2 * k):
                if 0 <= p < 18:
                    for part, value in ((z, rows), (2 + z, halo)):
                        total = q0[p + 3, part] + w[p, part] * value
                        if before is not None:
                            total = before[p, part] + total
                        out[p, part] = total


def defects(pf):
    def load(p):
        return [pf[p, part] for part in range(4)]

    here = load(1)
    below = added(load(0), here)
    for x in range(16):
        after = load(x + 2)
        above = added(here, after)
        summed = along_yz(added(below, above))
        yield here[:2], [SELF_WEIGHT * here[z] - SIDE_CUBE * summed[z] for z in range(2)]
        here, below = after, above


def middle_kernel(
    own, coarse, xr, yp, yr, sums, copies,
    xp, pf, w, iw1, iw2, h0_next, h12_next,
    h0_all, q0, h1_all, q1, h2_all, q2,
):
    counts = sweep_counts(own, 0)
    lo, hi, ylo, yhi = flags()[:4]
    load = column_fine(lambda x, z: own[z, x], 4, xr, X_FIRST["h0"], lo, hi)
    join_fine(load, 24, yr, Y_FIRST["h0"], ylo, yhi, h0_all, q0)
    load = column_fine(lambda x, z: own[z, OWN["w"] + x], 1, xr, X_FIRST["w"], 1.0, 1.0)
    join_weights(load, yr, Y_FIRST["w"], w)
    join_h1(yp, yr, Y_FIRST["h1"], h1_all, q1)
    join_h2(yp, yr, Y_FIRST, h2_all, q2)
    join_coarse_weights(coarse, xr, yr, iw1, iw2)
    relax_levels(counts, h0_all, q0, h1_all, q1, h2_all, q2)
    iterate(corrections(q1, iw1, q2, iw2, copies), q0, w, None, pf)

    rests = [[], []]
    for x, (_, defect) in enumerate(defects(pf)):
        for z in range(2):
            h0 = own[z, x] - LEVEL[0] * defect[z]
            h0_next[x, z] = h0
            rests[z].append(own[z, OWN["w"] + x] * h0)
    summed = [plane_sums(rest) for rest in rests]
    rows = [jnp.concatenate([summed[0][k], summed[1][k]], axis=1) for k in range(5)]
    total = exact_dot(jnp.concatenate(rows, axis=0), sums[...])
    h1 = []
    for k in range(4):
        weight = coarse[COARSE["w1"] + k]
        h1.append(0.5 * LEVEL[1] / LEVEL[0] * total[8 * k : 8 * k + 8, :128] / weight)
        h12_next[k] = h1[k]
    weight = inverse(coarse[COARSE["w2"]])
    h2 = 0.25 * LEVEL[2] / LEVEL[0] * total[32:40, 128:] * weight
    h12_next[4] = h2
    pack_x(lambda x, z: h0_next[x, z], h1, h2, xp, X_SECOND)


def last_kernel(
    own, m, f, h0, xr, yp, yr, pf, w, iw1, iw2, copies,
    solution_out, residual_out,
    h0_all, q0, h1_all, q1, h2_all, q2, pf_all, solved, left, sent,
):
    counts = sweep_counts(own, 1)
    lo, hi, ylo, yhi = flags()[:4]
    load = column_fine(lambda x, z: h0[x, z], 4, xr, X_SECOND["h0"], lo, hi)
    join_fine(load, 24, yr, Y_SECOND["h0"], ylo, yhi, h0_all, q0)
    join_h1(yp, yr, Y_SECOND["h1"], h1_all, q1)
    join_h2(yp, yr, Y_SECOND, h2_all, q2)
    relax_levels(counts, h0_all, q0, h1_all, q1, h2_all, q2)
    iterate(corrections(q1, iw1, q2, iw2, copies), q0, w, pf, pf_all)
    first = core() == 0
    for x, (here, defect) in enumerate(defects(pf_all)):
        mine, rest = (jnp.where(first, both[0], both[1]) for both in (here, defect))
        weight = m[x]
        solved[x] = mine / weight
        left[x] = f[x] - weight * rest
    sends = [
        pltpu.make_async_copy(source, target, sent.at[k])
        for k, (source, target) in enumerate(((solved, solution_out), (left, residual_out)))
    ]
    for send in sends:
        send.start()
    for send in sends:
        send.wait()


def call(kernel, outs, scratch, name, *operands, outside=0, outs_outside=False):
    whole = pl.BlockSpec(memory_space=pltpu.HBM)
    vmem = pl.BlockSpec(memory_space=pltpu.VMEM)
    return pl.pallas_call(
        kernel,
        out_shape=[jax.ShapeDtypeStruct(shape, F32) for shape in outs],
        in_specs=[whole] * outside + [vmem] * (len(operands) - outside),
        out_specs=[whole if outs_outside else vmem] * len(outs),
        scratch_shapes=scratch,
        compiler_params=pltpu.CompilerParams(vmem_limit_bytes=32 * 2**20),
        name=name,
    )(*(pltpu.with_memory_space_constraint(x, pltpu.HBM) for x in operands[:outside]), *operands[outside:])


def space(*dims):
    return pltpu.VMEM(tiles(*dims), F32)


def tiles(*dims):
    return (*dims, *TILE)


def share(value):
    return lax.all_gather(value, "group", axis=0)


def trade_x(packed):
    names = ("group", "gx", "gy")
    sizes = [lax.axis_size(name) for name in names]
    index = np.arange(np.prod(sizes)).reshape(sizes)
    inner = [
        np.stack([index[k, k:-1:2], index[k, k + 1 :: 2]], axis=-1)
        for k in range(2)
    ]
    ends = [index[1, 0], index[1, -1]]
    groups = np.concatenate([pair.reshape(-1, 2) for pair in [*inner, *ends]]).tolist()
    return share(lax.all_gather(packed, names, axis=0, axis_index_groups=groups))


def trade_y(packed, packed_far):
    size = lax.axis_size("gy")
    moves = []
    for i in range(size - 1):
        moves += [(size + i, i + 1), (i + 1, size + i)]
    near = lax.ppermute(packed, ("group", "gy"), moves)
    groups = [[i, size + i + 2] for i in range(size - 2)]
    groups += [[size - 2, size - 1], [size, size + 1]]
    far = lax.all_gather(packed_far, ("group", "gy"), axis=0, tiled=True, axis_index_groups=groups)
    return share(jnp.concatenate([near, far], axis=0))


def on_device(forcing, metric, sweeps):
    sums, copies = (jnp.asarray(matrix, jnp.bfloat16) for matrix in (WHOLE_SUMS, COPIES))
    spaces = [space(24, 4)] * 2 + [space(16, 2)] * 2 + [space(12, 2)] * 2

    (own,) = call(
        first_kernel,
        [tiles(OWN["size"])],
        [
            *(space(16), space(16), pltpu.VMEM(sweeps.shape, jnp.int32)),
            pltpu.SemaphoreType.DMA((3,)),
        ],
        "block_sums",
        *(metric, forcing, sweeps),
        outside=3,
    )
    own = share(own)
    xp, coarse = call(
        first_sides_kernel,
        [tiles(X_FIRST["size"]), tiles(COARSE["size"])],
        [],
        "first_sides",
        own,
    )
    xr = trade_x(xp)
    yp, y2p = call(
        first_rows_kernel,
        [tiles(Y_FIRST["size"]), tiles(3)],
        [],
        "first_rows",
        *(own, coarse, xr),
    )
    yr = trade_y(yp, y2p)
    xp, pf, w, iw1, iw2, h0, h12 = call(
        middle_kernel,
        [
            *(tiles(X_SECOND["size"]), tiles(18, 4), tiles(18, 4), tiles(10, 2), tiles(6, 2)),
            *(tiles(16, 2), tiles(5)),
        ],
        spaces,
        "first_cycle",
        *(own, coarse, xr, yp, yr, sums, copies),
    )
    xr = trade_x(xp)
    yp, y2p = call(
        second_rows_kernel,
        [tiles(Y_SECOND["size"]), tiles(3)],
        [],
        "second_rows",
        *(h0, h12, xr),
    )
    yr = trade_y(yp, y2p)
    return call(
        last_kernel,
        [tiles(16), tiles(16)],
        [*spaces, space(18, 4), space(16), space(16), pltpu.SemaphoreType.DMA((2,))],
        "second_cycle",
        *(own, metric, forcing, h0, xr, yp, yr, pf, w, iw1, iw2, copies),
        outs_outside=True,
    )


def solution(mesh):
    def program(forcing, metric, sweeps):
        return tuple(on_device(forcing, metric, sweeps))

    return jax.shard_map(
        program,
        mesh=mesh,
        in_specs=(P("gx", "gy", "group"), P("gx", "gy", "group"), P()),
        out_specs=(P("gx", "gy", "group"), P("gx", "gy", "group")),
        check_vma=False,
    )
```

```python
import jax
import jax.numpy as jnp
import numpy as np
from jax import lax
from jax.experimental import pallas as pl
from jax.experimental.pallas import tpu as pltpu
from jax.sharding import PartitionSpec as P

RELAXATION = 0.8
SIDE_WEIGHT = 0.05 ** (1.0 / 3.0)
SELF_WEIGHT = 3.4
SIDE_CUBE = SIDE_WEIGHT**3

KEEP = 1.0 - RELAXATION * SELF_WEIGHT / 3.0
SPREAD = RELAXATION * SIDE_CUBE / 3.0
LEVEL = [RELAXATION / (3.0 * 4.0**-level) for level in range(3)]

F32 = jnp.float32
TILE = (8, 128)

OWN = dict(h0=0, w=16, h1=32, w1=36, h2=40, w2=41, counts=42, size=43)
COARSE = dict(h1=0, w1=4, h2=8, w2=9, size=10)
X_FIRST = dict(h0=0, h1=8, h2=10, w=11, w12=13, size=14)
X_SECOND = dict(h0=0, h1=8, h2=10, size=11)
Y_FIRST = dict(h0=0, h1=24, h2=32, w=35, w12=41, size=43, far=43)
Y_SECOND = dict(h0=0, h1=24, h2=32, size=35, far=35)

LANES = np.arange(256)
WHOLE_SUMS = np.concatenate(
    [LANES[:, None] // 2 == LANES[None, :128], LANES[:, None] // 4 == LANES[None, :128]], axis=1
).astype(np.float32)
COPIES = WHOLE_SUMS.T * np.where(LANES[:, None] < 128, 0.5, 0.25).astype(np.float32)


def exact_dot(rows, matrix):
    parts = []
    rest = rows
    for _ in range(3):
        parts.append(rest.astype(jnp.bfloat16))
        rest = rest - parts[-1].astype(F32)
    out = lax.dot_general(
        jnp.concatenate(parts, axis=0),
        matrix,
        (((1,), (0,)), ((), ())),
        preferred_element_type=F32,
    )
    count = rows.shape[0]
    return out[:count] + (out[count : 2 * count] + out[2 * count :])


def sub_index():
    return lax.broadcasted_iota(jnp.int32, TILE, 0)


def lane_index():
    return lax.broadcasted_iota(jnp.int32, TILE, 1)


def turn(tile, by):
    by %= 8
    return pltpu.roll(tile, by, 0) if by else tile


def keep(where, tile):
    return jnp.where(where, tile, 0.0)


def inverse(tile):
    return jnp.where(tile > 0, 1.0 / jnp.where(tile > 0, tile, 1.0), 0.0)


def core():
    return lax.axis_index("group")


def odd_x():
    return lax.rem(lax.axis_index("gx"), 2)


def upward_x():
    return core() == odd_x()


def flags():
    gx, gy = lax.axis_index("gx"), lax.axis_index("gy")
    x_last, y_last = lax.axis_size("gx") - 1, lax.axis_size("gy") - 1
    places = [gx > 0, gx < x_last, gy > 0, gy < y_last, gy > 1, gy < y_last - 1]
    return [place.astype(F32) for place in places]


def pair_rows(first, second):
    sub = sub_index()
    first, second = (tile + turn(tile, 7) for tile in (first, second))
    low = jnp.where(sub == 0, first, turn(first, 7))
    low = jnp.where(sub < 2, low, jnp.where(sub == 2, turn(first, 6), turn(first, 5)))
    high = jnp.where(sub == 4, turn(second, 4), turn(second, 3))
    high = jnp.where(sub < 6, high, jnp.where(sub == 6, turn(second, 2), turn(second, 1)))
    return jnp.where(sub < 4, low, high)


def plane_sums(fine):
    sub = sub_index()
    sums = [fine[2 * k] + fine[2 * k + 1] for k in range(8)]
    one = [pair_rows(sums[2 * k], sums[2 * k + 1]) for k in range(4)]
    two = None
    for k in range(4):
        both = one[k] + turn(one[k], 4)
        both = both + turn(both, 7)
        placed = jnp.where(sub == 2 * k, turn(both, 2 * k), turn(both, 2 * k - 1))
        two = placed if k == 0 else jnp.where(sub < 2 * k, two, placed)
    return one + [two]


def half_sums():
    row = lax.broadcasted_iota(jnp.int32, (128, 128), 0)
    column = lax.broadcasted_iota(jnp.int32, (128, 128), 1)
    matrix = jnp.concatenate([row >> 1 == column, row >> 2 == column], axis=1)
    return jnp.where(matrix, 1.0, 0.0).astype(jnp.bfloat16)


def first_kernel(m_whole, f_whole, sweeps_whole, out, m, f, sweeps, arrived):
    moves = ((m_whole, m), (f_whole, f), (sweeps_whole, sweeps))
    copies = [
        pltpu.make_async_copy(source, target, arrived.at[k])
        for k, (source, target) in enumerate(moves)
    ]
    for copy in copies:
        copy.start()
    sums = half_sums()
    copies[0].wait()
    m_tiles = [m[x] for x in range(16)]
    m_sums = plane_sums(m_tiles)
    for x in range(16):
        out[OWN["w"] + x] = m_tiles[x]
    for copy in copies[1:]:
        copy.wait()
    f_tiles = [f[x] for x in range(16)]
    for x in range(16):
        out[OWN["h0"] + x] = LEVEL[0] * f_tiles[x] / m_tiles[x]
    rows = jnp.concatenate(m_sums + plane_sums(f_tiles), axis=0)
    total = exact_dot(rows, sums)
    out[OWN["counts"]] = jnp.zeros(TILE, F32)
    out[OWN["counts"], : sweeps.shape[0], : sweeps.shape[1]] = sweeps[...].astype(F32)
    upper = core() == 1
    for k in range(5):
        left, width = (0, 64) if k < 4 else (128, 32)
        weight, force = (
            total[row : row + 8, left : left + 128] for row in (8 * k, 40 + 8 * k)
        )
        weight = (0.125 if k < 4 else 0.125 * 0.125) * weight
        force = (0.5 * LEVEL[1] if k < 4 else 0.25 * LEVEL[2]) * force * inverse(weight)
        weight, force = (
            jnp.where(upper, pltpu.roll(tile, width, 1), tile) for tile in (weight, force)
        )
        out[(OWN["w1"] + k) if k < 4 else OWN["w2"]] = weight
        out[(OWN["h1"] + k) if k < 4 else OWN["h2"]] = force


def pack_x(fine, h1, h2, xp, at):
    upward = upward_x()
    start = jnp.where(upward, 12, 0)
    for k in range(4):
        for z in range(2):
            xp[at["h0"] + 2 * k + z] = fine(start + k, z)
    for k in range(2):
        xp[at["h1"] + k] = jnp.where(upward, h1[2 + k], h1[k])
    xp[at["h2"]] = h2


def first_sides_kernel(own, xp, coarse):
    total = [own[0, k] + own[1, k] for k in range(OWN["h1"], OWN["counts"])]
    for k in range(COARSE["size"]):
        coarse[k] = total[k]
    h1, w1 = total[:4], total[4:8]
    h2, w2 = total[8:]
    pack_x(lambda x, z: own[z, x], h1, h2, xp, X_FIRST)
    upward = upward_x()
    edge = OWN["w"] + jnp.where(upward, 15, 0)
    for z in range(2):
        xp[X_FIRST["w"] + z] = own[z, edge]
    sub = sub_index()
    edge_one = jnp.where(upward, turn(w1[3], 4), w1[0])
    edge_two = jnp.where(upward, turn(w2, 6), turn(w2, 4))
    xp[X_FIRST["w12"]] = jnp.where(sub < 4, edge_one, edge_two)


def column_fine(own, planes, xr, at, lo, hi):
    def load(p, z):
        if p < planes:
            return xr[1 - odd_x(), 0, at + 2 * p + z] * lo
        if p < 16 + planes:
            return own(p - planes, z)
        return xr[odd_x(), 1, at + 2 * (p - 16 - planes) + z] * hi

    return load


def pack_fine(load, planes, mine, yp, at):
    for k in range(planes // 2):
        for z in range(2):
            yp[at + 2 * k + z] = jnp.where(mine, load(2 * k, z), turn(load(2 * k + 1, z), 4))


def pack_y(own, h1, h2, xr, yp, y2p, x_at, at):
    lo, hi = flags()[:2]
    mine = (sub_index() < 4) == (core() == 0)
    pack_fine(column_fine(own, 4, xr, x_at["h0"], lo, hi), 24, mine, yp, at["h0"])
    for k in range(2):
        yp[at["h1"] + k] = xr[1 - odd_x(), 0, x_at["h1"] + k] * lo
        yp[at["h1"] + 6 + k] = xr[odd_x(), 1, x_at["h1"] + k] * hi
    for k in range(4):
        yp[at["h1"] + 2 + k] = h1(k)
    two = [xr[1 - odd_x(), 0, x_at["h2"]] * lo, h2(), xr[odd_x(), 1, x_at["h2"]] * hi]
    for k in range(3):
        yp[at["h2"] + k] = two[k]
        y2p[k] = two[k]


def column_w1(p, coarse, xr):
    if p in (0, 9):
        return (xr[1 - odd_x(), 0, X_FIRST["w12"]] if p == 0 else xr[odd_x(), 1, X_FIRST["w12"]]), 0
    return coarse[COARSE["w1"] + (p - 1) // 2], 4 * ((p - 1) % 2)


def column_w2(p, coarse, xr):
    if p in (0, 5):
        return (xr[1 - odd_x(), 0, X_FIRST["w12"]] if p == 0 else xr[odd_x(), 1, X_FIRST["w12"]]), 4
    return coarse[COARSE["w2"]], 2 * (p - 1)


def first_rows_kernel(own, coarse, xr, yp, y2p):
    at = Y_FIRST
    pack_y(
        lambda x, z: own[z, x],
        lambda k: coarse[k],
        lambda: coarse[COARSE["h2"]],
        *(xr, yp, y2p, X_FIRST, at),
    )
    sub = sub_index()
    weights = column_fine(lambda x, z: own[z, OWN["w"] + x], 1, xr, X_FIRST["w"], 1.0, 1.0)
    upward = core() == 1
    for k in range(3):
        for z in range(2):
            packed = None
            for i in range(min(8, 18 - 8 * k)):
                tile = weights(8 * k + i, z)
                row = turn(jnp.where(upward, turn(tile, 1), tile), i)
                packed = row if i == 0 else jnp.where(sub < i, packed, row)
            yp[at["w"] + 2 * k + z] = packed
    for k in range(2):
        packed = None
        for i in range(8):
            p = 8 * k + i
            if p < 10:
                (tile, start), last = column_w1(p, coarse, xr), 3
            else:
                (tile, start), last = column_w2(p - 10, coarse, xr), 1
            row = turn(jnp.where(upward, turn(tile, -start - last), turn(tile, -start)), i)
            packed = row if i == 0 else jnp.where(sub < i, packed, row)
        yp[at["w12"] + k] = packed


def second_rows_kernel(h0, h12, xr, yp, y2p):
    pack_y(
        lambda x, z: h0[x, z],
        lambda k: h12[k],
        lambda: h12[4],
        *(xr, yp, y2p, X_SECOND, Y_SECOND),
    )


def join_fine(load, planes, yr, at, ylo, yhi, *outs):
    sub = sub_index()
    for k in range(planes // 2):
        for z in range(2):
            above, below = yr[1, at + 2 * k + z] * yhi, yr[0, at + 2 * k + z] * ylo
            halos = (
                jnp.where(sub < 4, above, below),
                turn(jnp.where(sub < 4, below, above), 4),
            )
            for i in range(2):
                own = load(2 * k + i, z)
                for out in outs:
                    out[2 * k + i, z] = own
                    out[2 * k + i, 2 + z] = halos[i]


def join_weights(load, yr, at, out):
    sub = sub_index()
    for p in range(18):
        for z in range(2):
            tile, i = at + 2 * (p // 8) + z, p % 8
            above, below = turn(yr[1, tile], -i), turn(yr[0, tile], 7 - i)
            out[p, z] = load(p, z)
            out[p, 2 + z] = jnp.where(sub < 7, above, below)


def four_rows(own, above, below, i):
    sub = sub_index()
    turned = 4 * (1 - i)
    first = jnp.where(sub < 4, turn(own, 4 * i), turn(above, turned))
    return first, keep(sub >= 4, turn(below, turned))


def join_h1(yp, yr, at, *outs):
    ylo, yhi = flags()[2:4]
    for k in range(8):
        tile = at + k
        own, above, below = yp[tile], yr[1, tile] * yhi, yr[0, tile] * ylo
        for i in range(2):
            both = four_rows(own, above, below, i)
            for out in outs:
                out[2 * k + i, 0], out[2 * k + i, 1] = both


def join_coarse_weights(coarse, xr, yr, iw1, iw2):
    sub = sub_index()
    for p in range(16):
        packed, i = Y_FIRST["w12"] + p // 8, p % 8
        above, below = yr[1, packed], yr[0, packed]
        if p < 10:
            (tile, start), rows, out, plane = column_w1(p, coarse, xr), 4, iw1, p
        else:
            (tile, start), rows, out, plane = column_w2(p - 10, coarse, xr), 2, iw2, p - 10
        own = turn(tile, -start)
        out[plane, 0] = inverse(jnp.where(sub < rows, own, keep(sub == rows, turn(above, rows - i))))
        out[plane, 1] = inverse(keep(sub == 7, turn(below, 7 - i)))


def join_h2(yp, yr, at, *outs):
    ylo, yhi, ylo2, yhi2 = flags()[2:]
    sub = sub_index()
    for k in range(3):
        tile, far = at["h2"] + k, at["far"] + k
        own, above, below = yp[tile], yr[1, tile] * yhi, yr[0, tile] * ylo
        above2, below2 = yr[0, far + 3] * yhi2, yr[1, far] * ylo2
        for i in range(4):
            first = jnp.where(sub < 2, turn(own, -2 * i), turn(above, 2 - 2 * i))
            upper = keep(sub < 6, turn(above2, 4 - 2 * i))
            lower = jnp.where(sub < 6, turn(below2, 4 - 2 * i), turn(below, 6 - 2 * i))
            for out in outs:
                out[4 * k + i, 0] = jnp.where(sub < 4, first, upper)
                out[4 * k + i, 1] = keep(sub >= 4, lower)


def along_y(first, second):
    sub = sub_index()
    up_first, up_second = turn(first, 7), turn(second, 7)
    down_first, down_second = turn(first, 1), turn(second, 1)
    sides_first = jnp.where(sub == 7, up_second, up_first) + jnp.where(sub == 0, down_second, down_first)
    sides_second = jnp.where(sub == 7, up_first, up_second) + jnp.where(sub == 0, down_first, down_second)
    return (first + first) + sides_first, (second + second) + sides_second


def along_z_fine(left, right):
    lane = lane_index()
    up_left, up_right = pltpu.roll(left, 127, 1), pltpu.roll(right, 127, 1)
    down_left, down_right = pltpu.roll(left, 1, 1), pltpu.roll(right, 1, 1)
    sides_left = jnp.where(lane < 127, up_left, up_right) + keep(lane > 0, down_left)
    sides_right = keep(lane < 127, up_right) + jnp.where(lane > 0, down_right, down_left)
    return (left + left) + sides_left, (right + right) + sides_right


def along_z_half(mine, other, first):
    lane = lane_index()
    up = jnp.where(lane < 127, pltpu.roll(mine, 127, 1), keep(first, pltpu.roll(other, 127, 1)))
    down = jnp.where(lane > 0, pltpu.roll(mine, 1, 1), jnp.where(first, 0.0, pltpu.roll(other, 1, 1)))
    return (mine + mine) + (up + down)


def along_z_coarse(tile):
    lane = lane_index()
    sides = keep(lane < 127, pltpu.roll(tile, 127, 1)) + keep(lane > 0, pltpu.roll(tile, 1, 1))
    return (tile + tile) + sides


def along_yz(tiles):
    tiles = list(tiles)
    if len(tiles) == 4:
        for z in range(2):
            tiles[z], tiles[2 + z] = along_y(tiles[z], tiles[2 + z])
        for y in range(2):
            tiles[2 * y], tiles[2 * y + 1] = along_z_fine(tiles[2 * y], tiles[2 * y + 1])
        return tiles
    return [along_z_coarse(tile) for tile in along_y(*tiles)]


def added(first, second):
    return [a + b for a, b in zip(first, second)]


def relax_planes(q, h, start, planes, parts, before, masks, factors, active):
    def load(x):
        return [q[x, part] for part in range(parts)]

    kept = KEEP if active is None else 1.0 + active * (KEEP - 1.0)
    here = load(start)
    below = added(before, here)
    for i in range(planes):
        x = start + i
        after = load(x + 1)
        above = added(here, after)
        summed = along_yz(added(below, above))
        for part in range(parts):
            mask = masks[part // (parts // 2)]
            spread = (mask if factors[i] is None else mask * factors[i]) * summed[part]
            source = h[x, part] if active is None else active * h[x, part]
            q[x, part] = (kept * here[part] + spread) + source
        here, below = after, above


def relax_levels(counts, h0, q0, h1, q1, h2, q2):
    lo, hi, ylo, yhi, ylo2, yhi2 = flags()
    sub, lane = sub_index(), lane_index()
    spread = jnp.full(TILE, SPREAD, F32)
    above = jnp.where(sub < 2, 1.0, jnp.where(sub < 4, yhi, jnp.where(sub < 6, yhi2, 0.0)))
    below = jnp.where(sub < 4, 0.0, jnp.where(sub < 6, ylo2, ylo))
    masks2 = (keep(lane < 64, above * spread), keep(lane < 64, below * spread))
    masks1 = (jnp.where(sub < 4, 1.0, yhi) * spread, jnp.where(sub < 4, 0.0, ylo) * spread)
    masks0 = (spread, jnp.where(sub < 4, yhi, ylo) * spread)

    def coarse_sweep(k, _):
        for q, h, planes, masks, count in ((q2, h2, 12, masks2, counts[2]), (q1, h1, 16, masks1, counts[1])):
            active = jnp.where(count > k, 1.0, 0.0)
            factors = [active * lo] * 3 + [active] * (planes - 8) + [active * hi] * 3
            before = [q[0, part] for part in range(2)]
            relax_planes(q, h, 1, planes - 2, 2, before, masks, factors, active)
        return 0

    def fine_sweep(_, __):
        factors = [lo] * 3 + [None] * 16 + [hi] * 3
        before = [q0[0, part] for part in range(4)]
        relax_planes(q0, h0, 1, 22, 4, before, masks0, factors, None)
        return 0

    def both_sweeps(k, _):
        coarse_sweep(k, 0)
        return fine_sweep(k, 0)

    coarse_count = jnp.maximum(counts[1], counts[2])
    shared = jnp.minimum(counts[0], coarse_count)
    lax.fori_loop(1, shared, both_sweeps, 0)
    lax.fori_loop(shared, coarse_count, coarse_sweep, 0)
    lax.fori_loop(shared, counts[0], fine_sweep, 0)


def sweep_counts(own, cycle):
    held, sub, lane = own[0, OWN["counts"]], sub_index(), lane_index()
    return [
        jnp.max(keep((sub == cycle) & (lane == level), held)).astype(jnp.int32) for level in range(3)
    ]


def corrections(q1, iw1, q2, iw2, copies):
    sub = sub_index()
    one, two = (
        [
            jnp.where(sub < 7, q[p + 3, 0] * iw[p, 0], q[p + 3, 1] * iw[p, 1])
            for p in range(planes)
        ]
        for q, iw, planes in ((q1, iw1, 10), (q2, iw2, 6))
    )
    spread = []
    for tile in two:
        inner = jnp.where(sub < 3, turn(tile, 1), turn(tile, 2))
        spread.append(jnp.where((sub == 0) | (sub == 7), tile, inner))
    rows = [jnp.concatenate([one[p], spread[(p + 1) // 2]], axis=1) for p in range(10)]
    return exact_dot(jnp.concatenate(rows, axis=0), copies[...])


def iterate(coarse, q0, w, before, out):
    sub = sub_index()
    for k in range(10):
        for z in range(2):
            tile = coarse[8 * k : 8 * k + 8, 128 * z : 128 * z + 128]
            turned = [tile] + [turn(tile, by) for by in range(1, 5)]
            rows = turned[4]
            for by, last in ((3, 6), (2, 4), (1, 2), (0, 0)):
                rows = jnp.where(sub <= last, turned[by], rows)
            halo = jnp.where(sub < 7, turned[4], tile)
            for p in (2 * k - 1, 2 * k):
                if 0 <= p < 18:
                    for part, value in ((z, rows), (2 + z, halo)):
                        total = q0[p + 3, part] + w[p, part] * value
                        if before is not None:
                            total = before[p, part] + total
                        out[p, part] = total


def defects(pf, first=None):
    def load(p):
        return [pf[p, part] for part in range(4)]

    here = load(1)
    below = added(load(0), here)
    for x in range(16):
        after = load(x + 2)
        above = added(here, after)
        both = added(below, above)
        if first is None:
            own, summed = here[:2], along_yz(both)
        else:
            left, right = (along_y(both[z], both[2 + z])[0] for z in range(2))
            mine, other = jnp.where(first, left, right), jnp.where(first, right, left)
            own, summed = [jnp.where(first, here[0], here[1])], [along_z_half(mine, other, first)]
        yield own, [SELF_WEIGHT * a - SIDE_CUBE * b for a, b in zip(own, summed)]
        here, below = after, above


def middle_kernel(
    own, coarse, xr, yp, yr, sums, copies,
    xp, pf, w, iw1, iw2, h0_next, h12_next,
    h0_all, q0, h1_all, q1, h2_all, q2,
):
    counts = sweep_counts(own, 0)
    lo, hi, ylo, yhi = flags()[:4]
    load = column_fine(lambda x, z: own[z, x], 4, xr, X_FIRST["h0"], lo, hi)
    join_fine(load, 24, yr, Y_FIRST["h0"], ylo, yhi, h0_all, q0)
    load = column_fine(lambda x, z: own[z, OWN["w"] + x], 1, xr, X_FIRST["w"], 1.0, 1.0)
    join_weights(load, yr, Y_FIRST["w"], w)
    join_h1(yp, yr, Y_FIRST["h1"], h1_all, q1)
    join_h2(yp, yr, Y_FIRST, h2_all, q2)
    join_coarse_weights(coarse, xr, yr, iw1, iw2)
    relax_levels(counts, h0_all, q0, h1_all, q1, h2_all, q2)
    iterate(corrections(q1, iw1, q2, iw2, copies), q0, w, None, pf)

    rests = [[], []]
    for x, (_, defect) in enumerate(defects(pf)):
        for z in range(2):
            h0 = own[z, x] - LEVEL[0] * defect[z]
            h0_next[x, z] = h0
            rests[z].append(own[z, OWN["w"] + x] * h0)
    summed = [plane_sums(rest) for rest in rests]
    rows = [jnp.concatenate([summed[0][k], summed[1][k]], axis=1) for k in range(5)]
    total = exact_dot(jnp.concatenate(rows, axis=0), sums[...])
    h1 = []
    for k in range(4):
        weight = coarse[COARSE["w1"] + k]
        h1.append(0.5 * LEVEL[1] / LEVEL[0] * total[8 * k : 8 * k + 8, :128] / weight)
        h12_next[k] = h1[k]
    weight = inverse(coarse[COARSE["w2"]])
    h2 = 0.25 * LEVEL[2] / LEVEL[0] * total[32:40, 128:] * weight
    h12_next[4] = h2
    pack_x(lambda x, z: h0_next[x, z], h1, h2, xp, X_SECOND)


def last_kernel(
    own, m, f, h0, xr, yp, yr, pf, w, iw1, iw2, copies,
    solution_out, residual_out,
    h0_all, q0, h1_all, q1, h2_all, q2, pf_all, solved, left, sent,
):
    counts = sweep_counts(own, 1)
    lo, hi, ylo, yhi = flags()[:4]
    load = column_fine(lambda x, z: h0[x, z], 4, xr, X_SECOND["h0"], lo, hi)
    join_fine(load, 24, yr, Y_SECOND["h0"], ylo, yhi, h0_all, q0)
    join_h1(yp, yr, Y_SECOND["h1"], h1_all, q1)
    join_h2(yp, yr, Y_SECOND, h2_all, q2)
    relax_levels(counts, h0_all, q0, h1_all, q1, h2_all, q2)
    iterate(corrections(q1, iw1, q2, iw2, copies), q0, w, pf, pf_all)
    first = core() == 0
    for x, ((mine,), (rest,)) in enumerate(defects(pf_all, first)):
        weight = m[x]
        solved[x] = mine / weight
        left[x] = f[x] - weight * rest
    sends = [
        pltpu.make_async_copy(source, target, sent.at[k])
        for k, (source, target) in enumerate(((solved, solution_out), (left, residual_out)))
    ]
    for send in sends:
        send.start()
    for send in sends:
        send.wait()


def call(kernel, outs, scratch, name, *operands, outside=0, outs_outside=False):
    whole = pl.BlockSpec(memory_space=pltpu.HBM)
    vmem = pl.BlockSpec(memory_space=pltpu.VMEM)
    return pl.pallas_call(
        kernel,
        out_shape=[jax.ShapeDtypeStruct(shape, F32) for shape in outs],
        in_specs=[whole] * outside + [vmem] * (len(operands) - outside),
        out_specs=[whole if outs_outside else vmem] * len(outs),
        scratch_shapes=scratch,
        compiler_params=pltpu.CompilerParams(vmem_limit_bytes=32 * 2**20),
        name=name,
    )(*(pltpu.with_memory_space_constraint(x, pltpu.HBM) for x in operands[:outside]), *operands[outside:])


def space(*dims):
    return pltpu.VMEM(tiles(*dims), F32)


def tiles(*dims):
    return (*dims, *TILE)


def share(value):
    return lax.all_gather(value, "group", axis=0)


def trade_x(packed):
    names = ("group", "gx", "gy")
    sizes = [lax.axis_size(name) for name in names]
    index = np.arange(np.prod(sizes)).reshape(sizes)
    inner = [
        np.stack([index[k, k:-1:2], index[k, k + 1 :: 2]], axis=-1)
        for k in range(2)
    ]
    ends = [index[1, 0], index[1, -1]]
    groups = np.concatenate([pair.reshape(-1, 2) for pair in [*inner, *ends]]).tolist()
    return share(lax.all_gather(packed, names, axis=0, axis_index_groups=groups))


def trade_y(packed, packed_far):
    size = lax.axis_size("gy")
    moves = []
    for i in range(size - 1):
        moves += [(size + i, i + 1), (i + 1, size + i)]
    near = lax.ppermute(packed, ("group", "gy"), moves)
    groups = [[i, size + i + 2] for i in range(size - 2)]
    groups += [[size - 2, size - 1], [size, size + 1]]
    far = lax.all_gather(packed_far, ("group", "gy"), axis=0, tiled=True, axis_index_groups=groups)
    return share(jnp.concatenate([near, far], axis=0))


def on_device(forcing, metric, sweeps):
    sums, copies = (jnp.asarray(matrix, jnp.bfloat16) for matrix in (WHOLE_SUMS, COPIES))
    spaces = [space(24, 4)] * 2 + [space(16, 2)] * 2 + [space(12, 2)] * 2

    (own,) = call(
        first_kernel,
        [tiles(OWN["size"])],
        [
            *(space(16), space(16), pltpu.VMEM(sweeps.shape, jnp.int32)),
            pltpu.SemaphoreType.DMA((3,)),
        ],
        "block_sums",
        *(metric, forcing, sweeps),
        outside=3,
    )
    own = share(own)
    xp, coarse = call(
        first_sides_kernel,
        [tiles(X_FIRST["size"]), tiles(COARSE["size"])],
        [],
        "first_sides",
        own,
    )
    xr = trade_x(xp)
    yp, y2p = call(
        first_rows_kernel,
        [tiles(Y_FIRST["size"]), tiles(3)],
        [],
        "first_rows",
        *(own, coarse, xr),
    )
    yr = trade_y(yp, y2p)
    xp, pf, w, iw1, iw2, h0, h12 = call(
        middle_kernel,
        [
            *(tiles(X_SECOND["size"]), tiles(18, 4), tiles(18, 4), tiles(10, 2), tiles(6, 2)),
            *(tiles(16, 2), tiles(5)),
        ],
        spaces,
        "first_cycle",
        *(own, coarse, xr, yp, yr, sums, copies),
    )
    xr = trade_x(xp)
    yp, y2p = call(
        second_rows_kernel,
        [tiles(Y_SECOND["size"]), tiles(3)],
        [],
        "second_rows",
        *(h0, h12, xr),
    )
    yr = trade_y(yp, y2p)
    return call(
        last_kernel,
        [tiles(16), tiles(16)],
        [*spaces, space(18, 4), space(16), space(16), pltpu.SemaphoreType.DMA((2,))],
        "second_cycle",
        *(own, metric, forcing, h0, xr, yp, yr, pf, w, iw1, iw2, copies),
        outs_outside=True,
    )


def solution(mesh):
    def program(forcing, metric, sweeps):
        return tuple(on_device(forcing, metric, sweeps))

    return jax.shard_map(
        program,
        mesh=mesh,
        in_specs=(P("gx", "gy", "group"), P("gx", "gy", "group"), P()),
        out_specs=(P("gx", "gy", "group"), P("gx", "gy", "group")),
        check_vma=False,
    )
```

```python
import jax
import jax.numpy as jnp
import numpy as np
from jax import lax
from jax.experimental import pallas as pl
from jax.experimental.pallas import tpu as pltpu
from jax.sharding import PartitionSpec as P

RELAXATION = 0.8
SIDE_WEIGHT = 0.05 ** (1.0 / 3.0)
SELF_WEIGHT = 3.4
SIDE_CUBE = SIDE_WEIGHT**3

KEEP = 1.0 - RELAXATION * SELF_WEIGHT / 3.0
SPREAD = RELAXATION * SIDE_CUBE / 3.0
LEVEL = [RELAXATION / (3.0 * 4.0**-level) for level in range(3)]

F32 = jnp.float32
TILE = (8, 128)

OWN = dict(h0=0, w=16, h1=32, w1=36, h2=40, w2=41, counts=42, size=43)
COARSE = dict(h1=0, w1=4, h2=8, w2=9, size=10)
X_FIRST = dict(h0=0, h1=8, h2=10, w=11, w12=13, size=14)
X_SECOND = dict(h0=0, h1=8, h2=10, size=11)
Y_FIRST = dict(h0=0, h1=24, h2=32, w=35, w12=41, size=43, far=43)
Y_SECOND = dict(h0=0, h1=24, h2=32, size=35, far=35)

LANES = np.arange(256)
WHOLE_SUMS = np.concatenate(
    [LANES[:, None] // 2 == LANES[None, :128], LANES[:, None] // 4 == LANES[None, :128]], axis=1
).astype(np.float32)
COPIES = WHOLE_SUMS.T * np.where(LANES[:, None] < 128, 0.5, 0.25).astype(np.float32)


def exact_dot(rows, matrix):
    parts = []
    rest = rows
    for _ in range(3):
        parts.append(rest.astype(jnp.bfloat16))
        rest = rest - parts[-1].astype(F32)
    out = lax.dot_general(
        jnp.concatenate(parts, axis=0),
        matrix,
        (((1,), (0,)), ((), ())),
        preferred_element_type=F32,
    )
    count = rows.shape[0]
    return out[:count] + (out[count : 2 * count] + out[2 * count :])


def sub_index():
    return lax.broadcasted_iota(jnp.int32, TILE, 0)


def lane_index():
    return lax.broadcasted_iota(jnp.int32, TILE, 1)


def turn(tile, by):
    by %= 8
    return pltpu.roll(tile, by, 0) if by else tile


def keep(where, tile):
    return jnp.where(where, tile, 0.0)


def inverse(tile):
    return jnp.where(tile > 0, 1.0 / jnp.where(tile > 0, tile, 1.0), 0.0)


def core():
    return lax.axis_index("group")


def odd_x():
    return lax.rem(lax.axis_index("gx"), 2)


def upward_x():
    return core() == odd_x()


def flags():
    gx, gy = lax.axis_index("gx"), lax.axis_index("gy")
    x_last, y_last = lax.axis_size("gx") - 1, lax.axis_size("gy") - 1
    places = [gx > 0, gx < x_last, gy > 0, gy < y_last, gy > 1, gy < y_last - 1]
    return [place.astype(F32) for place in places]


def pair_rows(first, second):
    sub = sub_index()
    first, second = (tile + turn(tile, 7) for tile in (first, second))
    low = jnp.where(sub == 0, first, turn(first, 7))
    low = jnp.where(sub < 2, low, jnp.where(sub == 2, turn(first, 6), turn(first, 5)))
    high = jnp.where(sub == 4, turn(second, 4), turn(second, 3))
    high = jnp.where(sub < 6, high, jnp.where(sub == 6, turn(second, 2), turn(second, 1)))
    return jnp.where(sub < 4, low, high)


def plane_sums(fine):
    sub = sub_index()
    sums = [fine[2 * k] + fine[2 * k + 1] for k in range(8)]
    one = [pair_rows(sums[2 * k], sums[2 * k + 1]) for k in range(4)]
    two = None
    for k in range(4):
        both = one[k] + turn(one[k], 4)
        both = both + turn(both, 7)
        placed = jnp.where(sub == 2 * k, turn(both, 2 * k), turn(both, 2 * k - 1))
        two = placed if k == 0 else jnp.where(sub < 2 * k, two, placed)
    return one + [two]


def half_sums():
    row = lax.broadcasted_iota(jnp.int32, (128, 128), 0)
    column = lax.broadcasted_iota(jnp.int32, (128, 128), 1)
    matrix = jnp.concatenate([row >> 1 == column, row >> 2 == column], axis=1)
    return jnp.where(matrix, 1.0, 0.0).astype(jnp.bfloat16)


def first_kernel(m_whole, f_whole, sweeps_whole, out, m, f, sweeps, arrived):
    moves = ((m_whole, m), (f_whole, f), (sweeps_whole, sweeps))
    copies = [
        pltpu.make_async_copy(source, target, arrived.at[k])
        for k, (source, target) in enumerate(moves)
    ]
    for copy in copies:
        copy.start()
    sums = half_sums()
    copies[0].wait()
    m_tiles = [m[x] for x in range(16)]
    m_sums = plane_sums(m_tiles)
    for x in range(16):
        out[OWN["w"] + x] = m_tiles[x]
    for copy in copies[1:]:
        copy.wait()
    f_tiles = [f[x] for x in range(16)]
    for x in range(16):
        out[OWN["h0"] + x] = LEVEL[0] * f_tiles[x] / m_tiles[x]
    rows = jnp.concatenate(m_sums + plane_sums(f_tiles), axis=0)
    total = exact_dot(rows, sums)
    out[OWN["counts"]] = jnp.zeros(TILE, F32)
    out[OWN["counts"], : sweeps.shape[0], : sweeps.shape[1]] = sweeps[...].astype(F32)
    upper = core() == 1
    for k in range(5):
        left, width = (0, 64) if k < 4 else (128, 32)
        weight, force = (
            total[row : row + 8, left : left + 128] for row in (8 * k, 40 + 8 * k)
        )
        weight = (0.125 if k < 4 else 0.125 * 0.125) * weight
        force = (0.5 * LEVEL[1] if k < 4 else 0.25 * LEVEL[2]) * force * inverse(weight)
        weight, force = (
            jnp.where(upper, pltpu.roll(tile, width, 1), tile) for tile in (weight, force)
        )
        out[(OWN["w1"] + k) if k < 4 else OWN["w2"]] = weight
        out[(OWN["h1"] + k) if k < 4 else OWN["h2"]] = force


def pack_x(fine, h1, h2, xp, at):
    upward = upward_x()
    start = jnp.where(upward, 12, 0)
    for k in range(4):
        for z in range(2):
            xp[at["h0"] + 2 * k + z] = fine(start + k, z)
    for k in range(2):
        xp[at["h1"] + k] = jnp.where(upward, h1[2 + k], h1[k])
    xp[at["h2"]] = h2


def first_sides_kernel(own, xp, coarse):
    total = [own[0, k] + own[1, k] for k in range(OWN["h1"], OWN["counts"])]
    for k in range(COARSE["size"]):
        coarse[k] = total[k]
    h1, w1 = total[:4], total[4:8]
    h2, w2 = total[8:]
    pack_x(lambda x, z: own[z, x], h1, h2, xp, X_FIRST)
    upward = upward_x()
    edge = OWN["w"] + jnp.where(upward, 15, 0)
    for z in range(2):
        xp[X_FIRST["w"] + z] = own[z, edge]
    sub = sub_index()
    edge_one = jnp.where(upward, turn(w1[3], 4), w1[0])
    edge_two = jnp.where(upward, turn(w2, 6), turn(w2, 4))
    xp[X_FIRST["w12"]] = jnp.where(sub < 4, edge_one, edge_two)


def column_fine(own, planes, xr, at, lo, hi):
    def load(p, z):
        if p < planes:
            return xr[1 - odd_x(), 0, at + 2 * p + z] * lo
        if p < 16 + planes:
            return own(p - planes, z)
        return xr[odd_x(), 1, at + 2 * (p - 16 - planes) + z] * hi

    return load


def pack_fine(load, planes, mine, yp, at):
    for k in range(planes // 2):
        for z in range(2):
            yp[at + 2 * k + z] = jnp.where(mine, load(2 * k, z), turn(load(2 * k + 1, z), 4))


def pack_y(own, h1, h2, xr, yp, y2p, x_at, at):
    lo, hi = flags()[:2]
    mine = (sub_index() < 4) == (core() == 0)
    pack_fine(column_fine(own, 4, xr, x_at["h0"], lo, hi), 24, mine, yp, at["h0"])
    for k in range(2):
        yp[at["h1"] + k] = xr[1 - odd_x(), 0, x_at["h1"] + k] * lo
        yp[at["h1"] + 6 + k] = xr[odd_x(), 1, x_at["h1"] + k] * hi
    for k in range(4):
        yp[at["h1"] + 2 + k] = h1(k)
    two = [xr[1 - odd_x(), 0, x_at["h2"]] * lo, h2(), xr[odd_x(), 1, x_at["h2"]] * hi]
    for k in range(3):
        yp[at["h2"] + k] = two[k]
        y2p[k] = two[k]


def column_w1(p, coarse, xr):
    if p in (0, 9):
        return (xr[1 - odd_x(), 0, X_FIRST["w12"]] if p == 0 else xr[odd_x(), 1, X_FIRST["w12"]]), 0
    return coarse[COARSE["w1"] + (p - 1) // 2], 4 * ((p - 1) % 2)


def column_w2(p, coarse, xr):
    if p in (0, 5):
        return (xr[1 - odd_x(), 0, X_FIRST["w12"]] if p == 0 else xr[odd_x(), 1, X_FIRST["w12"]]), 4
    return coarse[COARSE["w2"]], 2 * (p - 1)


def first_rows_kernel(own, coarse, xr, yp, y2p):
    at = Y_FIRST
    pack_y(
        lambda x, z: own[z, x],
        lambda k: coarse[k],
        lambda: coarse[COARSE["h2"]],
        *(xr, yp, y2p, X_FIRST, at),
    )
    sub = sub_index()
    weights = column_fine(lambda x, z: own[z, OWN["w"] + x], 1, xr, X_FIRST["w"], 1.0, 1.0)
    upward = core() == 1
    for k in range(3):
        for z in range(2):
            packed = None
            for i in range(min(8, 18 - 8 * k)):
                tile = weights(8 * k + i, z)
                row = turn(jnp.where(upward, turn(tile, 1), tile), i)
                packed = row if i == 0 else jnp.where(sub < i, packed, row)
            yp[at["w"] + 2 * k + z] = packed
    for k in range(2):
        packed = None
        for i in range(8):
            p = 8 * k + i
            if p < 10:
                (tile, start), last = column_w1(p, coarse, xr), 3
            else:
                (tile, start), last = column_w2(p - 10, coarse, xr), 1
            row = turn(jnp.where(upward, turn(tile, -start - last), turn(tile, -start)), i)
            packed = row if i == 0 else jnp.where(sub < i, packed, row)
        yp[at["w12"] + k] = packed


def second_rows_kernel(h0, h12, xr, yp, y2p):
    pack_y(
        lambda x, z: h0[x, z],
        lambda k: h12[k],
        lambda: h12[4],
        *(xr, yp, y2p, X_SECOND, Y_SECOND),
    )


def join_fine(load, planes, yr, at, ylo, yhi, *outs):
    sub = sub_index()
    for k in range(planes // 2):
        for z in range(2):
            above, below = yr[1, at + 2 * k + z] * yhi, yr[0, at + 2 * k + z] * ylo
            halos = (
                jnp.where(sub < 4, above, below),
                turn(jnp.where(sub < 4, below, above), 4),
            )
            for i in range(2):
                own = load(2 * k + i, z)
                for out in outs:
                    out[2 * k + i, z] = own
                    out[2 * k + i, 2 + z] = halos[i]


def join_weights(load, yr, at, out):
    sub = sub_index()
    for p in range(18):
        for z in range(2):
            tile, i = at + 2 * (p // 8) + z, p % 8
            above, below = turn(yr[1, tile], -i), turn(yr[0, tile], 7 - i)
            out[p, z] = load(p, z)
            out[p, 2 + z] = jnp.where(sub < 7, above, below)


def four_rows(own, above, below, i):
    sub = sub_index()
    turned = 4 * (1 - i)
    first = jnp.where(sub < 4, turn(own, 4 * i), turn(above, turned))
    return first, keep(sub >= 4, turn(below, turned))


def join_h1(yp, yr, at, *outs):
    ylo, yhi = flags()[2:4]
    for k in range(8):
        tile = at + k
        own, above, below = yp[tile], yr[1, tile] * yhi, yr[0, tile] * ylo
        for i in range(2):
            both = four_rows(own, above, below, i)
            for out in outs:
                out[2 * k + i, 0], out[2 * k + i, 1] = both


def join_coarse_weights(coarse, xr, yr, iw1, iw2):
    sub = sub_index()
    for p in range(16):
        packed, i = Y_FIRST["w12"] + p // 8, p % 8
        above, below = yr[1, packed], yr[0, packed]
        if p < 10:
            (tile, start), rows, out, plane = column_w1(p, coarse, xr), 4, iw1, p
        else:
            (tile, start), rows, out, plane = column_w2(p - 10, coarse, xr), 2, iw2, p - 10
        own = turn(tile, -start)
        out[plane, 0] = inverse(jnp.where(sub < rows, own, keep(sub == rows, turn(above, rows - i))))
        out[plane, 1] = inverse(keep(sub == 7, turn(below, 7 - i)))


def join_h2(yp, yr, at, *outs):
    ylo, yhi, ylo2, yhi2 = flags()[2:]
    sub = sub_index()
    for k in range(3):
        tile, far = at["h2"] + k, at["far"] + k
        own, above, below = yp[tile], yr[1, tile] * yhi, yr[0, tile] * ylo
        above2, below2 = yr[0, far + 3] * yhi2, yr[1, far] * ylo2
        for i in range(4):
            first = jnp.where(sub < 2, turn(own, -2 * i), turn(above, 2 - 2 * i))
            upper = keep(sub < 6, turn(above2, 4 - 2 * i))
            lower = jnp.where(sub < 6, turn(below2, 4 - 2 * i), turn(below, 6 - 2 * i))
            for out in outs:
                out[4 * k + i, 0] = jnp.where(sub < 4, first, upper)
                out[4 * k + i, 1] = keep(sub >= 4, lower)


def along_y(first, second):
    sub = sub_index()
    up_first, up_second = turn(first, 7), turn(second, 7)
    down_first, down_second = turn(first, 1), turn(second, 1)
    sides_first = jnp.where(sub == 7, up_second, up_first) + jnp.where(sub == 0, down_second, down_first)
    sides_second = jnp.where(sub == 7, up_first, up_second) + jnp.where(sub == 0, down_first, down_second)
    return (first + first) + sides_first, (second + second) + sides_second


def along_z_fine(left, right):
    lane = lane_index()
    up_left, up_right = pltpu.roll(left, 127, 1), pltpu.roll(right, 127, 1)
    down_left, down_right = pltpu.roll(left, 1, 1), pltpu.roll(right, 1, 1)
    sides_left = jnp.where(lane < 127, up_left, up_right) + keep(lane > 0, down_left)
    sides_right = keep(lane < 127, up_right) + jnp.where(lane > 0, down_right, down_left)
    return (left + left) + sides_left, (right + right) + sides_right


def along_z_coarse(tile):
    lane = lane_index()
    sides = keep(lane < 127, pltpu.roll(tile, 127, 1)) + keep(lane > 0, pltpu.roll(tile, 1, 1))
    return (tile + tile) + sides


def along_yz(tiles):
    tiles = list(tiles)
    if len(tiles) == 4:
        for z in range(2):
            tiles[z], tiles[2 + z] = along_y(tiles[z], tiles[2 + z])
        for y in range(2):
            tiles[2 * y], tiles[2 * y + 1] = along_z_fine(tiles[2 * y], tiles[2 * y + 1])
        return tiles
    return [along_z_coarse(tile) for tile in along_y(*tiles)]


def added(first, second):
    return [a + b for a, b in zip(first, second)]


def relax_planes(q, h, start, planes, parts, before, masks, factors, active):
    def load(x):
        return [q[x, part] for part in range(parts)]

    kept = KEEP if active is None else 1.0 + active * (KEEP - 1.0)
    here = load(start)
    below = added(before, here)
    for i in range(planes):
        x = start + i
        after = load(x + 1)
        above = added(here, after)
        summed = along_yz(added(below, above))
        for part in range(parts):
            mask = masks[part // (parts // 2)]
            spread = (mask if factors[i] is None else mask * factors[i]) * summed[part]
            source = h[x, part] if active is None else active * h[x, part]
            q[x, part] = (kept * here[part] + spread) + source
        here, below = after, above


def relax_levels(counts, h0, q0, h1, q1, h2, q2):
    lo, hi, ylo, yhi, ylo2, yhi2 = flags()
    sub, lane = sub_index(), lane_index()
    spread = jnp.full(TILE, SPREAD, F32)
    above = jnp.where(sub < 2, 1.0, jnp.where(sub < 4, yhi, jnp.where(sub < 6, yhi2, 0.0)))
    below = jnp.where(sub < 4, 0.0, jnp.where(sub < 6, ylo2, ylo))
    masks2 = (keep(lane < 64, above * spread), keep(lane < 64, below * spread))
    masks1 = (jnp.where(sub < 4, 1.0, yhi) * spread, jnp.where(sub < 4, 0.0, ylo) * spread)
    masks0 = (spread, jnp.where(sub < 4, yhi, ylo) * spread)

    def coarse_sweep(k, _):
        for q, h, planes, masks, count in ((q2, h2, 12, masks2, counts[2]), (q1, h1, 16, masks1, counts[1])):
            active = jnp.where(count > k, 1.0, 0.0)
            factors = [active * lo] * 3 + [active] * (planes - 8) + [active * hi] * 3
            before = [q[0, part] for part in range(2)]
            relax_planes(q, h, 1, planes - 2, 2, before, masks, factors, active)
        return 0

    def fine_sweep(_, __):
        factors = [lo] * 3 + [None] * 16 + [hi] * 3
        before = [q0[0, part] for part in range(4)]
        relax_planes(q0, h0, 1, 22, 4, before, masks0, factors, None)
        return 0

    def both_sweeps(k, _):
        coarse_sweep(k, 0)
        return fine_sweep(k, 0)

    coarse_count = jnp.maximum(counts[1], counts[2])
    shared = jnp.minimum(counts[0], coarse_count)
    lax.fori_loop(1, shared, both_sweeps, 0)
    lax.fori_loop(shared, coarse_count, coarse_sweep, 0)
    lax.fori_loop(shared, counts[0], fine_sweep, 0)


def sweep_counts(own, cycle):
    held, sub, lane = own[0, OWN["counts"]], sub_index(), lane_index()
    return [
        jnp.max(keep((sub == cycle) & (lane == level), held)).astype(jnp.int32) for level in range(3)
    ]


def corrections(q1, iw1, q2, iw2, copies):
    sub = sub_index()
    one, two = (
        [
            jnp.where(sub < 7, q[p + 3, 0] * iw[p, 0], q[p + 3, 1] * iw[p, 1])
            for p in range(planes)
        ]
        for q, iw, planes in ((q1, iw1, 10), (q2, iw2, 6))
    )
    spread = []
    for tile in two:
        inner = jnp.where(sub < 3, turn(tile, 1), turn(tile, 2))
        spread.append(jnp.where((sub == 0) | (sub == 7), tile, inner))
    rows = [jnp.concatenate([one[p], spread[(p + 1) // 2]], axis=1) for p in range(10)]
    return exact_dot(jnp.concatenate(rows, axis=0), copies[...])


def iterate(coarse, q0, w, before, out):
    sub = sub_index()
    for k in range(10):
        for z in range(2):
            tile = coarse[8 * k : 8 * k + 8, 128 * z : 128 * z + 128]
            turned = [tile] + [turn(tile, by) for by in range(1, 5)]
            rows = turned[4]
            for by, last in ((3, 6), (2, 4), (1, 2), (0, 0)):
                rows = jnp.where(sub <= last, turned[by], rows)
            halo = jnp.where(sub < 7, turned[4], tile)
            for p in (2 * k - 1, 2 * k):
                if 0 <= p < 18:
                    for part, value in ((z, rows), (2 + z, halo)):
                        total = q0[p + 3, part] + w[p, part] * value
                        if before is not None:
                            total = before[p, part] + total
                        out[p, part] = total


def defects(pf):
    def load(p):
        return [pf[p, part] for part in range(4)]

    here = load(1)
    below = added(load(0), here)
    for x in range(16):
        after = load(x + 2)
        above = added(here, after)
        summed = along_yz(added(below, above))
        yield here[:2], [SELF_WEIGHT * here[z] - SIDE_CUBE * summed[z] for z in range(2)]
        here, below = after, above


def middle_kernel(
    own, coarse, xr, yp, yr, sums, copies,
    xp, pf, w, iw1, iw2, h0_next, h12_next,
    h0_all, q0, h1_all, q1, h2_all, q2,
):
    counts = sweep_counts(own, 0)
    lo, hi, ylo, yhi = flags()[:4]
    load = column_fine(lambda x, z: own[z, x], 4, xr, X_FIRST["h0"], lo, hi)
    join_fine(load, 24, yr, Y_FIRST["h0"], ylo, yhi, h0_all, q0)
    load = column_fine(lambda x, z: own[z, OWN["w"] + x], 1, xr, X_FIRST["w"], 1.0, 1.0)
    join_weights(load, yr, Y_FIRST["w"], w)
    join_h1(yp, yr, Y_FIRST["h1"], h1_all, q1)
    join_h2(yp, yr, Y_FIRST, h2_all, q2)
    join_coarse_weights(coarse, xr, yr, iw1, iw2)
    relax_levels(counts, h0_all, q0, h1_all, q1, h2_all, q2)
    iterate(corrections(q1, iw1, q2, iw2, copies), q0, w, None, pf)

    rests = [[], []]
    for x, (_, defect) in enumerate(defects(pf)):
        for z in range(2):
            h0 = own[z, x] - LEVEL[0] * defect[z]
            h0_next[x, z] = h0
            rests[z].append(own[z, OWN["w"] + x] * h0)
    summed = [plane_sums(rest) for rest in rests]
    rows = [jnp.concatenate([summed[0][k], summed[1][k]], axis=1) for k in range(5)]
    total = exact_dot(jnp.concatenate(rows, axis=0), sums[...])
    h1 = []
    for k in range(4):
        weight = coarse[COARSE["w1"] + k]
        h1.append(0.5 * LEVEL[1] / LEVEL[0] * total[8 * k : 8 * k + 8, :128] / weight)
        h12_next[k] = h1[k]
    weight = inverse(coarse[COARSE["w2"]])
    h2 = 0.25 * LEVEL[2] / LEVEL[0] * total[32:40, 128:] * weight
    h12_next[4] = h2
    pack_x(lambda x, z: h0_next[x, z], h1, h2, xp, X_SECOND)


def last_kernel(
    own, m, f, h0, xr, yp, yr, pf, w, iw1, iw2, copies,
    solution_out, residual_out,
    h0_all, q0, h1_all, q1, h2_all, q2, pf_all, solved, left, sent,
):
    counts = sweep_counts(own, 1)
    lo, hi, ylo, yhi = flags()[:4]
    load = column_fine(lambda x, z: h0[x, z], 4, xr, X_SECOND["h0"], lo, hi)
    join_fine(load, 24, yr, Y_SECOND["h0"], ylo, yhi, h0_all, q0)
    join_h1(yp, yr, Y_SECOND["h1"], h1_all, q1)
    join_h2(yp, yr, Y_SECOND, h2_all, q2)
    relax_levels(counts, h0_all, q0, h1_all, q1, h2_all, q2)
    iterate(corrections(q1, iw1, q2, iw2, copies), q0, w, pf, pf_all)
    first = core() == 0
    sends = [
        pltpu.make_async_copy(source, target, sent.at[k])
        for k, (source, target) in enumerate(((solved, solution_out), (left, residual_out)))
    ]
    for x in range(16):
        solved[x] = jnp.where(first, pf_all[x + 1, 0], pf_all[x + 1, 1]) / m[x]
    sends[0].start()
    for x, (_, defect) in enumerate(defects(pf_all)):
        left[x] = f[x] - m[x] * jnp.where(first, defect[0], defect[1])
    sends[1].start()
    for send in sends:
        send.wait()


def call(kernel, outs, scratch, name, *operands, outside=0, outs_outside=False):
    whole = pl.BlockSpec(memory_space=pltpu.HBM)
    vmem = pl.BlockSpec(memory_space=pltpu.VMEM)
    return pl.pallas_call(
        kernel,
        out_shape=[jax.ShapeDtypeStruct(shape, F32) for shape in outs],
        in_specs=[whole] * outside + [vmem] * (len(operands) - outside),
        out_specs=[whole if outs_outside else vmem] * len(outs),
        scratch_shapes=scratch,
        compiler_params=pltpu.CompilerParams(vmem_limit_bytes=32 * 2**20),
        name=name,
    )(*(pltpu.with_memory_space_constraint(x, pltpu.HBM) for x in operands[:outside]), *operands[outside:])


def space(*dims):
    return pltpu.VMEM(tiles(*dims), F32)


def tiles(*dims):
    return (*dims, *TILE)


def share(value):
    return lax.all_gather(value, "group", axis=0)


def trade_x(packed):
    names = ("group", "gx", "gy")
    sizes = [lax.axis_size(name) for name in names]
    index = np.arange(np.prod(sizes)).reshape(sizes)
    inner = [
        np.stack([index[k, k:-1:2], index[k, k + 1 :: 2]], axis=-1)
        for k in range(2)
    ]
    ends = [index[1, 0], index[1, -1]]
    groups = np.concatenate([pair.reshape(-1, 2) for pair in [*inner, *ends]]).tolist()
    return share(lax.all_gather(packed, names, axis=0, axis_index_groups=groups))


def trade_y(packed, packed_far):
    size = lax.axis_size("gy")
    moves = []
    for i in range(size - 1):
        moves += [(size + i, i + 1), (i + 1, size + i)]
    near = lax.ppermute(packed, ("group", "gy"), moves)
    groups = [[i, size + i + 2] for i in range(size - 2)]
    groups += [[size - 2, size - 1], [size, size + 1]]
    far = lax.all_gather(packed_far, ("group", "gy"), axis=0, tiled=True, axis_index_groups=groups)
    return share(jnp.concatenate([near, far], axis=0))


def on_device(forcing, metric, sweeps):
    sums, copies = (jnp.asarray(matrix, jnp.bfloat16) for matrix in (WHOLE_SUMS, COPIES))
    spaces = [space(24, 4)] * 2 + [space(16, 2)] * 2 + [space(12, 2)] * 2

    (own,) = call(
        first_kernel,
        [tiles(OWN["size"])],
        [
            *(space(16), space(16), pltpu.VMEM(sweeps.shape, jnp.int32)),
            pltpu.SemaphoreType.DMA((3,)),
        ],
        "block_sums",
        *(metric, forcing, sweeps),
        outside=3,
    )
    own = share(own)
    xp, coarse = call(
        first_sides_kernel,
        [tiles(X_FIRST["size"]), tiles(COARSE["size"])],
        [],
        "first_sides",
        own,
    )
    xr = trade_x(xp)
    yp, y2p = call(
        first_rows_kernel,
        [tiles(Y_FIRST["size"]), tiles(3)],
        [],
        "first_rows",
        *(own, coarse, xr),
    )
    yr = trade_y(yp, y2p)
    xp, pf, w, iw1, iw2, h0, h12 = call(
        middle_kernel,
        [
            *(tiles(X_SECOND["size"]), tiles(18, 4), tiles(18, 4), tiles(10, 2), tiles(6, 2)),
            *(tiles(16, 2), tiles(5)),
        ],
        spaces,
        "first_cycle",
        *(own, coarse, xr, yp, yr, sums, copies),
    )
    xr = trade_x(xp)
    yp, y2p = call(
        second_rows_kernel,
        [tiles(Y_SECOND["size"]), tiles(3)],
        [],
        "second_rows",
        *(h0, h12, xr),
    )
    yr = trade_y(yp, y2p)
    return call(
        last_kernel,
        [tiles(16), tiles(16)],
        [*spaces, space(18, 4), space(16), space(16), pltpu.SemaphoreType.DMA((2,))],
        "second_cycle",
        *(own, metric, forcing, h0, xr, yp, yr, pf, w, iw1, iw2, copies),
        outs_outside=True,
    )


def solution(mesh):
    def program(forcing, metric, sweeps):
        return tuple(on_device(forcing, metric, sweeps))

    return jax.shard_map(
        program,
        mesh=mesh,
        in_specs=(P("gx", "gy", "group"), P("gx", "gy", "group"), P()),
        out_specs=(P("gx", "gy", "group"), P("gx", "gy", "group")),
        check_vma=False,
    )
```
